128 devices in a mesh: lat: 8 (over z, core), lon: 16 (over x, y).
Axes of the slice: x: 4, y: 4, z: 4, core: 2. Of those that a mesh axis runs over, the one named last changes fastest.
Arguments:
- state: bfloat16 [1, 6, 24, 524288], P(None, None, None, ('lat', 'lon')), may hold values from -6 to 6
- conv_in: bfloat16 [64, 3, 6], replicated, may hold values from -1.5 to 1.5
- bias_in: float32 [64], replicated, may hold values from -3 to 3
- conv_out: bfloat16 [2, 3, 64], replicated, may hold values from -0.4375 to 0.4375
- bias_out: float32 [2], replicated, may hold values from -3 to 3
- spectral_gain: float32 [344], replicated, may hold values from 0.3 to 3
- mix_in: bfloat16 [64, 3, 8], replicated, may hold values from -1.25 to 1.25
- blend_bias: float32 [64], replicated, may hold values from -3 to 3
- mix_out: bfloat16 [6, 3, 64], replicated, may hold values from -0.4375 to 0.4375
- mix_out_bias: float32 [6], replicated, may hold values from -3 to 3
- level_order: int32 [48], replicated, may hold values from 0 to 47, each once
- wave_order: int32 [344], replicated, may hold values from 0 to 343, each once
Outputs:
- spectrum: float32 [48, 344, 688], P('lon', 'lat')
- increment: float32 [1, 6, 24, 524288], P(None, None, None, ('lat', 'lon'))
The draws below stay inside these ranges and needn't reach their ends.
Inputs may be any that keep to these rules, and one draw needn't show every extreme that they name: `level_order`: a permutation: each item slot holds a different field level. `wave_order`: a permutation: each wavenumber slot holds a different wavenumber.
All inputs are finite; a program needn't handle non-finite values.
Results may differ from the reference program's by a relative error of at most 0.0057.
Values may be sent and summed in bfloat16 or wider, within the bound.
No kernel may reach another device: no remote copies, remote signals or barrier semaphores. Data moves between devices by JAX's collectives and lax.ppermute only.
A program may use at most 128 MiB of HBM per device.

```python
import math
import jax
import jax.numpy as jnp
from jax import lax

NLAT = 512
NLON = 1024
M = 344
LV = 24
VARS = 6
CH = 64
FIELDS = 2
LEVEL_SPACING = 2
SMP = 1
ITEMS = 48
N_LAT = 8
N_LON = 16


def shard_levels(own_key, dims, shards, least, top_value):
    def one(axis_at, shards_of):
        heights = jax.random.uniform(jax.random.fold_in(jax.random.fold_in(own_key, 6), axis_at), (shards_of,), jnp.float32, least / len(shards), top_value / len(shards))
        return jnp.repeat(jnp.exp(heights), dims[axis_at] // shards_of).reshape((-1,) + (1,) * (len(dims) - axis_at - 1))

    loudness = one(*shards[0])
    for cut in shards[1:]:
        loudness = loudness * one(*cut)
    return loudness


def centred(key, shape, width, bound, pieces=(), kind=jnp.bfloat16):
    array = width * jax.random.normal(key, shape, jnp.float32)
    if pieces:
        array = array * shard_levels(key, shape, pieces, -0.22, 0.18)
    return jnp.clip(array, -bound, bound).astype(kind)


def setup_inputs(seed: int = 0) -> dict:
    splits = jax.random.split(jax.random.key(seed), 13)
    state = centred(splits[0], (SMP, VARS, LV, NLAT * NLON), 1.0, 6.0, ((3, 128),))
    conv_in = centred(splits[1], (CH, 3, VARS), (3 * VARS) ** -0.5, 1.5)
    bias_in = centred(splits[2], (CH,), 0.5, 3.0, (), jnp.float32)
    conv_out = centred(splits[3], (FIELDS, 3, CH), (3 * CH) ** -0.5, 0.4375)
    bias_out = centred(splits[4], (FIELDS,), 0.5, 3.0, (), jnp.float32)
    spectral_gain = jnp.clip(jnp.exp(jax.random.uniform(splits[5], (M,), jnp.float32, math.log(0.3), math.log(3.0))), 0.3, 3.0)
    mix_in = centred(splits[6], (CH, 3, FIELDS + VARS), (3 * (FIELDS + VARS)) ** -0.5, 1.25)
    blend_bias = centred(splits[7], (CH,), 0.5, 3.0, (), jnp.float32)
    mix_out = centred(splits[8], (VARS, 3, CH), (3 * CH) ** -0.5, 0.4375)
    mix_out_bias = centred(splits[9], (VARS,), 0.5, 3.0, (), jnp.float32)
    level_order = jax.random.permutation(splits[10], ITEMS).astype(jnp.int32)
    wave_order = jax.random.permutation(splits[11], M).astype(jnp.int32)
    return dict(state=state, conv_in=conv_in, bias_in=bias_in, conv_out=conv_out, bias_out=bias_out, spectral_gain=spectral_gain, mix_in=mix_in, blend_bias=blend_bias, mix_out=mix_out, mix_out_bias=mix_out_bias, level_order=level_order, wave_order=wave_order)


def rounded(value_entries):
    return lax.optimization_barrier(value_entries.astype(jnp.bfloat16))

def untile(value_entries, lat_total, lon_total):
    lead = value_entries.shape[:3]
    band_rows = lat_total // N_LAT
    segment_cols = lon_total // N_LON
    shaped = value_entries.reshape(lead + (N_LAT, N_LON, band_rows, segment_cols))
    return shaped.transpose(0, 1, 2, 3, 5, 4, 6).reshape(lead + (lat_total, lon_total))

def retile(value_entries):
    lead = value_entries.shape[:3]
    lat_total, lon_total = (value_entries.shape[3], value_entries.shape[4])
    band_rows = lat_total // N_LAT
    segment_cols = lon_total // N_LON
    shaped = value_entries.reshape(lead + (N_LAT, band_rows, N_LON, segment_cols))
    return shaped.transpose(0, 1, 2, 3, 5, 4, 6).reshape(lead + (lat_total * lon_total,))

def vertical_conv(value_entries, weight, offset):
    level_stack = value_entries.shape[2]
    padded_levels = jnp.pad(value_entries, ((0, 0), (0, 0), (LEVEL_SPACING, LEVEL_SPACING), (0, 0)))
    summed = offset.astype(jnp.float32)[None, :, None, None]
    for kernel_tap_index in range(3):
        sliding_frame = padded_levels[:, :, kernel_tap_index * LEVEL_SPACING:kernel_tap_index * LEVEL_SPACING + level_stack]
        summed = summed + jnp.einsum('oc,sclx->solx', weight[:, kernel_tap_index].astype(jnp.float32), sliding_frame.astype(jnp.float32))
    return summed

def legendre_tables(waves, lat_total, wave_total):
    lat_index = jnp.arange(lat_total, dtype=jnp.float32)
    latitude = jnp.pi * (lat_index + 0.5) / lat_total - jnp.pi / 2
    sine_lat = jnp.sin(latitude)[None, :]
    cosine = jnp.cos(latitude)[None, :]
    quadrature = jnp.pi * cosine / math.sqrt(lat_total)
    wave_float = waves.astype(jnp.float32)[:, None]
    log_start = 0.5 * jnp.log(jnp.float32(0.5)) + 0.5 * (lax.lgamma(wave_float + 1.5) - lax.lgamma(wave_float + 1.0) - lax.lgamma(jnp.float32(1.5))) + wave_float * jnp.log(cosine)

    def advance(carry, degree_up):
        previous, earlier, log_scale = carry
        degree = wave_float + degree_up
        below = degree - 1.0
        factor_up = jnp.sqrt((4.0 * degree * degree - 1.0) / jnp.maximum(degree * degree - wave_float * wave_float, 1.0))
        factor_down = jnp.sqrt(jnp.maximum(below * below - wave_float * wave_float, 0.0) / jnp.maximum(4.0 * below * below - 1.0, 1.0))
        stepped = factor_up * (sine_lat * previous - factor_down * earlier)
        current = jnp.where(degree_up == 0.0, jnp.ones_like(stepped), stepped)
        too_large = jnp.abs(current) > 1e+16
        shrink = jnp.where(too_large, 1e-16, 1.0)
        current = current * shrink
        previous = previous * shrink
        log_scale = log_scale + jnp.where(too_large, jnp.log(jnp.float32(1e+16)), 0.0)
        legendre = jnp.where(degree <= wave_total - 1, current * jnp.exp(log_scale), 0.0)
        return ((current, previous, log_scale), ((legendre * quadrature).astype(jnp.bfloat16), legendre.astype(jnp.bfloat16)))
    zeros = jnp.zeros_like(log_start)
    initial = (zeros, zeros, log_start)
    degrees_up = jnp.arange(0, wave_total, dtype=jnp.float32)
    _, tables = lax.scan(advance, initial, degrees_up, unroll=4)
    return (tables[0], tables[1])

def transform_tables(waves, lon_total, lat_total):
    lon_index = jnp.arange(lon_total, dtype=jnp.int32)
    phase_index = waves[None, :] * lon_index[:, None] % lon_total
    angles = 2.0 * jnp.pi * phase_index.astype(jnp.float32) / lon_total
    forward_table = (jnp.stack([jnp.cos(angles), jnp.sin(angles)], axis=2) / math.sqrt(lon_total)).reshape(lon_total, 2 * waves.shape[0])
    factor = jnp.where(waves == 0, 1.0, 2.0).astype(jnp.float32) / math.sqrt(lat_total * lon_total)
    inverse_table = jnp.stack([jnp.cos(angles).T, jnp.sin(angles).T], axis=1) * factor[:, None, None]
    inverse_table = inverse_table.reshape(2 * waves.shape[0], lon_total)
    return (forward_table.astype(jnp.bfloat16), inverse_table.astype(jnp.bfloat16))

def reference(state, conv_in, bias_in, conv_out, bias_out, spectral_gain, mix_in, blend_bias, mix_out, mix_out_bias, level_order, wave_order):
    state = untile(state, NLAT, NLON)
    samples, var_count, level_stack, lat_total, lon_total = state.shape
    fields = conv_out.shape[0]
    row_block = 8

    def first_rows(block_index, tendency):
        slab = lax.dynamic_slice_in_dim(state, block_index * row_block, row_block, 3).reshape(samples, var_count, level_stack, row_block * lon_total)
        hidden = rounded(jax.nn.gelu(vertical_conv(slab, conv_in, bias_in)))
        result = vertical_conv(hidden, conv_out, bias_out).astype(jnp.bfloat16).reshape(samples, fields, level_stack, row_block, lon_total)
        return lax.dynamic_update_slice_in_dim(tendency, result, block_index * row_block, 3)
    tendency = lax.fori_loop(0, lat_total // row_block, first_rows, jnp.zeros((samples, fields, level_stack, lat_total, lon_total), jnp.bfloat16))
    wave_total = spectral_gain.shape[0]
    all_waves = jnp.arange(wave_total, dtype=jnp.int32)
    forward_basis, inverse_basis = legendre_tables(all_waves, lat_total, wave_total)
    forward_wide = forward_basis.astype(jnp.float32)
    inverse_wide = inverse_basis.astype(jnp.float32)
    forward_table, inverse_table = transform_tables(all_waves, lon_total, lat_total)
    padded_gain = jnp.concatenate([spectral_gain, jnp.zeros_like(spectral_gain)])
    degree_gain = padded_gain[all_waves[:, None] + all_waves[None, :]]
    item_total = samples * fields * level_stack
    group = math.gcd(item_total, 12)

    def spectral_items(slab):
        coeffs = rounded(jnp.dot(slab.reshape(group * lat_total, lon_total), forward_table, preferred_element_type=jnp.float32))
        coeffs = coeffs.reshape(group, lat_total, wave_total, 2)
        natural = jnp.einsum('kml,nlmp->nmpk', forward_wide, coeffs.astype(jnp.float32))
        scaled = rounded(natural * degree_gain[None, :, None, :])
        returned = rounded(jnp.einsum('kml,nmpk->nlmp', inverse_wide, scaled.astype(jnp.float32)))
        returned = returned.reshape(group * lat_total, 2 * wave_total)
        filtered = jnp.dot(returned, inverse_table, preferred_element_type=jnp.float32).astype(jnp.bfloat16)
        return (natural, filtered.reshape(group, lat_total, lon_total))
    natural_all, filtered = lax.map(spectral_items, tendency.reshape(item_total // group, group, lat_total, lon_total))
    natural_all = natural_all.reshape(item_total, wave_total, 2, wave_total)
    spectrum = natural_all[level_order][:, wave_order].reshape(item_total, wave_total, 2 * wave_total)
    filtered = filtered.reshape(samples, fields, level_stack, lat_total, lon_total)

    def second_rows(block_index, increment):
        filtered_slab = lax.dynamic_slice_in_dim(filtered, block_index * row_block, row_block, 3)
        state_slab = lax.dynamic_slice_in_dim(state, block_index * row_block, row_block, 3)
        joined = jnp.concatenate([filtered_slab, state_slab], axis=1).reshape(samples, fields + var_count, level_stack, row_block * lon_total)
        mixed_hidden = rounded(jax.nn.gelu(vertical_conv(joined, mix_in, blend_bias)))
        result = vertical_conv(mixed_hidden, mix_out, mix_out_bias).reshape(samples, var_count, level_stack, row_block, lon_total)
        return lax.dynamic_update_slice_in_dim(increment, result, block_index * row_block, 3)
    increment = lax.fori_loop(0, lat_total // row_block, second_rows, jnp.zeros((samples, var_count, level_stack, lat_total, lon_total), jnp.float32))
    return (spectrum, retile(increment))
```

```python
import functools
import math

import jax
import jax.numpy as jnp
import ml_dtypes
import numpy as np
from jax import lax
from jax.experimental import pallas as pl
from jax.experimental.pallas import tpu as pltpu
from jax.sharding import PartitionSpec as P

NLAT, NLON, M = 512, 1024, 344
LV, VARS, CH, FIELDS = 24, 6, 64, 2
N_LAT, N_LON = 8, 16
ROWS, COLS = NLAT // N_LAT, NLON // N_LON
COLUMNS = ROWS * COLS
TILES = COLUMNS // 128
ITEMS = FIELDS * LV
GROUP = ITEMS // N_LON
OWNED = M // N_LAT
MP = 48
KP = 352
HALF = NLAT // 2
HID = CH * LV
SLAB = 49
BF, F32 = jnp.bfloat16, jnp.float32
NT = (((1,), (1,)), ((), ()))

BLOCKS = {(0, 0): (0, 0), (0, 1): (0, 1), (1, 0): (0, 2), (1, 1): (1, 2), (2, 0): (1, 0), (2, 1): (1, 1)}


def slab_of(tile, half):
    part, item = BLOCKS[(tile, half)]
    return part * GROUP + item


def iota(shape, dim):
    return lax.broadcasted_iota(jnp.int32, shape, dim)


def over_levels(index):
    return jnp.floor((index.astype(F32) + 0.5) * (1.0 / LV)).astype(jnp.int32)


def dot(a, b):
    return jnp.dot(a, b, preferred_element_type=F32)


def row_order():
    slots = np.arange(ROWS)
    return 2 * (slots % (ROWS // 2)) + slots // (ROWS // 2)


@functools.lru_cache(None)
def constants():
    n = np.arange(M)[:, None]
    angle = 2 * np.pi * ((n * np.arange(NLON)[None, :]) % NLON) / NLON
    factor = np.where(n == 0, 1.0, 2.0) / math.sqrt(NLAT * NLON)
    trig = np.concatenate(
        [np.cos(angle) / math.sqrt(NLON), np.sin(angle) / math.sqrt(NLON), np.cos(angle) * factor, np.sin(angle) * factor],
        axis=1,
    ).astype(ml_dtypes.bfloat16)
    slots = np.arange(NLAT)
    lat = (slots // ROWS) * ROWS + row_order()[slots % ROWS]
    phi = np.pi * (lat + 0.5) / NLAT - np.pi / 2
    sine, cosine = np.sin(phi), np.cos(phi)
    quad = (np.pi * cosine / math.sqrt(NLAT)).reshape(N_LAT, 1, ROWS)
    quad = np.tile(quad, (1, 1, 2 * GROUP)).astype(np.float32)
    lat_rows = np.zeros((8, HALF), np.float32)
    lat_rows[0], lat_rows[1] = sine[:HALF], np.log(cosine[:HALF])
    start = np.zeros((1, 384), np.float32)
    start[0, :M] = [
        0.5 * math.log(0.5) + 0.5 * (math.lgamma(m + 1.5) - math.lgamma(m + 1.0) - math.lgamma(1.5)) for m in range(M)
    ]
    return trig, quad, lat_rows, start


def weights_kernel(taps, w1_ref, vcol_ref, lcol_ref, w2_ref, frow_ref, lrow_ref, b2_ref, o1_ref, o2_ref, ob_ref):
    width = vcol_ref.shape[1]
    rows = frow_ref.shape[0]
    variables = taps // 3
    weights = w1_ref[...]
    r = iota((HID, CH), 0)
    spread = (over_levels(r) == iota((HID, CH), 1)).astype(F32).astype(BF)
    level_row = iota((HID, width), 0)
    level_row = level_row - LV * over_levels(level_row)
    level_col = lcol_ref[...]
    var_col = vcol_ref[...]
    pick = iota((weights.shape[1], width), 0)
    total = jnp.zeros((HID, width), F32)
    for tap in range(3):
        chosen = (pick == tap * variables + var_col).astype(F32).astype(BF)
        block = (0.5 * dot(weights.astype(BF), chosen)).astype(BF)
        wide = dot(spread, block)
        total = jnp.where(level_col == level_row + 2 * (tap - 1), wide, total)
    bias = 0.5 * weights[:, taps : taps + 1]
    high = bias.astype(BF).astype(F32)
    low = bias - high
    lane = iota((CH, width), 1)
    block = jnp.where(lane == width - 16, high, jnp.where(lane == width - 15, low, 0.0)).astype(BF)
    o1_ref[...] = (total + dot(spread, block)).astype(BF)
    second = w2_ref[...]
    c = iota((CH, HID), 1)
    spread2 = (over_levels(c) == iota((CH, HID), 0)).astype(F32).astype(BF)
    level_hid = iota((rows, HID), 1)
    level_hid = level_hid - LV * over_levels(level_hid)
    frow, lrow = frow_ref[...], lrow_ref[...]
    lane2 = iota((rows, second.shape[0]), 1)
    total2 = jnp.zeros((rows, HID), F32)
    for tap in range(3):
        chosen = (lane2 == 3 * frow + tap).astype(F32).astype(BF)
        block = dot(chosen, second.astype(BF)).astype(BF)
        wide = dot(block, spread2)
        total2 = jnp.where(level_hid == lrow + 2 * (tap - 1), wide, total2)
    o2_ref[...] = total2.astype(BF)
    bias2 = jnp.zeros((rows, 128), F32)
    for field in range(b2_ref.shape[0]):
        bias2 = jnp.where(frow == field, b2_ref[field], bias2)
    ob_ref[...] = bias2


def build_weights(w1, bias1, w2, bias2, vcol, lcol, frow, lrow):
    taps = 3 * w1.shape[2]
    w1p = jnp.concatenate([w1.reshape(CH, taps).astype(F32), bias1[:, None], jnp.zeros((CH, 31 - taps), F32)], axis=1)
    fields = w2.shape[0]
    w2p = jnp.pad(w2.reshape(3 * fields, CH).astype(F32), ((0, 32 - 3 * fields), (0, 0)))
    width, rows = vcol.shape[1], frow.shape[0]
    vmem = pl.BlockSpec(memory_space=pltpu.VMEM)
    return pl.pallas_call(
        functools.partial(weights_kernel, taps),
        out_shape=(
            jax.ShapeDtypeStruct((HID, width), BF),
            jax.ShapeDtypeStruct((rows, HID), BF),
            jax.ShapeDtypeStruct((rows, 128), F32),
        ),
        in_specs=[vmem] * 6 + [pl.BlockSpec(memory_space=pltpu.SMEM)],
        out_specs=(vmem, vmem, vmem),
        compiler_params=pltpu.CompilerParams(vmem_limit_bytes=40 * 2**20),
        cost_estimate=pl.CostEstimate(flops=2 * 10**8, bytes_accessed=2 * 10**6, transcendentals=0),
        name="build_weights",
    )(w1p, vcol, lcol, w2p, frow, lrow, bias2)


def hidden_layer(w1_ref, w2_ref, v_ref, h_ref):
    block = v_ref.shape[1]
    step = 256
    for col in range(0, block, step):
        for row in range(0, HID, 256):
            y = dot(w1_ref[row : row + 256, :], v_ref[:, col : col + step])
            u = y * (2 * math.sqrt(2 / math.pi) + (8 * 0.044715 * math.sqrt(2 / math.pi)) * (y * y))
            h_ref[row : row + 256, col : col + step] = (y + y * jnp.tanh(u)).astype(BF)
    return dot(w2_ref[...], h_ref[...])


def first_kernel(block, state_ref, w1_ref, w2_ref, b2_ref, out_ref, v_ref, h_ref, o_ref):
    step = pl.program_id(0)

    @pl.when(step == 0)
    def _():
        v_ref[VARS * LV :, :] = jnp.ones((16, block), BF)

    v_ref[: VARS * LV, :] = state_ref[...]
    result = hidden_layer(w1_ref, w2_ref, v_ref, h_ref)
    bias = b2_ref[...]
    for tile in range(block // 128):
        o_ref[pl.ds(step * (block // 128) + tile, ITEMS, stride=TILES + 1), :] = result[:, tile * 128 : (tile + 1) * 128] + bias

    @pl.when(step == pl.num_programs(0) - 1)
    def _():
        for item in range(ITEMS):
            out_ref[item] = o_ref[item * (TILES + 1) : item * (TILES + 1) + TILES, :].astype(BF)


def first_conv(state, w1, w2, b2, block=512):
    full = lambda *shape: pl.BlockSpec(shape, lambda i: (0,) * len(shape))
    return pl.pallas_call(
        functools.partial(first_kernel, block),
        grid=(COLUMNS // block,),
        out_shape=jax.ShapeDtypeStruct((ITEMS, TILES, 128), BF),
        in_specs=[
            pl.BlockSpec((VARS * LV, block), lambda i: (0, i)),
            full(HID, VARS * LV + 16),
            full(ITEMS, HID),
            full(ITEMS, 128),
        ],
        out_specs=full(ITEMS, TILES, 128),
        scratch_shapes=[
            pltpu.VMEM((VARS * LV + 16, block), BF),
            pltpu.VMEM((HID, block), BF),
            pltpu.VMEM((ITEMS * (TILES + 1), 128), F32),
        ],
        compiler_params=pltpu.CompilerParams(vmem_limit_bytes=40 * 2**20),
        cost_estimate=pl.CostEstimate(flops=3 * 10**9, bytes_accessed=2 * 10**6, transcendentals=HID * COLUMNS),
        name="first_conv",
    )(state, w1, w2, b2)


def second_kernel(block, state_ref, filt_ref, w1_ref, w2_ref, b2_ref, out_ref, v_ref, h_ref, f_ref):
    step = pl.program_id(0)
    base = VARS * LV

    @pl.when(step == 0)
    def _():
        v_ref[base + ITEMS :, :] = jnp.ones((16, block), BF)
        for item in range(ITEMS):
            f_ref[item * (TILES + 1) : item * (TILES + 1) + TILES, :] = filt_ref[item].astype(F32)

    v_ref[:base, :] = state_ref[...]
    for tile in range(block // 128):
        piece = f_ref[pl.ds(step * (block // 128) + tile, ITEMS, stride=TILES + 1), :]
        v_ref[base : base + ITEMS, tile * 128 : (tile + 1) * 128] = piece.astype(BF)
    result = hidden_layer(w1_ref, w2_ref, v_ref, h_ref)
    bias = b2_ref[...]
    for tile in range(block // 128):
        out_ref[:, tile * 128 : (tile + 1) * 128] = result[:, tile * 128 : (tile + 1) * 128] + bias


def second_conv(state, filtered, w1, w2, b2, block=512):
    full = lambda *shape: pl.BlockSpec(shape, lambda i: (0,) * len(shape))
    width = VARS * LV + ITEMS + 16
    return pl.pallas_call(
        functools.partial(second_kernel, block),
        grid=(COLUMNS // block,),
        out_shape=jax.ShapeDtypeStruct((VARS * LV, COLUMNS), F32),
        in_specs=[
            pl.BlockSpec((VARS * LV, block), lambda i: (0, i)),
            full(ITEMS, TILES, 128),
            full(HID, width),
            full(VARS * LV, HID),
            full(VARS * LV, 128),
        ],
        out_specs=pl.BlockSpec((VARS * LV, block), lambda i: (0, i)),
        scratch_shapes=[
            pltpu.VMEM((width, block), BF),
            pltpu.VMEM((HID, block), BF),
            pltpu.VMEM((ITEMS * (TILES + 1), 128), F32),
        ],
        compiler_params=pltpu.CompilerParams(vmem_limit_bytes=40 * 2**20),
        cost_estimate=pl.CostEstimate(flops=4 * 10**9, bytes_accessed=4 * 10**6, transcendentals=HID * COLUMNS),
        name="second_conv",
    )(state, filtered, w1, w2, b2)


CHUNK = 16
STRIDE = CHUNK + 1


def table_kernel(wave_ref, lat_ref, start_ref, out_ref, now_ref, old_ref, log_ref, ratio_ref, s_ref):
    step = pl.program_id(0)
    wave = jnp.broadcast_to(wave_ref[...], (MP, 128))
    sine = [lat_ref[0:1, 128 * h : 128 * h + 128] for h in range(2)]

    @pl.when(step == 0)
    def _():
        match = iota((MP, 384), 1).astype(F32) == wave_ref[...]
        start = jnp.sum(jnp.where(match, start_ref[...], 0.0), axis=1, keepdims=True)
        for h in range(2):
            log_cos = lat_ref[1:2, 128 * h : 128 * h + 128]
            log_ref[h] = jnp.where(wave > 500.0, -1e4, start + wave * log_cos)
            now_ref[h] = jnp.zeros((MP, 128), F32)
            old_ref[h] = jnp.zeros((MP, 128), F32)
        ratio_ref[...] = jnp.zeros((MP, 128), F32)

    now = [now_ref[h] for h in range(2)]
    old = [old_ref[h] for h in range(2)]
    log_scale = [log_ref[h] for h in range(2)]
    ratio = ratio_ref[...]
    scale = [None, None]
    first = (step * CHUNK).astype(F32)
    for kk in range(CHUNK):
        if kk % 8 == 0:
            for h in range(2):
                big = jnp.abs(now[h]) > 1e8
                shrink = jnp.where(big, 1e-12, 1.0)
                now[h] = now[h] * shrink
                old[h] = old[h] * shrink
                log_scale[h] = log_scale[h] + jnp.where(big, math.log(1e12), 0.0)
                scale[h] = jnp.exp(log_scale[h])
        k = first + kk
        n = wave + k
        top = 4.0 * (n * n) - 1.0
        bottom = k * (wave + n)
        root = lax.rsqrt(jnp.maximum(top * bottom, 1e-30))
        up = jnp.where(n <= M - 1.0, top * root, 0.0)
        for h in range(2):
            stepped = up * (sine[h] * now[h] - ratio * old[h])
            if kk == 0:
                stepped = jnp.where(step == 0, 1.0, stepped)
            old[h], now[h] = now[h], stepped
            s_ref[h, pl.ds(kk, MP, stride=STRIDE), :] = stepped * scale[h]
        ratio = bottom * root
    for h in range(2):
        now_ref[h], old_ref[h], log_ref[h] = now[h], old[h], log_scale[h]
    ratio_ref[...] = ratio
    for m in range(MP):
        for h in range(2):
            out_ref[m, :, 128 * h : 128 * h + 128] = s_ref[h, m * STRIDE : m * STRIDE + CHUNK, :].astype(BF)


def legendre_table(waves_f, lat_rows, start):
    full = lambda *shape: pl.BlockSpec(shape, lambda i: (0,) * len(shape))
    return pl.pallas_call(
        table_kernel,
        grid=(KP // CHUNK,),
        out_shape=jax.ShapeDtypeStruct((MP, KP, HALF), BF),
        in_specs=[full(MP, 1), full(8, HALF), full(1, 384)],
        out_specs=pl.BlockSpec((MP, CHUNK, HALF), lambda i: (0, i, 0)),
        scratch_shapes=[pltpu.VMEM((2, MP, 128), F32)] * 3
        + [pltpu.VMEM((MP, 128), F32), pltpu.VMEM((2, MP * STRIDE, 128), F32)],
        compiler_params=pltpu.CompilerParams(vmem_limit_bytes=32 * 2**20),
        cost_estimate=pl.CostEstimate(flops=2 * 10**8, bytes_accessed=9 * 10**6, transcendentals=0),
        name="legendre_table",
    )(waves_f, lat_rows, start)


def swap_halves(x):
    return pltpu.roll(x, 64, 1)


def forward_kernel(y_ref, f_ref, g_ref, q_ref, out_ref, x0_ref, x1_ref):
    low = iota((TILES, 128), 1) < 64
    x0_ref[192:256, :] = jnp.zeros((64, NLON), BF)
    x1_ref[0:64, :] = jnp.zeros((64, NLON), BF)
    place0, place1 = (0, 64, 128), (128, 192, 64)
    for pair in range(N_LON // 2):
        for item in range(GROUP):
            a = y_ref[2 * pair, item].astype(F32)
            b = y_ref[2 * pair + 1, item].astype(F32)
            even = jnp.where(low, a, swap_halves(b)).astype(BF)
            odd = jnp.where(low, swap_halves(a), b).astype(BF)
            lanes = slice(128 * pair, 128 * pair + 128)
            for ref, place in ((x0_ref, place0), (x1_ref, place1)):
                ref[place[item] : place[item] + 32, lanes] = even
                ref[place[item] + 32 : place[item] + 64, lanes] = odd
    quad = q_ref[...]
    cosines = lax.dot_general(f_ref[...], x0_ref[...], NT, preferred_element_type=F32)
    sines = lax.dot_general(g_ref[...], x1_ref[...], NT, preferred_element_type=F32)
    tiles = (cosines[:, :128], cosines[:, 128:] + sines[:, :128], sines[:, 128:])
    for t, value in enumerate(tiles):
        value = (value * quad[:, 128 * t : 128 * t + 128]).astype(BF)
        for group in range(N_LAT):
            out_ref[group, :, 128 * t : 128 * t + 128] = value[group * MP : (group + 1) * MP]


def forward_fourier(pieces, tables, quad):
    full = lambda *shape: pl.BlockSpec(shape, lambda i: (0,) * len(shape))
    return pl.pallas_call(
        forward_kernel,
        grid=(1,),
        out_shape=jax.ShapeDtypeStruct((N_LAT, MP, 384), BF),
        in_specs=[
            full(N_LON, GROUP, TILES, 128),
            pl.BlockSpec((N_LAT * MP, NLON), lambda i: (0, 0)),
            pl.BlockSpec((N_LAT * MP, NLON), lambda i: (0, 1)),
            full(1, 384),
        ],
        out_specs=full(N_LAT, MP, 384),
        scratch_shapes=[pltpu.VMEM((256, NLON), BF)] * 2,
        compiler_params=pltpu.CompilerParams(vmem_limit_bytes=32 * 2**20),
        cost_estimate=pl.CostEstimate(flops=4 * 10**8, bytes_accessed=3 * 10**6, transcendentals=0),
        name="forward_fourier",
    )(pieces, tables, tables, quad)


def inverse_kernel(r_ref, f_ref, g_ref, out_ref):
    turned = [r_ref[:, 128 * t : 128 * t + 128].astype(F32).T.astype(BF) for t in range(3)]
    cosines = jnp.concatenate([turned[0], turned[1][:64]], axis=0)
    sines = jnp.concatenate([turned[2], turned[1][64:]], axis=0)
    grid = dot(cosines, f_ref[...]) + dot(sines, g_ref[...])
    low = iota((TILES, 128), 1) < 64
    for pair in range(N_LON // 2):
        for item in range(GROUP):
            lanes = slice(128 * pair, 128 * pair + 128)
            even = grid[64 * item : 64 * item + 32, lanes]
            odd = grid[64 * item + 32 : 64 * item + 64, lanes]
            out_ref[2 * pair, item] = jnp.where(low, even, swap_halves(odd)).astype(BF)
            out_ref[2 * pair + 1, item] = jnp.where(low, swap_halves(even), odd).astype(BF)


def inverse_fourier(returned, tables):
    full = lambda *shape: pl.BlockSpec(shape, lambda i: (0,) * len(shape))
    return pl.pallas_call(
        inverse_kernel,
        grid=(1,),
        out_shape=jax.ShapeDtypeStruct((N_LON, GROUP, TILES, 128), BF),
        in_specs=[
            full(N_LAT * MP, 384),
            pl.BlockSpec((N_LAT * MP, NLON), lambda i: (0, 2)),
            pl.BlockSpec((N_LAT * MP, NLON), lambda i: (0, 3)),
        ],
        out_specs=full(N_LON, GROUP, TILES, 128),
        compiler_params=pltpu.CompilerParams(vmem_limit_bytes=32 * 2**20),
        cost_estimate=pl.CostEstimate(flops=4 * 10**8, bytes_accessed=3 * 10**6, transcendentals=0),
        name="inverse_fourier",
    )(returned, tables, tables)


WAVES = 8


def spectral_kernel(wave_ref, x_ref, t_ref, gain_ref, spec_ref, out_ref, c_ref, n_ref, r_ref, m_ref):
    step = pl.program_id(0)
    low = iota((MP, 128), 1) < 64
    mirror = (iota((HALF, HALF), 0) + iota((HALF, HALF), 1) == HALF - 1).astype(F32).astype(BF)

    @pl.when(step == 0)
    def _():
        for slab in (6, 7, 14, 15):
            for h in range(2):
                c_ref[h, slab * SLAB : slab * SLAB + MP, :] = jnp.zeros((MP, 128), F32)
        north = {}
        for pair in range(N_LAT // 2):
            for tile in range(3):
                a = x_ref[2 * pair, :, 128 * tile : 128 * tile + 128].astype(F32)
                b = x_ref[2 * pair + 1, :, 128 * tile : 128 * tile + 128].astype(F32)
                both = jnp.where(low, a, swap_halves(b)), jnp.where(low, swap_halves(a), b)
                for half in range(2):
                    slab = slab_of(tile, half)
                    if pair < 2:
                        c_ref[pair, slab * SLAB : slab * SLAB + MP, :] = both[half]
                    else:
                        m_ref[slab * MP : slab * MP + MP, 128 * (pair - 2) : 128 * (pair - 2) + 128] = both[half].astype(BF)
        turned = dot(m_ref[...], mirror)
        for slab in range(6):
            for h in range(2):
                a = c_ref[h, slab * SLAB : slab * SLAB + MP, :]
                b = turned[slab * MP : slab * MP + MP, 128 * h : 128 * h + 128]
                c_ref[h, slab * SLAB : slab * SLAB + MP, :] = a + b
                c_ref[h, (8 + slab) * SLAB : (8 + slab) * SLAB + MP, :] = a - b

    even = iota((8, KP), 1) % 2 == 0
    gain = gain_ref[...]
    for mm in range(WAVES):
        m = step * WAVES + mm
        left = jnp.concatenate([c_ref[h, pl.ds(m, 16, stride=SLAB), :] for h in range(2)], axis=1).astype(BF)
        table = t_ref[mm]
        both = lax.dot_general(left, table, NT, preferred_element_type=F32)
        natural = jnp.where(even, both[:8], both[8:])
        n_ref[0, pl.ds(m, 8, stride=SLAB), :] = natural[:, :128]
        n_ref[1, pl.ds(m, 8, stride=SLAB), :] = natural[:, 128:256]
        n_ref[2, pl.ds(m, 8, stride=SLAB), :] = jnp.concatenate([natural[:, 256:], jnp.zeros((8, 384 - KP), F32)], axis=1)
        scaled = natural * pltpu.roll(gain, 768 - wave_ref[m], 1)[:, :KP]
        right = jnp.concatenate([jnp.where(even, scaled, 0.0), jnp.where(even, 0.0, scaled)], axis=0).astype(BF)
        back = dot(right, table)
        north, south = back[:8] + back[8:], back[:8] - back[8:]
        for h in range(2):
            r_ref[h, pl.ds(m, 8, stride=SLAB), :] = north[:, 128 * h : 128 * h + 128]
            r_ref[2 + h, pl.ds(m, 8, stride=SLAB), :] = south[:, 128 * h : 128 * h + 128]

    @pl.when(step == pl.num_programs(0) - 1)
    def _():
        for slab in range(6):
            for h in range(2):
                m_ref[slab * MP : slab * MP + MP, 128 * h : 128 * h + 128] = r_ref[2 + h, slab * SLAB : slab * SLAB + MP, :].astype(BF)
        turned = dot(m_ref[...], mirror)

        def tile_of(slab, j):
            if j < 2:
                return r_ref[j, slab * SLAB : slab * SLAB + MP, :]
            return turned[slab * MP : slab * MP + MP, 128 * (j - 2) : 128 * (j - 2) + 128]

        for pair in range(N_LAT // 2):
            for tile in range(3):
                a = tile_of(slab_of(tile, 0), pair)
                b = tile_of(slab_of(tile, 1), pair)
                lanes = slice(128 * tile, 128 * tile + 128)
                out_ref[2 * pair, :, lanes] = jnp.where(low, a, swap_halves(b)).astype(BF)
                out_ref[2 * pair + 1, :, lanes] = jnp.where(low, swap_halves(a), b).astype(BF)
        wide = iota((MP, 768), 1) < M
        zeros = jnp.zeros((MP, 384), F32)
        for item in range(GROUP):
            parts = []
            for part in range(2):
                at = (part * GROUP + item) * SLAB
                parts.append(jnp.concatenate([n_ref[h, at : at + MP, :] for h in range(3)] + [zeros], axis=1))
            value = jnp.where(wide, parts[0], pltpu.roll(parts[1], M, 1))
            spec_ref[item] = value[:OWNED, : 2 * M]


def spectral_step(waves, coeffs, table, gain):
    full = lambda *shape: pl.BlockSpec(shape, lambda i, w: (0,) * len(shape))
    return pl.pallas_call(
        spectral_kernel,
        grid_spec=pltpu.PrefetchScalarGridSpec(
            num_scalar_prefetch=1,
            grid=(MP // WAVES,),
            in_specs=[
                full(N_LAT, MP, 384),
                pl.BlockSpec((WAVES, KP, HALF), lambda i, w: (i, 0, 0)),
                full(8, 768),
            ],
            out_specs=(full(GROUP, OWNED, 2 * M), full(N_LAT, MP, 384)),
            scratch_shapes=[
                pltpu.VMEM((2, 16 * SLAB, 128), F32),
                pltpu.VMEM((3, 8 * SLAB, 128), F32),
                pltpu.VMEM((4, 8 * SLAB, 128), F32),
                pltpu.VMEM((6 * MP, HALF), BF),
            ],
        ),
        out_shape=(
            jax.ShapeDtypeStruct((GROUP, OWNED, 2 * M), F32),
            jax.ShapeDtypeStruct((N_LAT, MP, 384), BF),
        ),
        compiler_params=pltpu.CompilerParams(vmem_limit_bytes=40 * 2**20),
        cost_estimate=pl.CostEstimate(flops=4 * 10**9, bytes_accessed=10**7, transcendentals=0),
        name="spectral_step",
    )(waves, coeffs, table, gain)


def per_device(
    state, conv_in, bias_in, conv_out, bias_out, spectral_gain, mix_in, blend_bias, mix_out, mix_out_bias, level_order, wave_order
):
    trig, quad, lat_rows, start = constants()
    band = lax.axis_index("lat")
    columns = state.reshape(VARS * LV, COLUMNS)

    slot_field = (level_order >= LV).astype(jnp.int32)
    slot_level = level_order - LV * slot_field
    state_rows = np.arange(VARS * LV, dtype=np.int32)
    none = np.full((16,), -100, np.int32)
    w1, w2, b2 = build_weights(
        conv_in,
        bias_in,
        conv_out,
        bias_out,
        jnp.asarray(np.concatenate([state_rows // LV, none])[None]),
        jnp.asarray(np.concatenate([state_rows % LV, none])[None]),
        slot_field[:, None],
        slot_level[:, None],
    )
    tendency = first_conv(columns, w1, w2, b2)
    pieces = lax.all_to_all(tendency.reshape(N_LON, GROUP, TILES, 128), "lon", 0, 0, tiled=True)

    grouped = jnp.pad(wave_order.reshape(N_LAT, OWNED), ((0, 0), (0, MP - OWNED)), constant_values=-1)
    chosen = (grouped.reshape(N_LAT * MP)[:, None] == jnp.arange(M, dtype=jnp.int32)[None, :]).astype(BF)
    tables = dot(chosen, jnp.asarray(trig)).astype(BF)
    owned = lax.dynamic_slice_in_dim(grouped, band, 1, 0)[0]
    waves_f = jnp.where(owned < 0, 1000, owned).astype(F32)[:, None]
    table = legendre_table(waves_f, jnp.asarray(lat_rows), jnp.asarray(start))
    band_quad = lax.dynamic_slice_in_dim(jnp.asarray(quad), band, 1, 0)[0]
    gain = jnp.broadcast_to(jnp.pad(spectral_gain, (0, 768 - M))[None], (8, 768))

    coeffs = forward_fourier(pieces, tables, band_quad)
    coeffs = lax.all_to_all(coeffs, "lat", 0, 0, tiled=True)
    spectrum, returned = spectral_step(jnp.maximum(owned, 0), coeffs, table, gain)
    returned = lax.all_to_all(returned, "lat", 0, 0, tiled=True)
    grid_values = inverse_fourier(returned.reshape(N_LAT * MP, 384), tables)
    filtered = lax.all_to_all(grid_values, "lon", 0, 0, tiled=True)

    m1, m2, mb = build_weights(
        mix_in,
        blend_bias,
        mix_out,
        mix_out_bias,
        jnp.concatenate([jnp.asarray(FIELDS + state_rows // LV), slot_field, jnp.asarray(none)])[None],
        jnp.concatenate([jnp.asarray(state_rows % LV), slot_level, jnp.asarray(none)])[None],
        jnp.asarray(state_rows // LV)[:, None],
        jnp.asarray(state_rows % LV)[:, None],
    )
    increment = second_conv(columns, filtered.reshape(ITEMS, TILES, 128), m1, m2, mb)
    return spectrum, increment.reshape(1, VARS, LV, COLUMNS)


def solution(mesh):
    return jax.shard_map(
        per_device,
        mesh=mesh,
        in_specs=(P(None, None, None, ("lat", "lon")),) + (P(),) * 11,
        out_specs=(P("lon", "lat", None), P(None, None, None, ("lat", "lon"))),
        check_vma=False,
    )
```

```python
import functools
import math

import jax
import jax.numpy as jnp
import ml_dtypes
import numpy as np
from jax import lax
from jax.experimental import pallas as pl
from jax.experimental.pallas import tpu as pltpu
from jax.sharding import PartitionSpec as P

NLAT, NLON, M = 512, 1024, 344
LV, VARS, CH, FIELDS = 24, 6, 64, 2
N_LAT, N_LON = 8, 16
ROWS, COLS = NLAT // N_LAT, NLON // N_LON
COLUMNS = ROWS * COLS
TILES = COLUMNS // 128
ITEMS = FIELDS * LV
GROUP = ITEMS // N_LON
OWNED = M // N_LAT
MP = 48
MH = MP // 2
KP = 352
HALF = NLAT // 2
HID = CH * LV
SLAB = 49
BF, F32 = jnp.bfloat16, jnp.float32
NT = (((1,), (1,)), ((), ()))

BLOCKS = {(0, 0): (0, 0), (0, 1): (0, 1), (1, 0): (0, 2), (1, 1): (1, 2), (2, 0): (1, 0), (2, 1): (1, 1)}


def slab_of(tile, half):
    part, item = BLOCKS[(tile, half)]
    return part * GROUP + item


def iota(shape, dim):
    return lax.broadcasted_iota(jnp.int32, shape, dim)


def over_levels(index):
    return jnp.floor((index.astype(F32) + 0.5) * (1.0 / LV)).astype(jnp.int32)


def hbm(x):
    return pltpu.with_memory_space_constraint(x, pltpu.HBM)


def dot(a, b):
    return jnp.dot(a, b, preferred_element_type=F32)


def row_order():
    slots = np.arange(ROWS)
    return 2 * (slots % (ROWS // 2)) + slots // (ROWS // 2)


@functools.lru_cache(None)
def constants():
    n = np.arange(M)[:, None]
    angle = 2 * np.pi * ((n * np.arange(NLON)[None, :]) % NLON) / NLON
    factor = np.where(n == 0, 1.0, 2.0) / math.sqrt(NLAT * NLON)
    trig = np.concatenate(
        [np.cos(angle) / math.sqrt(NLON), np.sin(angle) / math.sqrt(NLON), np.cos(angle) * factor, np.sin(angle) * factor],
        axis=1,
    ).astype(ml_dtypes.bfloat16)
    slots = np.arange(NLAT)
    lat = (slots // ROWS) * ROWS + row_order()[slots % ROWS]
    phi = np.pi * (lat + 0.5) / NLAT - np.pi / 2
    sine, cosine = np.sin(phi), np.cos(phi)
    quad = (np.pi * cosine / math.sqrt(NLAT)).reshape(N_LAT, 1, ROWS)
    quad = np.tile(quad, (1, 1, 2 * GROUP)).astype(np.float32)
    lat_rows = np.zeros((8, HALF), np.float32)
    lat_rows[0], lat_rows[1] = sine[:HALF], np.log(cosine[:HALF])
    start = np.zeros((1, 384), np.float32)
    start[0, :M] = [
        0.5 * math.log(0.5) + 0.5 * (math.lgamma(m + 1.5) - math.lgamma(m + 1.0) - math.lgamma(1.5)) for m in range(M)
    ]
    return trig, quad, lat_rows, start


def to_column(row):
    n = row.shape[1]
    return jnp.sum(jnp.where(iota((n, n), 0) == iota((n, n), 1), row, jnp.zeros_like(row)), axis=1, keepdims=True)


def make_weights(w1_ref, bias1_ref, w2_ref, order_ref, bias2_ref, slots_in, o1_ref, o2_ref, ob_ref):
    width, rows = o1_ref.shape[1], o2_ref.shape[0]
    variables, fields = w1_ref.shape[1], w2_ref.shape[1]
    order = order_ref[...]
    base = VARS * LV
    column = iota((1, width), 1)
    var_col = over_levels(column)
    level_col = column - LV * var_col
    if slots_in:
        wide_order = jnp.concatenate([jnp.zeros((1, base), jnp.int32), order, jnp.zeros((1, width - base - ITEMS), jnp.int32)], axis=1)
        slot_field = (wide_order >= LV).astype(jnp.int32)
        var_col = jnp.where(column < base, var_col + FIELDS, slot_field)
        level_col = jnp.where(column < base, level_col, wide_order - LV * slot_field)
    level_col = jnp.where(column < width - 16, level_col, -100)
    r = iota((HID, CH), 0)
    spread = (over_levels(r) == iota((HID, CH), 1)).astype(F32).astype(BF)
    level_row = iota((HID, width), 0)
    level_row = level_row - LV * over_levels(level_row)
    total = jnp.zeros((HID, width), F32)
    pick = (iota((variables, width), 0) == var_col).astype(F32).astype(BF)
    for tap in range(3):
        tall = lax.dot_general(spread, w1_ref[tap], NT, preferred_element_type=F32)
        wide = dot((0.5 * tall).astype(BF), pick)
        total = jnp.where(level_col == level_row + 2 * (tap - 1), wide, total)
    bias = 0.5 * to_column(bias1_ref[...])
    high = bias.astype(BF).astype(F32)
    low = bias - high
    block = jnp.where(column == width - 16, high, jnp.where(column == width - 15, low, 0.0)).astype(BF)
    o1_ref[...] = (total + dot(spread, block)).astype(BF)
    if slots_in:
        row = iota((rows, 1), 0)
        field_row = over_levels(row)
    else:
        row = to_column(order.astype(F32)).astype(jnp.int32)
        field_row = (row >= LV).astype(jnp.int32)
    level_out = row - LV * field_row
    c = iota((CH, HID), 1)
    spread2 = (over_levels(c) == iota((CH, HID), 0)).astype(F32).astype(BF)
    level_hid = iota((rows, HID), 1)
    level_hid = level_hid - LV * over_levels(level_hid)
    total2 = jnp.zeros((rows, HID), F32)
    bias2 = jnp.zeros((rows, 128), F32)
    for tap in range(3):
        block = jnp.zeros((rows, CH), F32)
        for field in range(fields):
            block = jnp.where(field_row == field, w2_ref[tap].astype(F32)[field : field + 1, :], block)
        wide = dot(block.astype(BF), spread2)
        total2 = jnp.where(level_hid == level_out + 2 * (tap - 1), wide, total2)
    o2_ref[...] = total2.astype(BF)
    for field in range(fields):
        bias2 = jnp.where(field_row == field, bias2_ref[0:1, field : field + 1], bias2)
    ob_ref[...] = bias2


def weights_kernel(w1_ref, bias1_ref, w2_ref, order_ref, bias2_ref, o1_ref, o2_ref, ob_ref):
    make_weights(w1_ref, bias1_ref, w2_ref, order_ref, bias2_ref, True, o1_ref, o2_ref, ob_ref)


def second_weights(w1, bias1, w2, bias2, order):
    full = lambda *shape: pl.BlockSpec(shape, lambda i: (0,) * len(shape))
    width, rows = VARS * LV + ITEMS + 16, VARS * LV
    return pl.pallas_call(
        weights_kernel,
        out_shape=(
            pltpu.HBM((HID, width), BF),
            pltpu.HBM((rows, HID), BF),
            pltpu.HBM((rows, 128), F32),
        ),
        grid=(1,),
        in_specs=[full(*w1.shape), full(1, CH), full(*w2.shape), full(1, ITEMS), full(1, bias2.shape[0])],
        out_specs=(full(HID, width), full(rows, HID), full(rows, 128)),
        compiler_params=pltpu.CompilerParams(vmem_limit_bytes=20 * 2**20),
        cost_estimate=pl.CostEstimate(flops=2 * 10**8, bytes_accessed=2 * 10**6, transcendentals=0),
        name="second_weights",
    )(hbm(w1), hbm(bias1.reshape(1, CH)), hbm(w2), hbm(order.reshape(1, ITEMS)), hbm(bias2.reshape(1, -1)))


def hidden_layer(w1_ref, w2_ref, v_ref, h_ref):
    block = v_ref.shape[1]
    step = 256
    for col in range(0, block, step):
        for row in range(0, HID, 256):
            y = dot(w1_ref[row : row + 256, :], v_ref[:, col : col + step])
            u = y * (2 * math.sqrt(2 / math.pi) + (8 * 0.044715 * math.sqrt(2 / math.pi)) * (y * y))
            h_ref[row : row + 256, col : col + step] = (y + y * jnp.tanh(u)).astype(BF)
    return dot(w2_ref[...], h_ref[...])


def first_kernel(
    block, state_ref, c1_ref, bias1_ref, c2_ref, order_ref, bias2_ref, out_ref, w1_ref, w2_ref, b2_ref, v_ref, h_ref, o_ref
):
    step = pl.program_id(0)

    @pl.when(step == 0)
    def _():
        make_weights(c1_ref, bias1_ref, c2_ref, order_ref, bias2_ref, False, w1_ref, w2_ref, b2_ref)
        v_ref[VARS * LV :, :] = jnp.ones((16, block), BF)

    v_ref[: VARS * LV, :] = state_ref[...]
    result = hidden_layer(w1_ref, w2_ref, v_ref, h_ref)
    bias = b2_ref[...]
    for tile in range(block // 128):
        o_ref[pl.ds(step * (block // 128) + tile, ITEMS, stride=TILES + 1), :] = result[:, tile * 128 : (tile + 1) * 128] + bias

    @pl.when(step == pl.num_programs(0) - 1)
    def _():
        for item in range(ITEMS):
            out_ref[item] = o_ref[item * (TILES + 1) : item * (TILES + 1) + TILES, :].astype(BF)


def first_conv(state, w1, bias1, w2, bias2, order, block=512):
    full = lambda *shape: pl.BlockSpec(shape, lambda i: (0,) * len(shape))
    return pl.pallas_call(
        functools.partial(first_kernel, block),
        grid=(COLUMNS // block,),
        out_shape=pltpu.HBM((ITEMS, TILES, 128), BF),
        in_specs=[
            pl.BlockSpec((VARS * LV, block), lambda i: (0, i)),
            full(*w1.shape),
            full(1, CH),
            full(*w2.shape),
            full(1, ITEMS),
            full(1, bias2.shape[0]),
        ],
        out_specs=full(ITEMS, TILES, 128),
        scratch_shapes=[
            pltpu.VMEM((HID, VARS * LV + 16), BF),
            pltpu.VMEM((ITEMS, HID), BF),
            pltpu.VMEM((ITEMS, 128), F32),
            pltpu.VMEM((VARS * LV + 16, block), BF),
            pltpu.VMEM((HID, block), BF),
            pltpu.VMEM((ITEMS * (TILES + 1), 128), F32),
        ],
        compiler_params=pltpu.CompilerParams(vmem_limit_bytes=24 * 2**20),
        cost_estimate=pl.CostEstimate(flops=3 * 10**9, bytes_accessed=2 * 10**6, transcendentals=HID * COLUMNS),
        name="first_conv",
    )(hbm(state), hbm(w1), hbm(bias1.reshape(1, CH)), hbm(w2), hbm(order.reshape(1, ITEMS)), hbm(bias2.reshape(1, -1)))


def second_kernel(block, state_ref, filt_ref, w1_ref, w2_ref, b2_ref, out_ref, v_ref, h_ref, f_ref):
    step = pl.program_id(0)
    base = VARS * LV

    @pl.when(step == 0)
    def _():
        v_ref[base + ITEMS :, :] = jnp.ones((16, block), BF)
        for item in range(ITEMS):
            f_ref[item * (TILES + 1) : item * (TILES + 1) + TILES, :] = filt_ref[item].astype(F32)

    v_ref[:base, :] = state_ref[...]
    for tile in range(block // 128):
        piece = f_ref[pl.ds(step * (block // 128) + tile, ITEMS, stride=TILES + 1), :]
        v_ref[base : base + ITEMS, tile * 128 : (tile + 1) * 128] = piece.astype(BF)
    result = hidden_layer(w1_ref, w2_ref, v_ref, h_ref)
    bias = b2_ref[...]
    for tile in range(block // 128):
        out_ref[:, tile * 128 : (tile + 1) * 128] = result[:, tile * 128 : (tile + 1) * 128] + bias


def second_conv(state, filtered, w1, w2, b2, block=512):
    full = lambda *shape: pl.BlockSpec(shape, lambda i: (0,) * len(shape))
    width = VARS * LV + ITEMS + 16
    return pl.pallas_call(
        functools.partial(second_kernel, block),
        grid=(COLUMNS // block,),
        out_shape=pltpu.HBM((VARS * LV, COLUMNS), F32),
        in_specs=[
            pl.BlockSpec((VARS * LV, block), lambda i: (0, i)),
            full(ITEMS, TILES, 128),
            full(HID, width),
            full(VARS * LV, HID),
            full(VARS * LV, 128),
        ],
        out_specs=pl.BlockSpec((VARS * LV, block), lambda i: (0, i)),
        scratch_shapes=[
            pltpu.VMEM((width, block), BF),
            pltpu.VMEM((HID, block), BF),
            pltpu.VMEM((ITEMS * (TILES + 1), 128), F32),
        ],
        compiler_params=pltpu.CompilerParams(vmem_limit_bytes=24 * 2**20),
        cost_estimate=pl.CostEstimate(flops=4 * 10**9, bytes_accessed=4 * 10**6, transcendentals=HID * COLUMNS),
        name="second_conv",
    )(hbm(state), filtered, w1, w2, b2)


CHUNK = 16
STRIDE = CHUNK + 1


def table_kernel(wave_ref, lat_ref, start_ref, out_ref, now_ref, old_ref, log_ref, ratio_ref, s_ref):
    step = pl.program_id(0)
    wave = jnp.broadcast_to(wave_ref[...], (MH, 128))
    sine = [lat_ref[0:1, 128 * h : 128 * h + 128] for h in range(2)]

    @pl.when(step == 0)
    def _():
        match = iota((MH, 384), 1).astype(F32) == wave_ref[...]
        start = jnp.sum(jnp.where(match, start_ref[...], 0.0), axis=1, keepdims=True)
        for h in range(2):
            log_cos = lat_ref[1:2, 128 * h : 128 * h + 128]
            log_ref[h] = jnp.where(wave > 500.0, -1e4, start + wave * log_cos)
            now_ref[h] = jnp.zeros((MH, 128), F32)
            old_ref[h] = jnp.zeros((MH, 128), F32)
        ratio_ref[...] = jnp.zeros((MH, 128), F32)

    now = [now_ref[h] for h in range(2)]
    old = [old_ref[h] for h in range(2)]
    log_scale = [log_ref[h] for h in range(2)]
    ratio = ratio_ref[...]
    scale = [None, None]
    first = (step * CHUNK).astype(F32)
    for kk in range(CHUNK):
        if kk % 8 == 0:
            for h in range(2):
                big = jnp.abs(now[h]) > 1e8
                shrink = jnp.where(big, 1e-12, 1.0)
                now[h] = now[h] * shrink
                old[h] = old[h] * shrink
                log_scale[h] = log_scale[h] + jnp.where(big, math.log(1e12), 0.0)
                scale[h] = jnp.exp(log_scale[h])
        k = first + kk
        n = wave + k
        top = 4.0 * (n * n) - 1.0
        bottom = k * (wave + n)
        root = lax.rsqrt(jnp.maximum(top * bottom, 1e-30))
        up = jnp.where(n <= M - 1.0, top * root, 0.0)
        for h in range(2):
            stepped = up * (sine[h] * now[h] - ratio * old[h])
            if kk == 0:
                stepped = jnp.where(step == 0, 1.0, stepped)
            old[h], now[h] = now[h], stepped
            s_ref[h, pl.ds(kk, MH, stride=STRIDE), :] = stepped * scale[h]
        ratio = bottom * root
    for h in range(2):
        now_ref[h], old_ref[h], log_ref[h] = now[h], old[h], log_scale[h]
    ratio_ref[...] = ratio
    for m in range(MH):
        for h in range(2):
            out_ref[m, :, 128 * h : 128 * h + 128] = s_ref[h, m * STRIDE : m * STRIDE + CHUNK, :].astype(BF)


def legendre_table(waves_f, lat_rows, start):
    full = lambda *shape: pl.BlockSpec(shape, lambda i: (0,) * len(shape))
    return pl.pallas_call(
        table_kernel,
        grid=(KP // CHUNK,),
        out_shape=pltpu.HBM((MH, KP, HALF), BF),
        in_specs=[full(MH, 1), full(8, HALF), full(1, 384)],
        out_specs=pl.BlockSpec((MH, CHUNK, HALF), lambda i: (0, i, 0)),
        scratch_shapes=[pltpu.VMEM((2, MH, 128), F32)] * 3
        + [pltpu.VMEM((MH, 128), F32), pltpu.VMEM((2, MH * STRIDE, 128), F32)],
        compiler_params=pltpu.CompilerParams(vmem_limit_bytes=20 * 2**20),
        cost_estimate=pl.CostEstimate(flops=2 * 10**8, bytes_accessed=9 * 10**6, transcendentals=0),
        name="legendre_table",
    )(waves_f, lat_rows, start)


def swap_halves(x):
    return pltpu.roll(x, 64, 1)


def forward_kernel(y_ref, f_ref, g_ref, q_ref, out_ref, x0_ref, x1_ref):
    low = iota((TILES, 128), 1) < 64
    x0_ref[192:256, :] = jnp.zeros((64, NLON), BF)
    x1_ref[0:64, :] = jnp.zeros((64, NLON), BF)
    place0, place1 = (0, 64, 128), (128, 192, 64)
    for pair in range(N_LON // 2):
        for item in range(GROUP):
            a = y_ref[2 * pair, item].astype(F32)
            b = y_ref[2 * pair + 1, item].astype(F32)
            even = jnp.where(low, a, swap_halves(b)).astype(BF)
            odd = jnp.where(low, swap_halves(a), b).astype(BF)
            lanes = slice(128 * pair, 128 * pair + 128)
            for ref, place in ((x0_ref, place0), (x1_ref, place1)):
                ref[place[item] : place[item] + 32, lanes] = even
                ref[place[item] + 32 : place[item] + 64, lanes] = odd
    quad = q_ref[...]
    cosines = lax.dot_general(f_ref[...], x0_ref[...], NT, preferred_element_type=F32)
    sines = lax.dot_general(g_ref[...], x1_ref[...], NT, preferred_element_type=F32)
    tiles = (cosines[:, :128], cosines[:, 128:] + sines[:, :128], sines[:, 128:])
    for t, value in enumerate(tiles):
        value = (value * quad[:, 128 * t : 128 * t + 128]).astype(BF)
        for group in range(N_LAT):
            out_ref[group, :, 128 * t : 128 * t + 128] = value[group * MP : (group + 1) * MP]


def forward_fourier(pieces, tables, quad):
    full = lambda *shape: pl.BlockSpec(shape, lambda i: (0,) * len(shape))
    return pl.pallas_call(
        forward_kernel,
        grid=(1,),
        out_shape=pltpu.HBM((N_LAT, MP, 384), BF),
        in_specs=[
            full(N_LON, GROUP, TILES, 128),
            pl.BlockSpec((N_LAT * MP, NLON), lambda i: (0, 0)),
            pl.BlockSpec((N_LAT * MP, NLON), lambda i: (0, 1)),
            full(1, 384),
        ],
        out_specs=full(N_LAT, MP, 384),
        scratch_shapes=[pltpu.VMEM((256, NLON), BF)] * 2,
        compiler_params=pltpu.CompilerParams(vmem_limit_bytes=20 * 2**20),
        cost_estimate=pl.CostEstimate(flops=4 * 10**8, bytes_accessed=3 * 10**6, transcendentals=0),
        name="forward_fourier",
    )(pieces, tables, tables, quad)


def inverse_kernel(r_ref, f_ref, g_ref, out_ref):
    turned = [r_ref[:, 128 * t : 128 * t + 128].astype(F32).T.astype(BF) for t in range(3)]
    cosines = jnp.concatenate([turned[0], turned[1][:64]], axis=0)
    sines = jnp.concatenate([turned[2], turned[1][64:]], axis=0)
    grid = dot(cosines, f_ref[...]) + dot(sines, g_ref[...])
    low = iota((TILES, 128), 1) < 64
    for pair in range(N_LON // 2):
        for item in range(GROUP):
            lanes = slice(128 * pair, 128 * pair + 128)
            even = grid[64 * item : 64 * item + 32, lanes]
            odd = grid[64 * item + 32 : 64 * item + 64, lanes]
            out_ref[2 * pair, item] = jnp.where(low, even, swap_halves(odd)).astype(BF)
            out_ref[2 * pair + 1, item] = jnp.where(low, swap_halves(even), odd).astype(BF)


def inverse_fourier(returned, tables):
    full = lambda *shape: pl.BlockSpec(shape, lambda i: (0,) * len(shape))
    return pl.pallas_call(
        inverse_kernel,
        grid=(1,),
        out_shape=pltpu.HBM((N_LON, GROUP, TILES, 128), BF),
        in_specs=[
            full(N_LAT * MP, 384),
            pl.BlockSpec((N_LAT * MP, NLON), lambda i: (0, 0)),
            pl.BlockSpec((N_LAT * MP, NLON), lambda i: (0, 1)),
        ],
        out_specs=full(N_LON, GROUP, TILES, 128),
        compiler_params=pltpu.CompilerParams(vmem_limit_bytes=20 * 2**20),
        cost_estimate=pl.CostEstimate(flops=4 * 10**8, bytes_accessed=3 * 10**6, transcendentals=0),
        name="inverse_fourier",
    )(returned, tables, tables)


WAVES = 8


def spectral_kernel(wave_ref, x_ref, t0_ref, t1_ref, gain_ref, spec_ref, out_ref, c_ref, n_ref, r_ref, m_ref):
    step = pl.program_id(0)
    low = iota((MP, 128), 1) < 64
    mirror = (iota((HALF, HALF), 0) + iota((HALF, HALF), 1) == HALF - 1).astype(F32).astype(BF)

    @pl.when(step == 0)
    def _():
        for slab in (6, 7, 14, 15):
            for h in range(2):
                c_ref[h, slab * SLAB : slab * SLAB + MP, :] = jnp.zeros((MP, 128), F32)
        north = {}
        for pair in range(N_LAT // 2):
            for tile in range(3):
                a = x_ref[2 * pair, :, 128 * tile : 128 * tile + 128].astype(F32)
                b = x_ref[2 * pair + 1, :, 128 * tile : 128 * tile + 128].astype(F32)
                both = jnp.where(low, a, swap_halves(b)), jnp.where(low, swap_halves(a), b)
                for half in range(2):
                    slab = slab_of(tile, half)
                    if pair < 2:
                        c_ref[pair, slab * SLAB : slab * SLAB + MP, :] = both[half]
                    else:
                        m_ref[slab * MP : slab * MP + MP, 128 * (pair - 2) : 128 * (pair - 2) + 128] = both[half].astype(BF)
        turned = dot(m_ref[...], mirror)
        for slab in range(6):
            for h in range(2):
                a = c_ref[h, slab * SLAB : slab * SLAB + MP, :]
                b = turned[slab * MP : slab * MP + MP, 128 * h : 128 * h + 128]
                c_ref[h, slab * SLAB : slab * SLAB + MP, :] = a + b
                c_ref[h, (8 + slab) * SLAB : (8 + slab) * SLAB + MP, :] = a - b

    even = iota((8, KP), 1) % 2 == 0
    gain = gain_ref[...]

    def waves(t_ref):
        for mm in range(WAVES):
            m = step * WAVES + mm
            left = jnp.concatenate([c_ref[h, pl.ds(m, 16, stride=SLAB), :] for h in range(2)], axis=1).astype(BF)
            table = t_ref[mm]
            both = lax.dot_general(left, table, NT, preferred_element_type=F32)
            natural = jnp.where(even, both[:8], both[8:])
            n_ref[0, pl.ds(m, 8, stride=SLAB), :] = natural[:, :128]
            n_ref[1, pl.ds(m, 8, stride=SLAB), :] = natural[:, 128:256]
            n_ref[2, pl.ds(m, 8, stride=SLAB), :] = jnp.concatenate([natural[:, 256:], jnp.zeros((8, 384 - KP), F32)], axis=1)
            scaled = natural * pltpu.roll(gain, 768 - wave_ref[m], 1)[:, :KP]
            right = jnp.concatenate([jnp.where(even, scaled, 0.0), jnp.where(even, 0.0, scaled)], axis=0).astype(BF)
            back = dot(right, table)
            north, south = back[:8] + back[8:], back[:8] - back[8:]
            for h in range(2):
                r_ref[h, pl.ds(m, 8, stride=SLAB), :] = north[:, 128 * h : 128 * h + 128]
                r_ref[2 + h, pl.ds(m, 8, stride=SLAB), :] = south[:, 128 * h : 128 * h + 128]

    pl.when(step < MH // WAVES)(lambda: waves(t0_ref))
    pl.when(step >= MH // WAVES)(lambda: waves(t1_ref))

    @pl.when(step == pl.num_programs(0) - 1)
    def _():
        for slab in range(6):
            for h in range(2):
                m_ref[slab * MP : slab * MP + MP, 128 * h : 128 * h + 128] = r_ref[2 + h, slab * SLAB : slab * SLAB + MP, :].astype(BF)
        turned = dot(m_ref[...], mirror)

        def tile_of(slab, j):
            if j < 2:
                return r_ref[j, slab * SLAB : slab * SLAB + MP, :]
            return turned[slab * MP : slab * MP + MP, 128 * (j - 2) : 128 * (j - 2) + 128]

        for pair in range(N_LAT // 2):
            for tile in range(3):
                a = tile_of(slab_of(tile, 0), pair)
                b = tile_of(slab_of(tile, 1), pair)
                lanes = slice(128 * tile, 128 * tile + 128)
                out_ref[2 * pair, :, lanes] = jnp.where(low, a, swap_halves(b)).astype(BF)
                out_ref[2 * pair + 1, :, lanes] = jnp.where(low, swap_halves(a), b).astype(BF)
        wide = iota((MP, 768), 1) < M
        zeros = jnp.zeros((MP, 384), F32)
        for item in range(GROUP):
            parts = []
            for part in range(2):
                at = (part * GROUP + item) * SLAB
                parts.append(jnp.concatenate([n_ref[h, at : at + MP, :] for h in range(3)] + [zeros], axis=1))
            value = jnp.where(wide, parts[0], pltpu.roll(parts[1], M, 1))
            spec_ref[item] = value[:OWNED, : 2 * M]


def spectral_step(waves, coeffs, table0, table1, gain):
    full = lambda *shape: pl.BlockSpec(shape, lambda i, w: (0,) * len(shape))
    return pl.pallas_call(
        spectral_kernel,
        grid_spec=pltpu.PrefetchScalarGridSpec(
            num_scalar_prefetch=1,
            grid=(MP // WAVES,),
            in_specs=[
                full(N_LAT, MP, 384),
                pl.BlockSpec((WAVES, KP, HALF), lambda i, w: (jnp.minimum(i, MH // WAVES - 1), 0, 0)),
                pl.BlockSpec((WAVES, KP, HALF), lambda i, w: (jnp.maximum(i - MH // WAVES, 0), 0, 0)),
                full(8, 768),
            ],
            out_specs=(full(GROUP, OWNED, 2 * M), full(N_LAT, MP, 384)),
            scratch_shapes=[
                pltpu.VMEM((2, 16 * SLAB, 128), F32),
                pltpu.VMEM((3, 8 * SLAB, 128), F32),
                pltpu.VMEM((4, 8 * SLAB, 128), F32),
                pltpu.VMEM((6 * MP, HALF), BF),
            ],
        ),
        out_shape=(
            pltpu.HBM((GROUP, OWNED, 2 * M), F32),
            pltpu.HBM((N_LAT, MP, 384), BF),
        ),
        compiler_params=pltpu.CompilerParams(vmem_limit_bytes=24 * 2**20),
        cost_estimate=pl.CostEstimate(flops=4 * 10**9, bytes_accessed=10**7, transcendentals=0),
        name="spectral_step",
    )(waves, coeffs, hbm(table0), hbm(table1), gain)


def per_device(
    state, conv_in, bias_in, conv_out, bias_out, spectral_gain, mix_in, blend_bias, mix_out, mix_out_bias, level_order, wave_order
):
    trig, quad, lat_rows, start = constants()
    band = lax.axis_index("lat")
    columns = state.reshape(VARS * LV, COLUMNS)

    tendency = first_conv(columns, conv_in.transpose(1, 2, 0), bias_in, conv_out.transpose(1, 0, 2), bias_out, level_order)
    tendency, wave_order, spectral_gain = lax.optimization_barrier((tendency, wave_order, spectral_gain))
    pieces = lax.all_to_all(tendency.reshape(N_LON, GROUP, TILES, 128), "lon", 0, 0, tiled=True)

    grouped = jnp.pad(wave_order.reshape(N_LAT, OWNED), ((0, 0), (0, MP - OWNED)), constant_values=-1)
    chosen = (grouped.reshape(N_LAT * MP)[:, None] == jnp.arange(M, dtype=jnp.int32)[None, :]).astype(BF)
    tables = dot(chosen, jnp.asarray(trig[:, : 2 * NLON])).astype(BF)
    owned = lax.dynamic_slice_in_dim(grouped, band, 1, 0)[0]
    waves_f = jnp.where(owned < 0, 1000, owned).astype(F32)[:, None]
    lat_rows, start = jnp.asarray(lat_rows), jnp.asarray(start)
    band_quad = lax.dynamic_slice_in_dim(jnp.asarray(quad), band, 1, 0)[0]
    gain = jnp.broadcast_to(jnp.pad(spectral_gain, (0, 768 - M))[None], (8, 768))
    owned = jnp.maximum(owned, 0)
    table0 = legendre_table(waves_f[:MH], lat_rows, start)
    pieces, table0, tables, gain, owned = lax.optimization_barrier((pieces, table0, tables, gain, owned))

    coeffs = forward_fourier(pieces, tables, band_quad)
    coeffs, waves_late, chosen = lax.optimization_barrier((coeffs, waves_f[MH:], chosen))
    coeffs = lax.all_to_all(coeffs, "lat", 0, 0, tiled=True)
    table1 = legendre_table(waves_late, lat_rows, start)
    inverse_tables = dot(chosen, jnp.asarray(trig[:, 2 * NLON :])).astype(BF)
    coeffs, table1, inverse_tables = lax.optimization_barrier((coeffs, table1, inverse_tables))

    spectrum, returned = spectral_step(owned, coeffs, table0, table1, gain)
    returned, mix_in, blend_bias, mix_out, mix_out_bias, level_order = lax.optimization_barrier(
        (returned, mix_in, blend_bias, mix_out, mix_out_bias, level_order)
    )
    returned = lax.all_to_all(returned, "lat", 0, 0, tiled=True)
    m1, m2, mb = second_weights(mix_in.transpose(1, 2, 0), blend_bias, mix_out.transpose(1, 0, 2), mix_out_bias, level_order)
    returned, m1, m2, mb = lax.optimization_barrier((returned, m1, m2, mb))
    grid_values = inverse_fourier(returned.reshape(N_LAT * MP, 384), inverse_tables)
    filtered = lax.all_to_all(grid_values, "lon", 0, 0, tiled=True)
    increment = second_conv(columns, filtered.reshape(ITEMS, TILES, 128), m1, m2, mb)
    return spectrum, increment.reshape(1, VARS, LV, COLUMNS)


def solution(mesh):
    return jax.shard_map(
        per_device,
        mesh=mesh,
        in_specs=(P(None, None, None, ("lat", "lon")),) + (P(),) * 11,
        out_specs=(P("lon", "lat", None), P(None, None, None, ("lat", "lon"))),
        check_vma=False,
    )
```

```python
import functools
import math

import jax
import jax.numpy as jnp
import ml_dtypes
import numpy as np
from jax import lax
from jax.experimental import pallas as pl
from jax.experimental.pallas import tpu as pltpu
from jax.sharding import PartitionSpec as P

NLAT, NLON, M = 512, 1024, 344
LV, VARS, CH, FIELDS = 24, 6, 64, 2
N_LAT, N_LON = 8, 16
ROWS, COLS = NLAT // N_LAT, NLON // N_LON
COLUMNS = ROWS * COLS
TILES = COLUMNS // 128
ITEMS = FIELDS * LV
GROUP = ITEMS // N_LON
OWNED = M // N_LAT
MP = 48
MH = MP // 2
KP = 352
HALF = NLAT // 2
HID = CH * LV
SLAB = 49
BF, F32 = jnp.bfloat16, jnp.float32
NT = (((1,), (1,)), ((), ()))

BLOCKS = {(0, 0): (0, 0), (0, 1): (0, 1), (1, 0): (0, 2), (1, 1): (1, 2), (2, 0): (1, 0), (2, 1): (1, 1)}


def slab_of(tile, half):
    part, item = BLOCKS[(tile, half)]
    return part * GROUP + item


def iota(shape, dim):
    return lax.broadcasted_iota(jnp.int32, shape, dim)


def over_levels(index):
    return jnp.floor((index.astype(F32) + 0.5) * (1.0 / LV)).astype(jnp.int32)


def hbm(x):
    return pltpu.with_memory_space_constraint(x, pltpu.HBM)


def dot(a, b):
    return jnp.dot(a, b, preferred_element_type=F32)


def row_order():
    slots = np.arange(ROWS)
    return 2 * (slots % (ROWS // 2)) + slots // (ROWS // 2)


@functools.lru_cache(None)
def constants():
    n = np.arange(M)[:, None]
    angle = 2 * np.pi * ((n * np.arange(NLON)[None, :]) % NLON) / NLON
    factor = np.where(n == 0, 1.0, 2.0) / math.sqrt(NLAT * NLON)
    trig = np.concatenate(
        [np.cos(angle) / math.sqrt(NLON), np.sin(angle) / math.sqrt(NLON), np.cos(angle) * factor, np.sin(angle) * factor],
        axis=1,
    ).astype(ml_dtypes.bfloat16)
    slots = np.arange(NLAT)
    lat = (slots // ROWS) * ROWS + row_order()[slots % ROWS]
    phi = np.pi * (lat + 0.5) / NLAT - np.pi / 2
    sine, cosine = np.sin(phi), np.cos(phi)
    quad = (np.pi * cosine / math.sqrt(NLAT)).reshape(N_LAT, 1, ROWS)
    quad = np.tile(quad, (1, 1, 2 * GROUP)).astype(np.float32)
    lat_rows = np.zeros((8, HALF), np.float32)
    lat_rows[0], lat_rows[1] = sine[:HALF], np.log(cosine[:HALF])
    start = np.zeros((1, 384), np.float32)
    start[0, :M] = [
        0.5 * math.log(0.5) + 0.5 * (math.lgamma(m + 1.5) - math.lgamma(m + 1.0) - math.lgamma(1.5)) for m in range(M)
    ]
    return trig, quad, lat_rows, start


def to_column(row):
    n = row.shape[1]
    return jnp.sum(jnp.where(iota((n, n), 0) == iota((n, n), 1), row, jnp.zeros_like(row)), axis=1, keepdims=True)


def make_weights(w1_ref, bias1_ref, w2_ref, order_ref, bias2_ref, slots_in, o1_ref, o2_ref, ob_ref):
    width, rows = o1_ref.shape[1], o2_ref.shape[0]
    variables, fields = w1_ref.shape[1], w2_ref.shape[1]
    order = order_ref[...]
    base = VARS * LV
    column = iota((1, width), 1)
    var_col = over_levels(column)
    level_col = column - LV * var_col
    if slots_in:
        wide_order = jnp.concatenate([jnp.zeros((1, base), jnp.int32), order, jnp.zeros((1, width - base - ITEMS), jnp.int32)], axis=1)
        slot_field = (wide_order >= LV).astype(jnp.int32)
        var_col = jnp.where(column < base, var_col + FIELDS, slot_field)
        level_col = jnp.where(column < base, level_col, wide_order - LV * slot_field)
    level_col = jnp.where(column < width - 16, level_col, -100)
    r = iota((HID, CH), 0)
    spread = (over_levels(r) == iota((HID, CH), 1)).astype(F32).astype(BF)
    level_row = iota((HID, width), 0)
    level_row = level_row - LV * over_levels(level_row)
    total = jnp.zeros((HID, width), F32)
    pick = (iota((variables, width), 0) == var_col).astype(F32).astype(BF)
    for tap in range(3):
        tall = lax.dot_general(spread, w1_ref[tap], NT, preferred_element_type=F32)
        wide = dot((0.5 * tall).astype(BF), pick)
        total = jnp.where(level_col == level_row + 2 * (tap - 1), wide, total)
    bias = 0.5 * to_column(bias1_ref[...])
    high = bias.astype(BF).astype(F32)
    low = bias - high
    block = jnp.where(column == width - 16, high, jnp.where(column == width - 15, low, 0.0)).astype(BF)
    o1_ref[...] = (total + dot(spread, block)).astype(BF)
    if slots_in:
        row = iota((rows, 1), 0)
        field_row = over_levels(row)
    else:
        row = to_column(order.astype(F32)).astype(jnp.int32)
        field_row = (row >= LV).astype(jnp.int32)
    level_out = row - LV * field_row
    c = iota((CH, HID), 1)
    spread2 = (over_levels(c) == iota((CH, HID), 0)).astype(F32).astype(BF)
    level_hid = iota((rows, HID), 1)
    level_hid = level_hid - LV * over_levels(level_hid)
    total2 = jnp.zeros((rows, HID), F32)
    bias2 = jnp.zeros((rows, 128), F32)
    for tap in range(3):
        block = jnp.zeros((rows, CH), F32)
        for field in range(fields):
            block = jnp.where(field_row == field, w2_ref[tap].astype(F32)[field : field + 1, :], block)
        wide = dot(block.astype(BF), spread2)
        total2 = jnp.where(level_hid == level_out + 2 * (tap - 1), wide, total2)
    o2_ref[...] = total2.astype(BF)
    for field in range(fields):
        bias2 = jnp.where(field_row == field, bias2_ref[0:1, field : field + 1], bias2)
    ob_ref[...] = bias2


def weights_kernel(w1_ref, bias1_ref, w2_ref, order_ref, bias2_ref, o1_ref, o2_ref, ob_ref):
    make_weights(w1_ref, bias1_ref, w2_ref, order_ref, bias2_ref, True, o1_ref, o2_ref, ob_ref)


def second_weights(w1, bias1, w2, bias2, order):
    full = lambda *shape: pl.BlockSpec(shape, lambda i: (0,) * len(shape))
    width, rows = VARS * LV + ITEMS + 16, VARS * LV
    return pl.pallas_call(
        weights_kernel,
        out_shape=(
            pltpu.HBM((HID, width), BF),
            pltpu.HBM((rows, HID), BF),
            pltpu.HBM((rows, 128), F32),
        ),
        grid=(1,),
        in_specs=[full(*w1.shape), full(1, CH), full(*w2.shape), full(1, ITEMS), full(1, bias2.shape[0])],
        out_specs=(full(HID, width), full(rows, HID), full(rows, 128)),
        compiler_params=pltpu.CompilerParams(vmem_limit_bytes=20 * 2**20),
        cost_estimate=pl.CostEstimate(flops=2 * 10**8, bytes_accessed=2 * 10**6, transcendentals=0),
        name="second_weights",
    )(hbm(w1), hbm(bias1.reshape(1, CH)), hbm(w2), hbm(order.reshape(1, ITEMS)), hbm(bias2.reshape(1, -1)))


def hidden_layer(w1_ref, w2_ref, v_ref, h_ref):
    block = v_ref.shape[1]
    step, tall = 256, HID // 2
    c1, c2 = 2 * math.sqrt(2 / math.pi), 8 * 0.044715 * math.sqrt(2 / math.pi)
    results = []
    for col in range(0, block, step):
        cols = slice(col, col + step)
        for row in range(0, HID, tall):
            y = dot(w1_ref[row : row + tall, :], v_ref[:, cols])
            u = y * (c1 + c2 * (y * y))
            h_ref[row : row + tall, cols] = (y + y * jnp.tanh(u)).astype(BF)
        results.append(dot(w2_ref[...], h_ref[:, cols]))
    return jnp.concatenate(results, axis=1)


def first_kernel(
    block, state_ref, c1_ref, bias1_ref, c2_ref, order_ref, bias2_ref, out_ref, w1_ref, w2_ref, b2_ref, v_ref, h_ref, o_ref
):
    step = pl.program_id(0)

    @pl.when(step == 0)
    def _():
        make_weights(c1_ref, bias1_ref, c2_ref, order_ref, bias2_ref, False, w1_ref, w2_ref, b2_ref)
        v_ref[VARS * LV :, :] = jnp.ones((16, block), BF)

    v_ref[: VARS * LV, :] = state_ref[...]
    result = hidden_layer(w1_ref, w2_ref, v_ref, h_ref)
    bias = b2_ref[...]
    for tile in range(block // 128):
        o_ref[pl.ds(step * (block // 128) + tile, ITEMS, stride=TILES + 1), :] = result[:, tile * 128 : (tile + 1) * 128] + bias

    @pl.when(step == pl.num_programs(0) - 1)
    def _():
        for item in range(ITEMS):
            out_ref[item] = o_ref[item * (TILES + 1) : item * (TILES + 1) + TILES, :].astype(BF)


def first_conv(state, w1, bias1, w2, bias2, order, block=1024):
    full = lambda *shape: pl.BlockSpec(shape, lambda i: (0,) * len(shape))
    return pl.pallas_call(
        functools.partial(first_kernel, block),
        grid=(COLUMNS // block,),
        out_shape=pltpu.HBM((ITEMS, TILES, 128), BF),
        in_specs=[
            pl.BlockSpec((VARS * LV, block), lambda i: (0, i)),
            full(*w1.shape),
            full(1, CH),
            full(*w2.shape),
            full(1, ITEMS),
            full(1, bias2.shape[0]),
        ],
        out_specs=full(ITEMS, TILES, 128),
        scratch_shapes=[
            pltpu.VMEM((HID, VARS * LV + 16), BF),
            pltpu.VMEM((ITEMS, HID), BF),
            pltpu.VMEM((ITEMS, 128), F32),
            pltpu.VMEM((VARS * LV + 16, block), BF),
            pltpu.VMEM((HID, block), BF),
            pltpu.VMEM((ITEMS * (TILES + 1), 128), F32),
        ],
        compiler_params=pltpu.CompilerParams(vmem_limit_bytes=24 * 2**20),
        cost_estimate=pl.CostEstimate(flops=3 * 10**9, bytes_accessed=2 * 10**6, transcendentals=HID * COLUMNS),
        name="first_conv",
    )(hbm(state), hbm(w1), hbm(bias1.reshape(1, CH)), hbm(w2), hbm(order.reshape(1, ITEMS)), hbm(bias2.reshape(1, -1)))


def second_kernel(block, state_ref, filt_ref, w1_ref, w2_ref, b2_ref, out_ref, v_ref, h_ref, f_ref):
    step = pl.program_id(0)
    base = VARS * LV

    @pl.when(step == 0)
    def _():
        v_ref[base + ITEMS :, :] = jnp.ones((16, block), BF)
        for item in range(ITEMS):
            f_ref[item * (TILES + 1) : item * (TILES + 1) + TILES, :] = filt_ref[item].astype(F32)

    v_ref[:base, :] = state_ref[...]
    for tile in range(block // 128):
        piece = f_ref[pl.ds(step * (block // 128) + tile, ITEMS, stride=TILES + 1), :]
        v_ref[base : base + ITEMS, tile * 128 : (tile + 1) * 128] = piece.astype(BF)
    result = hidden_layer(w1_ref, w2_ref, v_ref, h_ref)
    bias = b2_ref[...]
    for tile in range(block // 128):
        out_ref[:, tile * 128 : (tile + 1) * 128] = result[:, tile * 128 : (tile + 1) * 128] + bias


def second_conv(state, filtered, w1, w2, b2, block=1024):
    full = lambda *shape: pl.BlockSpec(shape, lambda i: (0,) * len(shape))
    width = VARS * LV + ITEMS + 16
    return pl.pallas_call(
        functools.partial(second_kernel, block),
        grid=(COLUMNS // block,),
        out_shape=pltpu.HBM((VARS * LV, COLUMNS), F32),
        in_specs=[
            pl.BlockSpec((VARS * LV, block), lambda i: (0, i)),
            full(ITEMS, TILES, 128),
            full(HID, width),
            full(VARS * LV, HID),
            full(VARS * LV, 128),
        ],
        out_specs=pl.BlockSpec((VARS * LV, block), lambda i: (0, i)),
        scratch_shapes=[
            pltpu.VMEM((width, block), BF),
            pltpu.VMEM((HID, block), BF),
            pltpu.VMEM((ITEMS * (TILES + 1), 128), F32),
        ],
        compiler_params=pltpu.CompilerParams(vmem_limit_bytes=24 * 2**20),
        cost_estimate=pl.CostEstimate(flops=4 * 10**9, bytes_accessed=4 * 10**6, transcendentals=HID * COLUMNS),
        name="second_conv",
    )(hbm(state), filtered, w1, w2, b2)


CHUNK = 176
STRIDE = CHUNK + 1


def table_kernel(wave_ref, lat_ref, start_ref, out_ref, now_ref, old_ref, log_ref, ratio_ref, s_ref):
    step = pl.program_id(0)
    wave = jnp.broadcast_to(wave_ref[...], (MH, 128))
    sine = [lat_ref[0:1, 128 * h : 128 * h + 128] for h in range(2)]

    @pl.when(step == 0)
    def _():
        match = iota((MH, 384), 1).astype(F32) == wave_ref[...]
        start = jnp.sum(jnp.where(match, start_ref[...], 0.0), axis=1, keepdims=True)
        for h in range(2):
            log_cos = lat_ref[1:2, 128 * h : 128 * h + 128]
            log_ref[h] = jnp.where(wave > 500.0, -1e4, start + wave * log_cos)
            now_ref[h] = jnp.zeros((MH, 128), F32)
            old_ref[h] = jnp.zeros((MH, 128), F32)
        ratio_ref[...] = jnp.zeros((MH, 128), F32)

    now = [now_ref[h] for h in range(2)]
    old = [old_ref[h] for h in range(2)]
    log_scale = [log_ref[h] for h in range(2)]
    ratio = ratio_ref[...]
    scale = [None, None]
    first = (step * CHUNK).astype(F32)
    for kk in range(CHUNK):
        if kk % 8 == 0:
            for h in range(2):
                big = jnp.abs(now[h]) > 1e8
                shrink = jnp.where(big, 1e-12, 1.0)
                now[h] = now[h] * shrink
                old[h] = old[h] * shrink
                log_scale[h] = log_scale[h] + jnp.where(big, math.log(1e12), 0.0)
                scale[h] = jnp.exp(log_scale[h])
        k = first + kk
        n = wave + k
        top = 4.0 * (n * n) - 1.0
        bottom = k * (wave + n)
        root = lax.rsqrt(jnp.maximum(top * bottom, 1e-30))
        up = jnp.where(n <= M - 1.0, top * root, 0.0)
        for h in range(2):
            stepped = up * (sine[h] * now[h] - ratio * old[h])
            if kk == 0:
                stepped = jnp.where(step == 0, 1.0, stepped)
            old[h], now[h] = now[h], stepped
            s_ref[h, pl.ds(kk, MH, stride=STRIDE), :] = stepped * scale[h]
        ratio = bottom * root
    for h in range(2):
        now_ref[h], old_ref[h], log_ref[h] = now[h], old[h], log_scale[h]
    ratio_ref[...] = ratio
    for m in range(MH):
        for h in range(2):
            out_ref[m, :, 128 * h : 128 * h + 128] = s_ref[h, m * STRIDE : m * STRIDE + CHUNK, :].astype(BF)


def legendre_table(waves_f, lat_rows, start):
    full = lambda *shape: pl.BlockSpec(shape, lambda i: (0,) * len(shape))
    return pl.pallas_call(
        table_kernel,
        grid=(KP // CHUNK,),
        out_shape=pltpu.HBM((MH, KP, HALF), BF),
        in_specs=[full(MH, 1), full(8, HALF), full(1, 384)],
        out_specs=pl.BlockSpec((MH, CHUNK, HALF), lambda i: (0, i, 0)),
        scratch_shapes=[pltpu.VMEM((2, MH, 128), F32)] * 3
        + [pltpu.VMEM((MH, 128), F32), pltpu.VMEM((2, MH * STRIDE, 128), F32)],
        compiler_params=pltpu.CompilerParams(vmem_limit_bytes=20 * 2**20),
        cost_estimate=pl.CostEstimate(flops=2 * 10**8, bytes_accessed=9 * 10**6, transcendentals=0),
        name="legendre_table",
    )(waves_f, lat_rows, start)


def swap_halves(x):
    return pltpu.roll(x, 64, 1)


def forward_kernel(y_ref, f_ref, g_ref, q_ref, out_ref, x0_ref, x1_ref):
    low = iota((TILES, 128), 1) < 64
    x0_ref[192:256, :] = jnp.zeros((64, NLON), BF)
    x1_ref[0:64, :] = jnp.zeros((64, NLON), BF)
    place0, place1 = (0, 64, 128), (128, 192, 64)
    for pair in range(N_LON // 2):
        for item in range(GROUP):
            a = y_ref[2 * pair, item].astype(F32)
            b = y_ref[2 * pair + 1, item].astype(F32)
            even = jnp.where(low, a, swap_halves(b)).astype(BF)
            odd = jnp.where(low, swap_halves(a), b).astype(BF)
            lanes = slice(128 * pair, 128 * pair + 128)
            for ref, place in ((x0_ref, place0), (x1_ref, place1)):
                ref[place[item] : place[item] + 32, lanes] = even
                ref[place[item] + 32 : place[item] + 64, lanes] = odd
    quad = q_ref[...]
    cosines = lax.dot_general(f_ref[...], x0_ref[...], NT, preferred_element_type=F32)
    sines = lax.dot_general(g_ref[...], x1_ref[...], NT, preferred_element_type=F32)
    tiles = (cosines[:, :128], cosines[:, 128:] + sines[:, :128], sines[:, 128:])
    for t, value in enumerate(tiles):
        value = (value * quad[:, 128 * t : 128 * t + 128]).astype(BF)
        for group in range(N_LAT):
            out_ref[group, :, 128 * t : 128 * t + 128] = value[group * MP : (group + 1) * MP]


def forward_fourier(pieces, tables, quad):
    full = lambda *shape: pl.BlockSpec(shape, lambda i: (0,) * len(shape))
    return pl.pallas_call(
        forward_kernel,
        grid=(1,),
        out_shape=pltpu.HBM((N_LAT, MP, 384), BF),
        in_specs=[
            full(N_LON, GROUP, TILES, 128),
            pl.BlockSpec((N_LAT * MP, NLON), lambda i: (0, 0)),
            pl.BlockSpec((N_LAT * MP, NLON), lambda i: (0, 1)),
            full(1, 384),
        ],
        out_specs=full(N_LAT, MP, 384),
        scratch_shapes=[pltpu.VMEM((256, NLON), BF)] * 2,
        compiler_params=pltpu.CompilerParams(vmem_limit_bytes=20 * 2**20),
        cost_estimate=pl.CostEstimate(flops=4 * 10**8, bytes_accessed=3 * 10**6, transcendentals=0),
        name="forward_fourier",
    )(pieces, tables, tables, quad)


def inverse_kernel(r_ref, f_ref, g_ref, out_ref):
    turned = [r_ref[:, 128 * t : 128 * t + 128].astype(F32).T.astype(BF) for t in range(3)]
    cosines = jnp.concatenate([turned[0], turned[1][:64]], axis=0)
    sines = jnp.concatenate([turned[2], turned[1][64:]], axis=0)
    grid = dot(cosines, f_ref[...]) + dot(sines, g_ref[...])
    low = iota((TILES, 128), 1) < 64
    for pair in range(N_LON // 2):
        for item in range(GROUP):
            lanes = slice(128 * pair, 128 * pair + 128)
            even = grid[64 * item : 64 * item + 32, lanes]
            odd = grid[64 * item + 32 : 64 * item + 64, lanes]
            out_ref[2 * pair, item] = jnp.where(low, even, swap_halves(odd)).astype(BF)
            out_ref[2 * pair + 1, item] = jnp.where(low, swap_halves(even), odd).astype(BF)


def inverse_fourier(returned, tables):
    full = lambda *shape: pl.BlockSpec(shape, lambda i: (0,) * len(shape))
    return pl.pallas_call(
        inverse_kernel,
        grid=(1,),
        out_shape=pltpu.HBM((N_LON, GROUP, TILES, 128), BF),
        in_specs=[
            full(N_LAT * MP, 384),
            pl.BlockSpec((N_LAT * MP, NLON), lambda i: (0, 0)),
            pl.BlockSpec((N_LAT * MP, NLON), lambda i: (0, 1)),
        ],
        out_specs=full(N_LON, GROUP, TILES, 128),
        compiler_params=pltpu.CompilerParams(vmem_limit_bytes=20 * 2**20),
        cost_estimate=pl.CostEstimate(flops=4 * 10**8, bytes_accessed=3 * 10**6, transcendentals=0),
        name="inverse_fourier",
    )(returned, tables, tables)


WAVES = 8


def spectral_kernel(wave_ref, x_ref, t0_ref, t1_ref, gain_ref, spec_ref, out_ref, c_ref, n_ref, r_ref, m_ref):
    step = pl.program_id(0)
    low = iota((MP, 128), 1) < 64
    mirror = (iota((HALF, HALF), 0) + iota((HALF, HALF), 1) == HALF - 1).astype(F32).astype(BF)

    @pl.when(step == 0)
    def _():
        for slab in (6, 7, 14, 15):
            for h in range(2):
                c_ref[h, slab * SLAB : slab * SLAB + MP, :] = jnp.zeros((MP, 128), F32)
        north = {}
        for pair in range(N_LAT // 2):
            for tile in range(3):
                a = x_ref[2 * pair, :, 128 * tile : 128 * tile + 128].astype(F32)
                b = x_ref[2 * pair + 1, :, 128 * tile : 128 * tile + 128].astype(F32)
                both = jnp.where(low, a, swap_halves(b)), jnp.where(low, swap_halves(a), b)
                for half in range(2):
                    slab = slab_of(tile, half)
                    if pair < 2:
                        c_ref[pair, slab * SLAB : slab * SLAB + MP, :] = both[half]
                    else:
                        m_ref[slab * MP : slab * MP + MP, 128 * (pair - 2) : 128 * (pair - 2) + 128] = both[half].astype(BF)
        turned = dot(m_ref[...], mirror)
        for slab in range(6):
            for h in range(2):
                a = c_ref[h, slab * SLAB : slab * SLAB + MP, :]
                b = turned[slab * MP : slab * MP + MP, 128 * h : 128 * h + 128]
                c_ref[h, slab * SLAB : slab * SLAB + MP, :] = a + b
                c_ref[h, (8 + slab) * SLAB : (8 + slab) * SLAB + MP, :] = a - b

    even = iota((8, KP), 1) % 2 == 0
    gain = gain_ref[...]

    def waves(t_ref):
        for mm in range(WAVES):
            m = step * WAVES + mm
            left = jnp.concatenate([c_ref[h, pl.ds(m, 16, stride=SLAB), :] for h in range(2)], axis=1).astype(BF)
            table = t_ref[mm]
            both = lax.dot_general(left, table, NT, preferred_element_type=F32)
            natural = jnp.where(even, both[:8], both[8:])
            n_ref[0, pl.ds(m, 8, stride=SLAB), :] = natural[:, :128]
            n_ref[1, pl.ds(m, 8, stride=SLAB), :] = natural[:, 128:256]
            n_ref[2, pl.ds(m, 8, stride=SLAB), :] = jnp.concatenate([natural[:, 256:], jnp.zeros((8, 384 - KP), F32)], axis=1)
            scaled = natural * pltpu.roll(gain, 768 - wave_ref[m], 1)[:, :KP]
            right = jnp.concatenate([jnp.where(even, scaled, 0.0), jnp.where(even, 0.0, scaled)], axis=0).astype(BF)
            back = dot(right, table)
            north, south = back[:8] + back[8:], back[:8] - back[8:]
            for h in range(2):
                r_ref[h, pl.ds(m, 8, stride=SLAB), :] = north[:, 128 * h : 128 * h + 128]
                r_ref[2 + h, pl.ds(m, 8, stride=SLAB), :] = south[:, 128 * h : 128 * h + 128]

    pl.when(step < MH // WAVES)(lambda: waves(t0_ref))
    pl.when(step >= MH // WAVES)(lambda: waves(t1_ref))

    @pl.when(step == pl.num_programs(0) - 1)
    def _():
        for slab in range(6):
            for h in range(2):
                m_ref[slab * MP : slab * MP + MP, 128 * h : 128 * h + 128] = r_ref[2 + h, slab * SLAB : slab * SLAB + MP, :].astype(BF)
        turned = dot(m_ref[...], mirror)

        def tile_of(slab, j):
            if j < 2:
                return r_ref[j, slab * SLAB : slab * SLAB + MP, :]
            return turned[slab * MP : slab * MP + MP, 128 * (j - 2) : 128 * (j - 2) + 128]

        for pair in range(N_LAT // 2):
            for tile in range(3):
                a = tile_of(slab_of(tile, 0), pair)
                b = tile_of(slab_of(tile, 1), pair)
                lanes = slice(128 * tile, 128 * tile + 128)
                out_ref[2 * pair, :, lanes] = jnp.where(low, a, swap_halves(b)).astype(BF)
                out_ref[2 * pair + 1, :, lanes] = jnp.where(low, swap_halves(a), b).astype(BF)
        wide = iota((MP, 768), 1) < M
        zeros = jnp.zeros((MP, 384), F32)
        for item in range(GROUP):
            parts = []
            for part in range(2):
                at = (part * GROUP + item) * SLAB
                parts.append(jnp.concatenate([n_ref[h, at : at + MP, :] for h in range(3)] + [zeros], axis=1))
            value = jnp.where(wide, parts[0], pltpu.roll(parts[1], M, 1))
            spec_ref[item] = value[:OWNED, : 2 * M]


def spectral_step(waves, coeffs, table0, table1, gain):
    full = lambda *shape: pl.BlockSpec(shape, lambda i, w: (0,) * len(shape))
    return pl.pallas_call(
        spectral_kernel,
        grid_spec=pltpu.PrefetchScalarGridSpec(
            num_scalar_prefetch=1,
            grid=(MP // WAVES,),
            in_specs=[
                full(N_LAT, MP, 384),
                pl.BlockSpec((WAVES, KP, HALF), lambda i, w: (jnp.minimum(i, MH // WAVES - 1), 0, 0)),
                pl.BlockSpec((WAVES, KP, HALF), lambda i, w: (jnp.maximum(i - MH // WAVES, 0), 0, 0)),
                full(8, 768),
            ],
            out_specs=(full(GROUP, OWNED, 2 * M), full(N_LAT, MP, 384)),
            scratch_shapes=[
                pltpu.VMEM((2, 16 * SLAB, 128), F32),
                pltpu.VMEM((3, 8 * SLAB, 128), F32),
                pltpu.VMEM((4, 8 * SLAB, 128), F32),
                pltpu.VMEM((6 * MP, HALF), BF),
            ],
        ),
        out_shape=(
            pltpu.HBM((GROUP, OWNED, 2 * M), F32),
            pltpu.HBM((N_LAT, MP, 384), BF),
        ),
        compiler_params=pltpu.CompilerParams(vmem_limit_bytes=24 * 2**20),
        cost_estimate=pl.CostEstimate(flops=4 * 10**9, bytes_accessed=10**7, transcendentals=0),
        name="spectral_step",
    )(waves, coeffs, hbm(table0), hbm(table1), gain)


def per_device(
    state, conv_in, bias_in, conv_out, bias_out, spectral_gain, mix_in, blend_bias, mix_out, mix_out_bias, level_order, wave_order
):
    trig, quad, lat_rows, start = constants()
    band = lax.axis_index("lat")
    columns = state.reshape(VARS * LV, COLUMNS)

    tendency = first_conv(columns, conv_in.transpose(1, 2, 0), bias_in, conv_out.transpose(1, 0, 2), bias_out, level_order)
    tendency, wave_order, spectral_gain = lax.optimization_barrier((tendency, wave_order, spectral_gain))
    pieces = lax.all_to_all(tendency.reshape(N_LON, GROUP, TILES, 128), "lon", 0, 0, tiled=True)

    grouped = jnp.pad(wave_order.reshape(N_LAT, OWNED), ((0, 0), (0, MP - OWNED)), constant_values=-1)
    chosen = (grouped.reshape(N_LAT * MP)[:, None] == jnp.arange(M, dtype=jnp.int32)[None, :]).astype(BF)
    tables = dot(chosen, jnp.asarray(trig[:, : 2 * NLON])).astype(BF)
    owned = lax.dynamic_slice_in_dim(grouped, band, 1, 0)[0]
    waves_f = jnp.where(owned < 0, 1000, owned).astype(F32)[:, None]
    lat_rows, start = jnp.asarray(lat_rows), jnp.asarray(start)
    band_quad = lax.dynamic_slice_in_dim(jnp.asarray(quad), band, 1, 0)[0]
    gain = jnp.broadcast_to(jnp.pad(spectral_gain, (0, 768 - M))[None], (8, 768))
    owned = jnp.maximum(owned, 0)
    table0 = legendre_table(waves_f[:MH], lat_rows, start)
    pieces, table0, tables, gain, owned = lax.optimization_barrier((pieces, table0, tables, gain, owned))

    coeffs = forward_fourier(pieces, tables, band_quad)
    coeffs, waves_late, chosen = lax.optimization_barrier((coeffs, waves_f[MH:], chosen))
    coeffs = lax.all_to_all(coeffs, "lat", 0, 0, tiled=True)
    table1 = legendre_table(waves_late, lat_rows, start)
    inverse_tables = dot(chosen, jnp.asarray(trig[:, 2 * NLON :])).astype(BF)
    coeffs, table1, inverse_tables = lax.optimization_barrier((coeffs, table1, inverse_tables))

    spectrum, returned = spectral_step(owned, coeffs, table0, table1, gain)
    returned, mix_in, blend_bias, mix_out, mix_out_bias, level_order = lax.optimization_barrier(
        (returned, mix_in, blend_bias, mix_out, mix_out_bias, level_order)
    )
    returned = lax.all_to_all(returned, "lat", 0, 0, tiled=True)
    m1, m2, mb = second_weights(mix_in.transpose(1, 2, 0), blend_bias, mix_out.transpose(1, 0, 2), mix_out_bias, level_order)
    returned, m1, m2, mb = lax.optimization_barrier((returned, m1, m2, mb))
    grid_values = inverse_fourier(returned.reshape(N_LAT * MP, 384), inverse_tables)
    filtered = lax.all_to_all(grid_values, "lon", 0, 0, tiled=True)
    increment = second_conv(columns, filtered.reshape(ITEMS, TILES, 128), m1, m2, mb)
    return spectrum, increment.reshape(1, VARS, LV, COLUMNS)


def solution(mesh):
    return jax.shard_map(
        per_device,
        mesh=mesh,
        in_specs=(P(None, None, None, ("lat", "lon")),) + (P(),) * 11,
        out_specs=(P("lon", "lat", None), P(None, None, None, ("lat", "lon"))),
        check_vma=False,
    )
```

```python
import functools
import math

import jax
import jax.numpy as jnp
import ml_dtypes
import numpy as np
from jax import lax
from jax.experimental import pallas as pl
from jax.experimental.pallas import tpu as pltpu
from jax.sharding import PartitionSpec as P

NLAT, NLON, M = 512, 1024, 344
LV, VARS, CH, FIELDS = 24, 6, 64, 2
N_LAT, N_LON = 8, 16
ROWS, COLS = NLAT // N_LAT, NLON // N_LON
COLUMNS = ROWS * COLS
TILES = COLUMNS // 128
ITEMS = FIELDS * LV
GROUP = ITEMS // N_LON
OWNED = M // N_LAT
MP = 48
MH = MP // 2
KP = 352
HALF = NLAT // 2
HID = CH * LV
SLAB = 49
BF, F32 = jnp.bfloat16, jnp.float32
NT = (((1,), (1,)), ((), ()))

BLOCKS = {(0, 0): (0, 0), (0, 1): (0, 1), (1, 0): (0, 2), (1, 1): (1, 2), (2, 0): (1, 0), (2, 1): (1, 1)}


def slab_of(tile, half):
    part, item = BLOCKS[(tile, half)]
    return part * GROUP + item


def iota(shape, dim):
    return lax.broadcasted_iota(jnp.int32, shape, dim)


def over_levels(index):
    return jnp.floor((index.astype(F32) + 0.5) * (1.0 / LV)).astype(jnp.int32)


def hbm(x):
    return pltpu.with_memory_space_constraint(x, pltpu.HBM)


def dot(a, b):
    return jnp.dot(a, b, preferred_element_type=F32)


def row_order():
    slots = np.arange(ROWS)
    return 2 * (slots % (ROWS // 2)) + slots // (ROWS // 2)


@functools.lru_cache(None)
def constants():
    n = np.arange(M)[:, None]
    angle = 2 * np.pi * ((n * np.arange(NLON)[None, :]) % NLON) / NLON
    factor = np.where(n == 0, 1.0, 2.0) / math.sqrt(NLAT * NLON)
    trig = np.concatenate(
        [np.cos(angle) / math.sqrt(NLON), np.sin(angle) / math.sqrt(NLON), np.cos(angle) * factor, np.sin(angle) * factor],
        axis=1,
    ).astype(ml_dtypes.bfloat16)
    slots = np.arange(NLAT)
    lat = (slots // ROWS) * ROWS + row_order()[slots % ROWS]
    phi = np.pi * (lat + 0.5) / NLAT - np.pi / 2
    sine, cosine = np.sin(phi), np.cos(phi)
    quad = (np.pi * cosine / math.sqrt(NLAT)).reshape(N_LAT, 1, ROWS)
    quad = np.tile(quad, (1, 1, 2 * GROUP)).astype(np.float32)
    lat_rows = np.zeros((8, HALF), np.float32)
    lat_rows[0], lat_rows[1] = sine[:HALF], np.log(cosine[:HALF])
    start = np.zeros((1, 384), np.float32)
    start[0, :M] = [
        0.5 * math.log(0.5) + 0.5 * (math.lgamma(m + 1.5) - math.lgamma(m + 1.0) - math.lgamma(1.5)) for m in range(M)
    ]
    return trig, quad, lat_rows, start


def to_column(row):
    n = row.shape[1]
    return jnp.sum(jnp.where(iota((n, n), 0) == iota((n, n), 1), row, jnp.zeros_like(row)), axis=1, keepdims=True)


def make_weights(w1_ref, bias1_ref, w2_ref, order_ref, bias2_ref, slots_in, o1_ref, o2_ref, ob_ref):
    width, rows = o1_ref.shape[1], o2_ref.shape[0]
    variables, fields = w1_ref.shape[1], w2_ref.shape[1]
    order = order_ref[...]
    base = VARS * LV
    column = iota((1, width), 1)
    var_col = over_levels(column)
    level_col = column - LV * var_col
    if slots_in:
        wide_order = jnp.concatenate([jnp.zeros((1, base), jnp.int32), order, jnp.zeros((1, width - base - ITEMS), jnp.int32)], axis=1)
        slot_field = (wide_order >= LV).astype(jnp.int32)
        var_col = jnp.where(column < base, var_col + FIELDS, slot_field)
        level_col = jnp.where(column < base, level_col, wide_order - LV * slot_field)
    level_col = jnp.where(column < width - 16, level_col, -100)
    r = iota((HID, CH), 0)
    spread = (over_levels(r) == iota((HID, CH), 1)).astype(F32).astype(BF)
    level_row = iota((HID, width), 0)
    level_row = level_row - LV * over_levels(level_row)
    total = jnp.zeros((HID, width), F32)
    pick = (iota((variables, width), 0) == var_col).astype(F32).astype(BF)
    for tap in range(3):
        tall = lax.dot_general(spread, w1_ref[tap], NT, preferred_element_type=F32)
        wide = dot((0.5 * tall).astype(BF), pick)
        total = jnp.where(level_col == level_row + 2 * (tap - 1), wide, total)
    bias = 0.5 * to_column(bias1_ref[...])
    high = bias.astype(BF).astype(F32)
    low = bias - high
    block = jnp.where(column == width - 16, high, jnp.where(column == width - 15, low, 0.0)).astype(BF)
    o1_ref[...] = (total + dot(spread, block)).astype(BF)
    if slots_in:
        row = iota((rows, 1), 0)
        field_row = over_levels(row)
    else:
        row = to_column(order.astype(F32)).astype(jnp.int32)
        field_row = (row >= LV).astype(jnp.int32)
    level_out = row - LV * field_row
    c = iota((CH, HID), 1)
    spread2 = (over_levels(c) == iota((CH, HID), 0)).astype(F32).astype(BF)
    level_hid = iota((rows, HID), 1)
    level_hid = level_hid - LV * over_levels(level_hid)
    total2 = jnp.zeros((rows, HID), F32)
    bias2 = jnp.zeros((rows, 128), F32)
    for tap in range(3):
        block = jnp.zeros((rows, CH), F32)
        for field in range(fields):
            block = jnp.where(field_row == field, w2_ref[tap].astype(F32)[field : field + 1, :], block)
        wide = dot(block.astype(BF), spread2)
        total2 = jnp.where(level_hid == level_out + 2 * (tap - 1), wide, total2)
    o2_ref[...] = total2.astype(BF)
    for field in range(fields):
        bias2 = jnp.where(field_row == field, bias2_ref[0:1, field : field + 1], bias2)
    ob_ref[...] = bias2


def weights_kernel(w1_ref, bias1_ref, w2_ref, order_ref, bias2_ref, o1_ref, o2_ref, ob_ref):
    make_weights(w1_ref, bias1_ref, w2_ref, order_ref, bias2_ref, True, o1_ref, o2_ref, ob_ref)


def second_weights(w1, bias1, w2, bias2, order):
    full = lambda *shape: pl.BlockSpec(shape, lambda i: (0,) * len(shape))
    width, rows = VARS * LV + ITEMS + 16, VARS * LV
    return pl.pallas_call(
        weights_kernel,
        out_shape=(
            pltpu.HBM((HID, width), BF),
            pltpu.HBM((rows, HID), BF),
            pltpu.HBM((rows, 128), F32),
        ),
        grid=(1,),
        in_specs=[full(*w1.shape), full(1, CH), full(*w2.shape), full(1, ITEMS), full(1, bias2.shape[0])],
        out_specs=(full(HID, width), full(rows, HID), full(rows, 128)),
        compiler_params=pltpu.CompilerParams(vmem_limit_bytes=20 * 2**20),
        cost_estimate=pl.CostEstimate(flops=2 * 10**8, bytes_accessed=2 * 10**6, transcendentals=0),
        name="second_weights",
    )(hbm(w1), hbm(bias1.reshape(1, CH)), hbm(w2), hbm(order.reshape(1, ITEMS)), hbm(bias2.reshape(1, -1)))


def hidden_layer(w1_ref, w2_ref, v_ref, h_ref):
    block = v_ref.shape[1]
    step, tall = 256, HID // 2
    c1, c2 = 2 * math.sqrt(2 / math.pi), 8 * 0.044715 * math.sqrt(2 / math.pi)
    results = []
    for col in range(0, block, step):
        cols = slice(col, col + step)
        for row in range(0, HID, tall):
            y = dot(w1_ref[row : row + tall, :], v_ref[:, cols])
            u = y * (c1 + c2 * (y * y))
            h_ref[row : row + tall, cols] = (y + y * jnp.tanh(u)).astype(BF)
        results.append(dot(w2_ref[...], h_ref[:, cols]))
    return jnp.concatenate(results, axis=1)


def first_kernel(
    block, state_ref, c1_ref, bias1_ref, c2_ref, order_ref, bias2_ref, out_ref, w1_ref, w2_ref, b2_ref, v_ref, h_ref, o_ref
):
    step = pl.program_id(0)

    @pl.when(step == 0)
    def _():
        make_weights(c1_ref, bias1_ref, c2_ref, order_ref, bias2_ref, False, w1_ref, w2_ref, b2_ref)
        v_ref[VARS * LV :, :] = jnp.ones((16, block), BF)

    v_ref[: VARS * LV, :] = state_ref[...]
    result = hidden_layer(w1_ref, w2_ref, v_ref, h_ref)
    bias = b2_ref[...]
    for tile in range(block // 128):
        o_ref[pl.ds(step * (block // 128) + tile, ITEMS, stride=TILES + 1), :] = result[:, tile * 128 : (tile + 1) * 128] + bias

    @pl.when(step == pl.num_programs(0) - 1)
    def _():
        for item in range(ITEMS):
            out_ref[item] = o_ref[item * (TILES + 1) : item * (TILES + 1) + TILES, :].astype(BF)


def first_conv(state, w1, bias1, w2, bias2, order, block=1024):
    full = lambda *shape: pl.BlockSpec(shape, lambda i: (0,) * len(shape))
    return pl.pallas_call(
        functools.partial(first_kernel, block),
        grid=(COLUMNS // block,),
        out_shape=pltpu.HBM((ITEMS, TILES, 128), BF),
        in_specs=[
            pl.BlockSpec((VARS * LV, block), lambda i: (0, i)),
            full(*w1.shape),
            full(1, CH),
            full(*w2.shape),
            full(1, ITEMS),
            full(1, bias2.shape[0]),
        ],
        out_specs=full(ITEMS, TILES, 128),
        scratch_shapes=[
            pltpu.VMEM((HID, VARS * LV + 16), BF),
            pltpu.VMEM((ITEMS, HID), BF),
            pltpu.VMEM((ITEMS, 128), F32),
            pltpu.VMEM((VARS * LV + 16, block), BF),
            pltpu.VMEM((HID, block), BF),
            pltpu.VMEM((ITEMS * (TILES + 1), 128), F32),
        ],
        compiler_params=pltpu.CompilerParams(vmem_limit_bytes=24 * 2**20),
        cost_estimate=pl.CostEstimate(flops=3 * 10**9, bytes_accessed=2 * 10**6, transcendentals=HID * COLUMNS),
        name="first_conv",
    )(hbm(state), hbm(w1), hbm(bias1.reshape(1, CH)), hbm(w2), hbm(order.reshape(1, ITEMS)), hbm(bias2.reshape(1, -1)))


def second_kernel(block, state_ref, filt_ref, w1_ref, w2_ref, b2_ref, out_ref, v_ref, h_ref, f_ref):
    step = pl.program_id(0)
    base = VARS * LV

    @pl.when(step == 0)
    def _():
        v_ref[base + ITEMS :, :] = jnp.ones((16, block), BF)
        for item in range(ITEMS):
            f_ref[item * (TILES + 1) : item * (TILES + 1) + TILES, :] = filt_ref[item].astype(F32)

    v_ref[:base, :] = state_ref[...]
    for tile in range(block // 128):
        piece = f_ref[pl.ds(step * (block // 128) + tile, ITEMS, stride=TILES + 1), :]
        v_ref[base : base + ITEMS, tile * 128 : (tile + 1) * 128] = piece.astype(BF)
    result = hidden_layer(w1_ref, w2_ref, v_ref, h_ref)
    bias = b2_ref[...]
    for tile in range(block // 128):
        out_ref[:, tile * 128 : (tile + 1) * 128] = result[:, tile * 128 : (tile + 1) * 128] + bias


def second_conv(state, filtered, w1, w2, b2, block=1024):
    full = lambda *shape: pl.BlockSpec(shape, lambda i: (0,) * len(shape))
    width = VARS * LV + ITEMS + 16
    return pl.pallas_call(
        functools.partial(second_kernel, block),
        grid=(COLUMNS // block,),
        out_shape=pltpu.HBM((VARS * LV, COLUMNS), F32),
        in_specs=[
            pl.BlockSpec((VARS * LV, block), lambda i: (0, i)),
            full(ITEMS, TILES, 128),
            full(HID, width),
            full(VARS * LV, HID),
            full(VARS * LV, 128),
        ],
        out_specs=pl.BlockSpec((VARS * LV, block), lambda i: (0, i)),
        scratch_shapes=[
            pltpu.VMEM((width, block), BF),
            pltpu.VMEM((HID, block), BF),
            pltpu.VMEM((ITEMS * (TILES + 1), 128), F32),
        ],
        compiler_params=pltpu.CompilerParams(vmem_limit_bytes=24 * 2**20),
        cost_estimate=pl.CostEstimate(flops=4 * 10**9, bytes_accessed=4 * 10**6, transcendentals=HID * COLUMNS),
        name="second_conv",
    )(hbm(state), filtered, w1, w2, b2)


CHUNK = 176
STRIDE = CHUNK + 1


def table_kernel(wave_ref, lat_ref, start_ref, out_ref, now_ref, old_ref, log_ref, ratio_ref, s_ref):
    step = pl.program_id(0)
    wave = jnp.broadcast_to(wave_ref[...], (MH, 128))
    sine = [lat_ref[0:1, 128 * h : 128 * h + 128] for h in range(2)]

    @pl.when(step == 0)
    def _():
        match = iota((MH, 384), 1).astype(F32) == wave_ref[...]
        start = jnp.sum(jnp.where(match, start_ref[...], 0.0), axis=1, keepdims=True)
        for h in range(2):
            log_cos = lat_ref[1:2, 128 * h : 128 * h + 128]
            log_ref[h] = jnp.where(wave > 500.0, -1e4, start + wave * log_cos)
            now_ref[h] = jnp.zeros((MH, 128), F32)
            old_ref[h] = jnp.zeros((MH, 128), F32)
        ratio_ref[...] = jnp.zeros((MH, 128), F32)

    now = [now_ref[h] for h in range(2)]
    old = [old_ref[h] for h in range(2)]
    log_scale = [log_ref[h] for h in range(2)]
    ratio = ratio_ref[...]
    scale = [None, None]
    first = (step * CHUNK).astype(F32)
    for kk in range(CHUNK):
        if kk % 8 == 0:
            for h in range(2):
                big = jnp.abs(now[h]) > 1e8
                shrink = jnp.where(big, 1e-12, 1.0)
                now[h] = now[h] * shrink
                old[h] = old[h] * shrink
                log_scale[h] = log_scale[h] + jnp.where(big, math.log(1e12), 0.0)
                scale[h] = jnp.exp(log_scale[h])
        k = first + kk
        n = wave + k
        top = 4.0 * (n * n) - 1.0
        bottom = k * (wave + n)
        root = lax.rsqrt(jnp.maximum(top * bottom, 1e-30))
        up = jnp.where(n <= M - 1.0, top * root, 0.0)
        for h in range(2):
            stepped = up * (sine[h] * now[h] - ratio * old[h])
            if kk == 0:
                stepped = jnp.where(step == 0, 1.0, stepped)
            old[h], now[h] = now[h], stepped
            s_ref[h, pl.ds(kk, MH, stride=STRIDE), :] = stepped * scale[h]
        ratio = bottom * root
    for h in range(2):
        now_ref[h], old_ref[h], log_ref[h] = now[h], old[h], log_scale[h]
    ratio_ref[...] = ratio
    for m in range(MH):
        for h in range(2):
            out_ref[m, :, 128 * h : 128 * h + 128] = s_ref[h, m * STRIDE : m * STRIDE + CHUNK, :].astype(BF)


def legendre_table(waves_f, lat_rows, start):
    full = lambda *shape: pl.BlockSpec(shape, lambda i: (0,) * len(shape))
    return pl.pallas_call(
        table_kernel,
        grid=(KP // CHUNK,),
        out_shape=pltpu.HBM((MH, KP, HALF), BF),
        in_specs=[full(MH, 1), full(8, HALF), full(1, 384)],
        out_specs=pl.BlockSpec((MH, CHUNK, HALF), lambda i: (0, i, 0)),
        scratch_shapes=[pltpu.VMEM((2, MH, 128), F32)] * 3
        + [pltpu.VMEM((MH, 128), F32), pltpu.VMEM((2, MH * STRIDE, 128), F32)],
        compiler_params=pltpu.CompilerParams(vmem_limit_bytes=20 * 2**20),
        cost_estimate=pl.CostEstimate(flops=2 * 10**8, bytes_accessed=9 * 10**6, transcendentals=0),
        name="legendre_table",
    )(waves_f, lat_rows, start)


def swap_halves(x):
    return pltpu.roll(x, 64, 1)


def forward_kernel(y_ref, f_ref, g_ref, q_ref, out_ref, x0_ref, x1_ref):
    low = iota((TILES, 128), 1) < 64
    x0_ref[192:256, :] = jnp.zeros((64, NLON), BF)
    x1_ref[0:64, :] = jnp.zeros((64, NLON), BF)
    place0, place1 = (0, 64, 128), (128, 192, 64)
    for pair in range(N_LON // 2):
        for item in range(GROUP):
            a = y_ref[2 * pair, item].astype(F32)
            b = y_ref[2 * pair + 1, item].astype(F32)
            even = jnp.where(low, a, swap_halves(b)).astype(BF)
            odd = jnp.where(low, swap_halves(a), b).astype(BF)
            lanes = slice(128 * pair, 128 * pair + 128)
            for ref, place in ((x0_ref, place0), (x1_ref, place1)):
                ref[place[item] : place[item] + 32, lanes] = even
                ref[place[item] + 32 : place[item] + 64, lanes] = odd
    quad = q_ref[...]
    cosines = lax.dot_general(f_ref[...], x0_ref[...], NT, preferred_element_type=F32)
    sines = lax.dot_general(g_ref[...], x1_ref[...], NT, preferred_element_type=F32)
    tiles = (cosines[:, :128], cosines[:, 128:] + sines[:, :128], sines[:, 128:])
    for t, value in enumerate(tiles):
        value = (value * quad[:, 128 * t : 128 * t + 128]).astype(BF)
        for group in range(N_LAT):
            out_ref[group, :, 128 * t : 128 * t + 128] = value[group * MP : (group + 1) * MP]


def forward_fourier(pieces, tables, quad):
    full = lambda *shape: pl.BlockSpec(shape, lambda i: (0,) * len(shape))
    return pl.pallas_call(
        forward_kernel,
        grid=(1,),
        out_shape=pltpu.HBM((N_LAT, MP, 384), BF),
        in_specs=[
            full(N_LON, GROUP, TILES, 128),
            pl.BlockSpec((N_LAT * MP, NLON), lambda i: (0, 0)),
            pl.BlockSpec((N_LAT * MP, NLON), lambda i: (0, 1)),
            full(1, 384),
        ],
        out_specs=full(N_LAT, MP, 384),
        scratch_shapes=[pltpu.VMEM((256, NLON), BF)] * 2,
        compiler_params=pltpu.CompilerParams(vmem_limit_bytes=20 * 2**20),
        cost_estimate=pl.CostEstimate(flops=4 * 10**8, bytes_accessed=3 * 10**6, transcendentals=0),
        name="forward_fourier",
    )(pieces, tables, tables, quad)


def inverse_kernel(r_ref, f_ref, g_ref, out_ref):
    turned = [r_ref[:, 128 * t : 128 * t + 128].astype(F32).T.astype(BF) for t in range(3)]
    cosines = jnp.concatenate([turned[0], turned[1][:64]], axis=0)
    sines = jnp.concatenate([turned[2], turned[1][64:]], axis=0)
    grid = dot(cosines, f_ref[...]) + dot(sines, g_ref[...])
    low = iota((TILES, 128), 1) < 64
    for pair in range(N_LON // 2):
        for item in range(GROUP):
            lanes = slice(128 * pair, 128 * pair + 128)
            even = grid[64 * item : 64 * item + 32, lanes]
            odd = grid[64 * item + 32 : 64 * item + 64, lanes]
            out_ref[2 * pair, item] = jnp.where(low, even, swap_halves(odd)).astype(BF)
            out_ref[2 * pair + 1, item] = jnp.where(low, swap_halves(even), odd).astype(BF)


def inverse_fourier(returned, tables):
    full = lambda *shape: pl.BlockSpec(shape, lambda i: (0,) * len(shape))
    return pl.pallas_call(
        inverse_kernel,
        grid=(1,),
        out_shape=pltpu.HBM((N_LON, GROUP, TILES, 128), BF),
        in_specs=[
            full(N_LAT * MP, 384),
            pl.BlockSpec((N_LAT * MP, NLON), lambda i: (0, 0)),
            pl.BlockSpec((N_LAT * MP, NLON), lambda i: (0, 1)),
        ],
        out_specs=full(N_LON, GROUP, TILES, 128),
        compiler_params=pltpu.CompilerParams(vmem_limit_bytes=20 * 2**20),
        cost_estimate=pl.CostEstimate(flops=4 * 10**8, bytes_accessed=3 * 10**6, transcendentals=0),
        name="inverse_fourier",
    )(returned, tables, tables)


WAVES = 8
GROUPS = -(-OWNED // WAVES)
LAST = OWNED - (GROUPS - 1) * WAVES


def spectral_kernel(wave_ref, x_ref, t0_ref, t1_ref, gain_ref, spec_ref, out_ref, c_ref, n_ref, r_ref, m_ref, t_ref, sems):
    step = pl.program_id(0)
    low = iota((MP, 128), 1) < 64

    def table_copy(group):
        first, count = group * WAVES, LAST if group == GROUPS - 1 else WAVES
        source, at = (t0_ref, first) if first < MH else (t1_ref, first - MH)
        return pltpu.make_async_copy(source.at[pl.ds(at, count)], t_ref.at[pl.ds(first, count)], sems.at[group])

    @pl.when(step == 0)
    def _():
        for group in range(GROUPS):
            table_copy(group).start()

    mirror = (iota((HALF, HALF), 0) + iota((HALF, HALF), 1) == HALF - 1).astype(F32).astype(BF)

    @pl.when(step == 0)
    def _():
        for slab in (6, 7, 14, 15):
            for h in range(2):
                c_ref[h, slab * SLAB : slab * SLAB + MP, :] = jnp.zeros((MP, 128), F32)
        for slab in range(6):
            for h in range(4):
                r_ref[h, slab * SLAB + OWNED : slab * SLAB + MP, :] = jnp.zeros((MP - OWNED, 128), F32)
        for pair in range(N_LAT // 2):
            for tile in range(3):
                a = x_ref[2 * pair, :, 128 * tile : 128 * tile + 128].astype(F32)
                b = x_ref[2 * pair + 1, :, 128 * tile : 128 * tile + 128].astype(F32)
                both = jnp.where(low, a, swap_halves(b)), jnp.where(low, swap_halves(a), b)
                for half in range(2):
                    slab = slab_of(tile, half)
                    if pair < 2:
                        c_ref[pair, slab * SLAB : slab * SLAB + MP, :] = both[half]
                    else:
                        m_ref[slab * MP : slab * MP + MP, 128 * (pair - 2) : 128 * (pair - 2) + 128] = both[half].astype(BF)
        turned = dot(m_ref[...], mirror)
        for slab in range(6):
            for h in range(2):
                a = c_ref[h, slab * SLAB : slab * SLAB + MP, :]
                b = turned[slab * MP : slab * MP + MP, 128 * h : 128 * h + 128]
                c_ref[h, slab * SLAB : slab * SLAB + MP, :] = a + b
                c_ref[h, (8 + slab) * SLAB : (8 + slab) * SLAB + MP, :] = a - b

    even = iota((8, KP), 1) % 2 == 0
    gain = gain_ref[...]

    def waves(count):
        boths = []
        for mm in range(count):
            m = step * WAVES + mm
            left = jnp.concatenate([c_ref[h, pl.ds(m, 16, stride=SLAB), :] for h in range(2)], axis=1).astype(BF)
            boths.append(lax.dot_general(left, t_ref[m], NT, preferred_element_type=F32))
        rights = []
        for mm in range(count):
            m = step * WAVES + mm
            natural = jnp.where(even, boths[mm][:8], boths[mm][8:])
            n_ref[0, pl.ds(m, 8, stride=SLAB), :] = natural[:, :128]
            n_ref[1, pl.ds(m, 8, stride=SLAB), :] = natural[:, 128:256]
            n_ref[2, pl.ds(m, 8, stride=SLAB), :] = jnp.concatenate([natural[:, 256:], jnp.zeros((8, 384 - KP), F32)], axis=1)
            scaled = natural * pltpu.roll(gain, 768 - wave_ref[m], 1)[:, :KP]
            rights.append(jnp.concatenate([jnp.where(even, scaled, 0.0), jnp.where(even, 0.0, scaled)], axis=0).astype(BF))
        for mm in range(count):
            m = step * WAVES + mm
            back = dot(rights[mm], t_ref[m])
            north, south = back[:8] + back[8:], back[:8] - back[8:]
            for h in range(2):
                r_ref[h, pl.ds(m, 8, stride=SLAB), :] = north[:, 128 * h : 128 * h + 128]
                r_ref[2 + h, pl.ds(m, 8, stride=SLAB), :] = south[:, 128 * h : 128 * h + 128]

    for group in range(GROUPS):

        @pl.when(step == group)
        def _():
            table_copy(group).wait()

    pl.when(step < GROUPS - 1)(lambda: waves(WAVES))
    pl.when(step == GROUPS - 1)(lambda: waves(LAST))

    @pl.when(step == pl.num_programs(0) - 1)
    def _():
        for slab in range(6):
            for h in range(2):
                m_ref[slab * MP : slab * MP + MP, 128 * h : 128 * h + 128] = r_ref[2 + h, slab * SLAB : slab * SLAB + MP, :].astype(BF)
        turned = dot(m_ref[...], mirror)

        def tile_of(slab, j):
            if j < 2:
                return r_ref[j, slab * SLAB : slab * SLAB + MP, :]
            return turned[slab * MP : slab * MP + MP, 128 * (j - 2) : 128 * (j - 2) + 128]

        for pair in range(N_LAT // 2):
            for tile in range(3):
                a = tile_of(slab_of(tile, 0), pair)
                b = tile_of(slab_of(tile, 1), pair)
                lanes = slice(128 * tile, 128 * tile + 128)
                out_ref[2 * pair, :, lanes] = jnp.where(low, a, swap_halves(b)).astype(BF)
                out_ref[2 * pair + 1, :, lanes] = jnp.where(low, swap_halves(a), b).astype(BF)
        wide = iota((MP, 768), 1) < M
        zeros = jnp.zeros((MP, 384), F32)
        for item in range(GROUP):
            parts = []
            for part in range(2):
                at = (part * GROUP + item) * SLAB
                parts.append(jnp.concatenate([n_ref[h, at : at + MP, :] for h in range(3)] + [zeros], axis=1))
            value = jnp.where(wide, parts[0], pltpu.roll(parts[1], M, 1))
            spec_ref[item] = value[:OWNED, : 2 * M]


def spectral_step(waves, coeffs, table0, table1, gain):
    full = lambda *shape: pl.BlockSpec(shape, lambda i, w: (0,) * len(shape))
    return pl.pallas_call(
        spectral_kernel,
        grid_spec=pltpu.PrefetchScalarGridSpec(
            num_scalar_prefetch=1,
            grid=(GROUPS,),
            in_specs=[
                full(N_LAT, MP, 384),
                pl.BlockSpec(memory_space=pltpu.HBM),
                pl.BlockSpec(memory_space=pltpu.HBM),
                full(8, 768),
            ],
            out_specs=(full(GROUP, OWNED, 2 * M), full(N_LAT, MP, 384)),
            scratch_shapes=[
                pltpu.VMEM((2, 16 * SLAB, 128), F32),
                pltpu.VMEM((3, 8 * SLAB, 128), F32),
                pltpu.VMEM((4, 8 * SLAB, 128), F32),
                pltpu.VMEM((6 * MP, HALF), BF),
                pltpu.VMEM((OWNED, KP, HALF), BF),
                pltpu.SemaphoreType.DMA((GROUPS,)),
            ],
        ),
        out_shape=(
            pltpu.HBM((GROUP, OWNED, 2 * M), F32),
            pltpu.HBM((N_LAT, MP, 384), BF),
        ),
        compiler_params=pltpu.CompilerParams(vmem_limit_bytes=24 * 2**20),
        cost_estimate=pl.CostEstimate(flops=4 * 10**9, bytes_accessed=10**7, transcendentals=0),
        name="spectral_step",
    )(waves, coeffs, hbm(table0), hbm(table1), gain)


def per_device(
    state, conv_in, bias_in, conv_out, bias_out, spectral_gain, mix_in, blend_bias, mix_out, mix_out_bias, level_order, wave_order
):
    trig, quad, lat_rows, start = constants()
    band = lax.axis_index("lat")
    columns = state.reshape(VARS * LV, COLUMNS)

    tendency = first_conv(columns, conv_in.transpose(1, 2, 0), bias_in, conv_out.transpose(1, 0, 2), bias_out, level_order)
    tendency, wave_order, spectral_gain = lax.optimization_barrier((tendency, wave_order, spectral_gain))
    pieces = lax.all_to_all(tendency.reshape(N_LON, GROUP, TILES, 128), "lon", 0, 0, tiled=True)

    grouped = jnp.pad(wave_order.reshape(N_LAT, OWNED), ((0, 0), (0, MP - OWNED)), constant_values=-1)
    chosen = (grouped.reshape(N_LAT * MP)[:, None] == jnp.arange(M, dtype=jnp.int32)[None, :]).astype(BF)
    tables = dot(chosen, jnp.asarray(trig[:, : 2 * NLON])).astype(BF)
    owned = lax.dynamic_slice_in_dim(grouped, band, 1, 0)[0]
    waves_f = jnp.where(owned < 0, 1000, owned).astype(F32)[:, None]
    lat_rows, start = jnp.asarray(lat_rows), jnp.asarray(start)
    band_quad = lax.dynamic_slice_in_dim(jnp.asarray(quad), band, 1, 0)[0]
    gain = jnp.broadcast_to(jnp.pad(spectral_gain, (0, 768 - M))[None], (8, 768))
    owned = jnp.maximum(owned, 0)
    table0 = legendre_table(waves_f[:MH], lat_rows, start)
    pieces, table0, tables, gain, owned = lax.optimization_barrier((pieces, table0, tables, gain, owned))

    coeffs = forward_fourier(pieces, tables, band_quad)
    coeffs, waves_late, chosen = lax.optimization_barrier((coeffs, waves_f[MH:], chosen))
    coeffs = lax.all_to_all(coeffs, "lat", 0, 0, tiled=True)
    table1 = legendre_table(waves_late, lat_rows, start)
    inverse_tables = dot(chosen, jnp.asarray(trig[:, 2 * NLON :])).astype(BF)
    coeffs, table1, inverse_tables = lax.optimization_barrier((coeffs, table1, inverse_tables))

    spectrum, returned = spectral_step(owned, coeffs, table0, table1, gain)
    returned, mix_in, blend_bias, mix_out, mix_out_bias, level_order = lax.optimization_barrier(
        (returned, mix_in, blend_bias, mix_out, mix_out_bias, level_order)
    )
    returned = lax.all_to_all(returned, "lat", 0, 0, tiled=True)
    m1, m2, mb = second_weights(mix_in.transpose(1, 2, 0), blend_bias, mix_out.transpose(1, 0, 2), mix_out_bias, level_order)
    returned, m1, m2, mb = lax.optimization_barrier((returned, m1, m2, mb))
    grid_values = inverse_fourier(returned.reshape(N_LAT * MP, 384), inverse_tables)
    filtered = lax.all_to_all(grid_values, "lon", 0, 0, tiled=True)
    increment = second_conv(columns, filtered.reshape(ITEMS, TILES, 128), m1, m2, mb)
    return spectrum, increment.reshape(1, VARS, LV, COLUMNS)


def solution(mesh):
    return jax.shard_map(
        per_device,
        mesh=mesh,
        in_specs=(P(None, None, None, ("lat", "lon")),) + (P(),) * 11,
        out_specs=(P("lon", "lat", None), P(None, None, None, ("lat", "lon"))),
        check_vma=False,
    )
```

```python
import functools
import math

import jax
import jax.numpy as jnp
import ml_dtypes
import numpy as np
from jax import lax
from jax.experimental import pallas as pl
from jax.experimental.pallas import tpu as pltpu
from jax.sharding import PartitionSpec as P

NLAT, NLON, M = 512, 1024, 344
LV, VARS, CH, FIELDS = 24, 6, 64, 2
N_LAT, N_LON = 8, 16
ROWS, COLS = NLAT // N_LAT, NLON // N_LON
COLUMNS = ROWS * COLS
TILES = COLUMNS // 128
ITEMS = FIELDS * LV
GROUP = ITEMS // N_LON
OWNED = M // N_LAT
MP = 48
MH = MP // 2
KP = 352
HALF = NLAT // 2
HID = CH * LV
SLAB = 49
BF, F32 = jnp.bfloat16, jnp.float32
NT = (((1,), (1,)), ((), ()))

BLOCKS = {(0, 0): (0, 0), (0, 1): (0, 1), (1, 0): (0, 2), (1, 1): (1, 2), (2, 0): (1, 0), (2, 1): (1, 1)}


def slab_of(tile, half):
    part, item = BLOCKS[(tile, half)]
    return part * GROUP + item


def iota(shape, dim):
    return lax.broadcasted_iota(jnp.int32, shape, dim)


def over_levels(index):
    return jnp.floor((index.astype(F32) + 0.5) * (1.0 / LV)).astype(jnp.int32)


def hbm(x):
    return pltpu.with_memory_space_constraint(x, pltpu.HBM)


def dot(a, b):
    return jnp.dot(a, b, preferred_element_type=F32)


def row_order():
    slots = np.arange(ROWS)
    return 2 * (slots % (ROWS // 2)) + slots // (ROWS // 2)


@functools.lru_cache(None)
def constants():
    n = np.arange(M)[:, None]
    angle = 2 * np.pi * ((n * np.arange(NLON)[None, :]) % NLON) / NLON
    factor = np.where(n == 0, 1.0, 2.0) / math.sqrt(NLAT * NLON)
    trig = np.concatenate(
        [np.cos(angle) / math.sqrt(NLON), np.sin(angle) / math.sqrt(NLON), np.cos(angle) * factor, np.sin(angle) * factor],
        axis=1,
    ).astype(ml_dtypes.bfloat16)
    slots = np.arange(NLAT)
    lat = (slots // ROWS) * ROWS + row_order()[slots % ROWS]
    phi = np.pi * (lat + 0.5) / NLAT - np.pi / 2
    sine, cosine = np.sin(phi), np.cos(phi)
    quad = (np.pi * cosine / math.sqrt(NLAT)).reshape(N_LAT, 1, ROWS)
    quad = np.tile(quad, (1, 1, 2 * GROUP)).astype(np.float32)
    lat_rows = np.zeros((8, HALF), np.float32)
    lat_rows[0], lat_rows[1] = sine[:HALF], np.log(cosine[:HALF])
    start = np.zeros((1, 384), np.float32)
    start[0, :M] = [
        0.5 * math.log(0.5) + 0.5 * (math.lgamma(m + 1.5) - math.lgamma(m + 1.0) - math.lgamma(1.5)) for m in range(M)
    ]
    return trig, quad, lat_rows, start


def to_column(row):
    n = row.shape[1]
    return jnp.sum(jnp.where(iota((n, n), 0) == iota((n, n), 1), row, jnp.zeros_like(row)), axis=1, keepdims=True)


def make_weights(w1_ref, bias1_ref, w2_ref, order_ref, bias2_ref, slots_in, o1_ref, o2_ref, ob_ref):
    width, rows = o1_ref.shape[1], o2_ref.shape[0]
    variables, fields = w1_ref.shape[1], w2_ref.shape[1]
    order = order_ref[...]
    base = VARS * LV
    column = iota((1, width), 1)
    var_col = over_levels(column)
    level_col = column - LV * var_col
    if slots_in:
        wide_order = jnp.concatenate([jnp.zeros((1, base), jnp.int32), order, jnp.zeros((1, width - base - ITEMS), jnp.int32)], axis=1)
        slot_field = (wide_order >= LV).astype(jnp.int32)
        var_col = jnp.where(column < base, var_col + FIELDS, slot_field)
        level_col = jnp.where(column < base, level_col, wide_order - LV * slot_field)
    level_col = jnp.where(column < width - 16, level_col, -100)
    pick = (iota((variables, width), 0) == var_col).astype(F32).astype(BF)
    same = (iota((CH, CH), 0) == iota((CH, CH), 1)).astype(F32).astype(BF)
    blocks = []
    for tap in range(3):
        turned = lax.dot_general(same, w1_ref[tap], NT, preferred_element_type=F32)
        blocks.append(dot((0.5 * turned).astype(BF), pick))
    bias = 0.5 * to_column(bias1_ref[...])
    high = bias.astype(BF).astype(F32)
    low = bias - high
    bias_block = jnp.where(column == width - 16, high, jnp.where(column == width - 15, low, 0.0))
    level_row = iota((LV, width), 0)
    hits = [level_col == level_row + 2 * (tap - 1) for tap in range(3)]
    for channel in range(0, CH, 2):
        pair = []
        for o in (channel, channel + 1):
            rows_o = jnp.broadcast_to(bias_block[o : o + 1], (LV, width))
            for tap in range(3):
                rows_o = jnp.where(hits[tap], blocks[tap][o : o + 1], rows_o)
            pair.append(rows_o)
        o1_ref[channel * LV : (channel + 2) * LV, :] = jnp.concatenate(pair, axis=0).astype(BF)
    if slots_in:
        row = iota((rows, 1), 0)
        field_row = over_levels(row)
    else:
        row = to_column(order.astype(F32)).astype(jnp.int32)
        field_row = (row >= LV).astype(jnp.int32)
    level_out = row - LV * field_row
    spread2 = (over_levels(iota((1, HID), 1)) == iota((CH, HID), 0)).astype(F32).astype(BF)
    level_hid = iota((1, HID), 1)
    level_hid = level_hid - LV * over_levels(level_hid)
    total2 = jnp.zeros((rows, HID), F32)
    bias2 = jnp.zeros((rows, 128), F32)
    for tap in range(3):
        block = jnp.zeros((rows, CH), F32)
        for field in range(fields):
            block = jnp.where(field_row == field, w2_ref[tap].astype(F32)[field : field + 1, :], block)
        wide = dot(block.astype(BF), spread2)
        total2 = jnp.where(level_hid == level_out + 2 * (tap - 1), wide, total2)
    o2_ref[...] = total2.astype(BF)
    for field in range(fields):
        bias2 = jnp.where(field_row == field, bias2_ref[0:1, field : field + 1], bias2)
    ob_ref[...] = bias2


def weights_kernel(w1_ref, bias1_ref, w2_ref, order_ref, bias2_ref, o1_ref, o2_ref, ob_ref):
    make_weights(w1_ref, bias1_ref, w2_ref, order_ref, bias2_ref, True, o1_ref, o2_ref, ob_ref)


def second_weights(w1, bias1, w2, bias2, order):
    full = lambda *shape: pl.BlockSpec(shape, lambda i: (0,) * len(shape))
    width, rows = VARS * LV + ITEMS + 16, VARS * LV
    return pl.pallas_call(
        weights_kernel,
        out_shape=(
            pltpu.HBM((HID, width), BF),
            pltpu.HBM((rows, HID), BF),
            pltpu.HBM((rows, 128), F32),
        ),
        grid=(1,),
        in_specs=[full(*w1.shape), full(1, CH), full(*w2.shape), full(1, ITEMS), full(1, bias2.shape[0])],
        out_specs=(full(HID, width), full(rows, HID), full(rows, 128)),
        compiler_params=pltpu.CompilerParams(vmem_limit_bytes=20 * 2**20),
        cost_estimate=pl.CostEstimate(flops=2 * 10**8, bytes_accessed=2 * 10**6, transcendentals=0),
        name="second_weights",
    )(hbm(w1), hbm(bias1.reshape(1, CH)), hbm(w2), hbm(order.reshape(1, ITEMS)), hbm(bias2.reshape(1, -1)))


def hidden_layer(w1_ref, w2_ref, v_ref, h_ref):
    block = v_ref.shape[1]
    step, tall = 256, HID // 2
    c1, c2 = 2 * math.sqrt(2 / math.pi), 8 * 0.044715 * math.sqrt(2 / math.pi)
    results = []
    for col in range(0, block, step):
        cols = slice(col, col + step)
        for row in range(0, HID, tall):
            y = dot(w1_ref[row : row + tall, :], v_ref[:, cols])
            u = y * (c1 + c2 * (y * y))
            h_ref[row : row + tall, cols] = (y + y * jnp.tanh(u)).astype(BF)
        results.append(dot(w2_ref[...], h_ref[:, cols]))
    return jnp.concatenate(results, axis=1)


def first_kernel(
    block, state_ref, c1_ref, bias1_ref, c2_ref, order_ref, bias2_ref, out_ref, w1_ref, w2_ref, b2_ref, v_ref, h_ref, o_ref
):
    step = pl.program_id(0)

    @pl.when(step == 0)
    def _():
        make_weights(c1_ref, bias1_ref, c2_ref, order_ref, bias2_ref, False, w1_ref, w2_ref, b2_ref)
        v_ref[VARS * LV :, :] = jnp.ones((16, block), BF)

    v_ref[: VARS * LV, :] = state_ref[...]
    result = hidden_layer(w1_ref, w2_ref, v_ref, h_ref)
    bias = b2_ref[...]
    for tile in range(block // 128):
        o_ref[pl.ds(step * (block // 128) + tile, ITEMS, stride=TILES + 1), :] = result[:, tile * 128 : (tile + 1) * 128] + bias

    @pl.when(step == pl.num_programs(0) - 1)
    def _():
        for item in range(ITEMS):
            out_ref[item] = o_ref[item * (TILES + 1) : item * (TILES + 1) + TILES, :].astype(BF)


def first_conv(state, w1, bias1, w2, bias2, order, block=1024):
    full = lambda *shape: pl.BlockSpec(shape, lambda i: (0,) * len(shape))
    return pl.pallas_call(
        functools.partial(first_kernel, block),
        grid=(COLUMNS // block,),
        out_shape=pltpu.HBM((ITEMS, TILES, 128), BF),
        in_specs=[
            pl.BlockSpec((VARS * LV, block), lambda i: (0, i)),
            full(*w1.shape),
            full(1, CH),
            full(*w2.shape),
            full(1, ITEMS),
            full(1, bias2.shape[0]),
        ],
        out_specs=full(ITEMS, TILES, 128),
        scratch_shapes=[
            pltpu.VMEM((HID, VARS * LV + 16), BF),
            pltpu.VMEM((ITEMS, HID), BF),
            pltpu.VMEM((ITEMS, 128), F32),
            pltpu.VMEM((VARS * LV + 16, block), BF),
            pltpu.VMEM((HID, block), BF),
            pltpu.VMEM((ITEMS * (TILES + 1), 128), F32),
        ],
        compiler_params=pltpu.CompilerParams(vmem_limit_bytes=24 * 2**20),
        cost_estimate=pl.CostEstimate(flops=3 * 10**9, bytes_accessed=2 * 10**6, transcendentals=HID * COLUMNS),
        name="first_conv",
    )(hbm(state), hbm(w1), hbm(bias1.reshape(1, CH)), hbm(w2), hbm(order.reshape(1, ITEMS)), hbm(bias2.reshape(1, -1)))


def second_kernel(block, state_ref, filt_ref, w1_ref, w2_ref, b2_ref, out_ref, v_ref, h_ref, f_ref):
    step = pl.program_id(0)
    base = VARS * LV

    @pl.when(step == 0)
    def _():
        v_ref[base + ITEMS :, :] = jnp.ones((16, block), BF)
        for item in range(ITEMS):
            f_ref[item * (TILES + 1) : item * (TILES + 1) + TILES, :] = filt_ref[item].astype(F32)

    v_ref[:base, :] = state_ref[...]
    for tile in range(block // 128):
        piece = f_ref[pl.ds(step * (block // 128) + tile, ITEMS, stride=TILES + 1), :]
        v_ref[base : base + ITEMS, tile * 128 : (tile + 1) * 128] = piece.astype(BF)
    result = hidden_layer(w1_ref, w2_ref, v_ref, h_ref)
    bias = b2_ref[...]
    for tile in range(block // 128):
        out_ref[:, tile * 128 : (tile + 1) * 128] = result[:, tile * 128 : (tile + 1) * 128] + bias


def second_conv(state, filtered, w1, w2, b2, block=1024):
    full = lambda *shape: pl.BlockSpec(shape, lambda i: (0,) * len(shape))
    width = VARS * LV + ITEMS + 16
    return pl.pallas_call(
        functools.partial(second_kernel, block),
        grid=(COLUMNS // block,),
        out_shape=pltpu.HBM((VARS * LV, COLUMNS), F32),
        in_specs=[
            pl.BlockSpec((VARS * LV, block), lambda i: (0, i)),
            full(ITEMS, TILES, 128),
            full(HID, width),
            full(VARS * LV, HID),
            full(VARS * LV, 128),
        ],
        out_specs=pl.BlockSpec((VARS * LV, block), lambda i: (0, i)),
        scratch_shapes=[
            pltpu.VMEM((width, block), BF),
            pltpu.VMEM((HID, block), BF),
            pltpu.VMEM((ITEMS * (TILES + 1), 128), F32),
        ],
        compiler_params=pltpu.CompilerParams(vmem_limit_bytes=24 * 2**20),
        cost_estimate=pl.CostEstimate(flops=4 * 10**9, bytes_accessed=4 * 10**6, transcendentals=HID * COLUMNS),
        name="second_conv",
    )(hbm(state), filtered, w1, w2, b2)


CHUNK = 176
STRIDE = CHUNK + 1
LANES = -(-CHUNK // 128) * 128


def table_kernel(wave_ref, lat_ref, start_ref, out_ref, now_ref, old_ref, log_ref, ratio_ref, s_ref):
    step = pl.program_id(0)
    wave = jnp.broadcast_to(wave_ref[...], (MH, 128))
    sine = [lat_ref[0:1, 128 * h : 128 * h + 128] for h in range(2)]

    @pl.when(step == 0)
    def _():
        match = iota((MH, 384), 1).astype(F32) == wave_ref[...]
        start = jnp.sum(jnp.where(match, start_ref[...], 0.0), axis=1, keepdims=True)
        for h in range(2):
            log_cos = lat_ref[1:2, 128 * h : 128 * h + 128]
            log_ref[h] = jnp.where(wave > 500.0, -1e4, start + wave * log_cos)
            now_ref[h] = jnp.zeros((MH, 128), F32)
            old_ref[h] = jnp.zeros((MH, 128), F32)
        ratio_ref[...] = jnp.zeros((MH, 128), F32)

    now = [now_ref[h] for h in range(2)]
    old = [old_ref[h] for h in range(2)]
    log_scale = [log_ref[h] for h in range(2)]
    ratio = ratio_ref[...]
    scale = [None, None]
    k = (step * CHUNK).astype(F32) + iota((MH, LANES), 1).astype(F32)
    m = jnp.broadcast_to(wave_ref[...], (MH, LANES))
    n = m + k
    top = 4.0 * (n * n) - 1.0
    bottom = k * (m + n)
    root = lax.rsqrt(jnp.maximum(top * bottom, 1e-30))
    ups = jnp.where(n <= M - 1.0, top * root, 0.0)
    ratios = bottom * root
    for kk in range(CHUNK):
        if kk % 8 == 0:
            for h in range(2):
                big = jnp.abs(now[h]) > 1e8
                shrink = jnp.where(big, 1e-12, 1.0)
                now[h] = now[h] * shrink
                old[h] = old[h] * shrink
                log_scale[h] = log_scale[h] + jnp.where(big, math.log(1e12), 0.0)
                scale[h] = jnp.exp(log_scale[h])
        up = jnp.broadcast_to(ups[:, kk : kk + 1], (MH, 128))
        for h in range(2):
            stepped = up * (sine[h] * now[h] - ratio * old[h])
            if kk == 0:
                stepped = jnp.where(step == 0, 1.0, stepped)
            old[h], now[h] = now[h], stepped
            s_ref[h, pl.ds(kk, MH, stride=STRIDE), :] = stepped * scale[h]
        ratio = jnp.broadcast_to(ratios[:, kk : kk + 1], (MH, 128))
    for h in range(2):
        now_ref[h], old_ref[h], log_ref[h] = now[h], old[h], log_scale[h]
    ratio_ref[...] = ratio
    for m in range(MH):
        for h in range(2):
            out_ref[m, :, 128 * h : 128 * h + 128] = s_ref[h, m * STRIDE : m * STRIDE + CHUNK, :].astype(BF)


def legendre_table(waves_f, lat_rows, start):
    full = lambda *shape: pl.BlockSpec(shape, lambda i: (0,) * len(shape))
    return pl.pallas_call(
        table_kernel,
        grid=(KP // CHUNK,),
        out_shape=pltpu.HBM((MH, KP, HALF), BF),
        in_specs=[full(MH, 1), full(8, HALF), full(1, 384)],
        out_specs=pl.BlockSpec((MH, CHUNK, HALF), lambda i: (0, i, 0)),
        scratch_shapes=[pltpu.VMEM((2, MH, 128), F32)] * 3
        + [pltpu.VMEM((MH, 128), F32), pltpu.VMEM((2, MH * STRIDE, 128), F32)],
        compiler_params=pltpu.CompilerParams(vmem_limit_bytes=20 * 2**20),
        cost_estimate=pl.CostEstimate(flops=2 * 10**8, bytes_accessed=9 * 10**6, transcendentals=0),
        name="legendre_table",
    )(waves_f, lat_rows, start)


def swap_halves(x):
    return pltpu.roll(x, 64, 1)


def forward_kernel(y_ref, f_ref, g_ref, q_ref, out_ref, x0_ref, x1_ref):
    low = iota((TILES, 128), 1) < 64
    x0_ref[192:256, :] = jnp.zeros((64, NLON), BF)
    x1_ref[0:64, :] = jnp.zeros((64, NLON), BF)
    place0, place1 = (0, 64, 128), (128, 192, 64)
    for pair in range(N_LON // 2):
        for item in range(GROUP):
            a = y_ref[2 * pair, item].astype(F32)
            b = y_ref[2 * pair + 1, item].astype(F32)
            even = jnp.where(low, a, swap_halves(b)).astype(BF)
            odd = jnp.where(low, swap_halves(a), b).astype(BF)
            lanes = slice(128 * pair, 128 * pair + 128)
            for ref, place in ((x0_ref, place0), (x1_ref, place1)):
                ref[place[item] : place[item] + 32, lanes] = even
                ref[place[item] + 32 : place[item] + 64, lanes] = odd
    quad = q_ref[...]
    cosines = lax.dot_general(f_ref[...], x0_ref[...], NT, preferred_element_type=F32)
    sines = lax.dot_general(g_ref[...], x1_ref[...], NT, preferred_element_type=F32)
    tiles = (cosines[:, :128], cosines[:, 128:] + sines[:, :128], sines[:, 128:])
    for t, value in enumerate(tiles):
        value = (value * quad[:, 128 * t : 128 * t + 128]).astype(BF)
        for group in range(N_LAT):
            out_ref[group, :, 128 * t : 128 * t + 128] = value[group * MP : (group + 1) * MP]


def forward_fourier(pieces, tables, quad):
    full = lambda *shape: pl.BlockSpec(shape, lambda i: (0,) * len(shape))
    return pl.pallas_call(
        forward_kernel,
        grid=(1,),
        out_shape=pltpu.HBM((N_LAT, MP, 384), BF),
        in_specs=[
            full(N_LON, GROUP, TILES, 128),
            pl.BlockSpec((N_LAT * MP, NLON), lambda i: (0, 0)),
            pl.BlockSpec((N_LAT * MP, NLON), lambda i: (0, 1)),
            full(1, 384),
        ],
        out_specs=full(N_LAT, MP, 384),
        scratch_shapes=[pltpu.VMEM((256, NLON), BF)] * 2,
        compiler_params=pltpu.CompilerParams(vmem_limit_bytes=20 * 2**20),
        cost_estimate=pl.CostEstimate(flops=4 * 10**8, bytes_accessed=3 * 10**6, transcendentals=0),
        name="forward_fourier",
    )(pieces, tables, tables, quad)


def inverse_kernel(r_ref, f_ref, g_ref, out_ref):
    turned = [r_ref[:, 128 * t : 128 * t + 128].astype(F32).T.astype(BF) for t in range(3)]
    cosines = jnp.concatenate([turned[0], turned[1][:64]], axis=0)
    sines = jnp.concatenate([turned[2], turned[1][64:]], axis=0)
    grid = dot(cosines, f_ref[...]) + dot(sines, g_ref[...])
    low = iota((TILES, 128), 1) < 64
    for pair in range(N_LON // 2):
        for item in range(GROUP):
            lanes = slice(128 * pair, 128 * pair + 128)
            even = grid[64 * item : 64 * item + 32, lanes]
            odd = grid[64 * item + 32 : 64 * item + 64, lanes]
            out_ref[2 * pair, item] = jnp.where(low, even, swap_halves(odd)).astype(BF)
            out_ref[2 * pair + 1, item] = jnp.where(low, swap_halves(even), odd).astype(BF)


def inverse_fourier(returned, tables):
    full = lambda *shape: pl.BlockSpec(shape, lambda i: (0,) * len(shape))
    return pl.pallas_call(
        inverse_kernel,
        grid=(1,),
        out_shape=pltpu.HBM((N_LON, GROUP, TILES, 128), BF),
        in_specs=[
            full(N_LAT * MP, 384),
            pl.BlockSpec((N_LAT * MP, NLON), lambda i: (0, 0)),
            pl.BlockSpec((N_LAT * MP, NLON), lambda i: (0, 1)),
        ],
        out_specs=full(N_LON, GROUP, TILES, 128),
        compiler_params=pltpu.CompilerParams(vmem_limit_bytes=20 * 2**20),
        cost_estimate=pl.CostEstimate(flops=4 * 10**8, bytes_accessed=3 * 10**6, transcendentals=0),
        name="inverse_fourier",
    )(returned, tables, tables)


WAVES = 8
GROUPS = -(-OWNED // WAVES)
LAST = OWNED - (GROUPS - 1) * WAVES


def spectral_kernel(wave_ref, x_ref, t0_ref, t1_ref, gain_ref, spec_ref, out_ref, c_ref, n_ref, r_ref, m_ref, t_ref, sems):
    step = pl.program_id(0)
    low = iota((MP, 128), 1) < 64

    def table_copy(group):
        first, count = group * WAVES, LAST if group == GROUPS - 1 else WAVES
        source, at = (t0_ref, first) if first < MH else (t1_ref, first - MH)
        return pltpu.make_async_copy(source.at[pl.ds(at, count)], t_ref.at[pl.ds(first, count)], sems.at[group])

    @pl.when(step == 0)
    def _():
        for group in range(GROUPS):
            table_copy(group).start()

    mirror = (iota((HALF, HALF), 0) + iota((HALF, HALF), 1) == HALF - 1).astype(F32).astype(BF)

    @pl.when(step == 0)
    def _():
        for slab in (6, 7, 14, 15):
            for h in range(2):
                c_ref[h, slab * SLAB : slab * SLAB + MP, :] = jnp.zeros((MP, 128), F32)
        for slab in range(6):
            for h in range(4):
                r_ref[h, slab * SLAB + OWNED : slab * SLAB + MP, :] = jnp.zeros((MP - OWNED, 128), F32)
        for pair in range(N_LAT // 2):
            for tile in range(3):
                a = x_ref[2 * pair, :, 128 * tile : 128 * tile + 128].astype(F32)
                b = x_ref[2 * pair + 1, :, 128 * tile : 128 * tile + 128].astype(F32)
                both = jnp.where(low, a, swap_halves(b)), jnp.where(low, swap_halves(a), b)
                for half in range(2):
                    slab = slab_of(tile, half)
                    if pair < 2:
                        c_ref[pair, slab * SLAB : slab * SLAB + MP, :] = both[half]
                    else:
                        m_ref[slab * MP : slab * MP + MP, 128 * (pair - 2) : 128 * (pair - 2) + 128] = both[half].astype(BF)
        turned = dot(m_ref[...], mirror)
        for slab in range(6):
            for h in range(2):
                a = c_ref[h, slab * SLAB : slab * SLAB + MP, :]
                b = turned[slab * MP : slab * MP + MP, 128 * h : 128 * h + 128]
                c_ref[h, slab * SLAB : slab * SLAB + MP, :] = a + b
                c_ref[h, (8 + slab) * SLAB : (8 + slab) * SLAB + MP, :] = a - b

    even = iota((8, KP), 1) % 2 == 0
    gain = gain_ref[...]

    def waves(count):
        boths = []
        for mm in range(count):
            m = step * WAVES + mm
            left = jnp.concatenate([c_ref[h, pl.ds(m, 16, stride=SLAB), :] for h in range(2)], axis=1).astype(BF)
            boths.append(lax.dot_general(left, t_ref[m], NT, preferred_element_type=F32))
        rights = []
        for mm in range(count):
            m = step * WAVES + mm
            natural = jnp.where(even, boths[mm][:8], boths[mm][8:])
            n_ref[0, pl.ds(m, 8, stride=SLAB), :] = natural[:, :128]
            n_ref[1, pl.ds(m, 8, stride=SLAB), :] = natural[:, 128:256]
            n_ref[2, pl.ds(m, 8, stride=SLAB), :] = jnp.concatenate([natural[:, 256:], jnp.zeros((8, 384 - KP), F32)], axis=1)
            scaled = natural * pltpu.roll(gain, 768 - wave_ref[m], 1)[:, :KP]
            rights.append(jnp.concatenate([jnp.where(even, scaled, 0.0), jnp.where(even, 0.0, scaled)], axis=0).astype(BF))
        for mm in range(count):
            m = step * WAVES + mm
            back = dot(rights[mm], t_ref[m])
            north, south = back[:8] + back[8:], back[:8] - back[8:]
            for h in range(2):
                r_ref[h, pl.ds(m, 8, stride=SLAB), :] = north[:, 128 * h : 128 * h + 128]
                r_ref[2 + h, pl.ds(m, 8, stride=SLAB), :] = south[:, 128 * h : 128 * h + 128]

    for group in range(GROUPS):

        @pl.when(step == group)
        def _():
            table_copy(group).wait()

    pl.when(step < GROUPS - 1)(lambda: waves(WAVES))
    pl.when(step == GROUPS - 1)(lambda: waves(LAST))

    @pl.when(step == pl.num_programs(0) - 1)
    def _():
        for slab in range(6):
            for h in range(2):
                m_ref[slab * MP : slab * MP + MP, 128 * h : 128 * h + 128] = r_ref[2 + h, slab * SLAB : slab * SLAB + MP, :].astype(BF)
        turned = dot(m_ref[...], mirror)

        def tile_of(slab, j):
            if j < 2:
                return r_ref[j, slab * SLAB : slab * SLAB + MP, :]
            return turned[slab * MP : slab * MP + MP, 128 * (j - 2) : 128 * (j - 2) + 128]

        for pair in range(N_LAT // 2):
            for tile in range(3):
                a = tile_of(slab_of(tile, 0), pair)
                b = tile_of(slab_of(tile, 1), pair)
                lanes = slice(128 * tile, 128 * tile + 128)
                out_ref[2 * pair, :, lanes] = jnp.where(low, a, swap_halves(b)).astype(BF)
                out_ref[2 * pair + 1, :, lanes] = jnp.where(low, swap_halves(a), b).astype(BF)
        wide = iota((MP, 768), 1) < M
        zeros = jnp.zeros((MP, 384), F32)
        for item in range(GROUP):
            parts = []
            for part in range(2):
                at = (part * GROUP + item) * SLAB
                parts.append(jnp.concatenate([n_ref[h, at : at + MP, :] for h in range(3)] + [zeros], axis=1))
            value = jnp.where(wide, parts[0], pltpu.roll(parts[1], M, 1))
            spec_ref[item] = value[:OWNED, : 2 * M]


def spectral_step(waves, coeffs, table0, table1, gain):
    full = lambda *shape: pl.BlockSpec(shape, lambda i, w: (0,) * len(shape))
    return pl.pallas_call(
        spectral_kernel,
        grid_spec=pltpu.PrefetchScalarGridSpec(
            num_scalar_prefetch=1,
            grid=(GROUPS,),
            in_specs=[
                full(N_LAT, MP, 384),
                pl.BlockSpec(memory_space=pltpu.HBM),
                pl.BlockSpec(memory_space=pltpu.HBM),
                full(8, 768),
            ],
            out_specs=(full(GROUP, OWNED, 2 * M), full(N_LAT, MP, 384)),
            scratch_shapes=[
                pltpu.VMEM((2, 16 * SLAB, 128), F32),
                pltpu.VMEM((3, 8 * SLAB, 128), F32),
                pltpu.VMEM((4, 8 * SLAB, 128), F32),
                pltpu.VMEM((6 * MP, HALF), BF),
                pltpu.VMEM((OWNED, KP, HALF), BF),
                pltpu.SemaphoreType.DMA((GROUPS,)),
            ],
        ),
        out_shape=(
            pltpu.HBM((GROUP, OWNED, 2 * M), F32),
            pltpu.HBM((N_LAT, MP, 384), BF),
        ),
        compiler_params=pltpu.CompilerParams(vmem_limit_bytes=24 * 2**20),
        cost_estimate=pl.CostEstimate(flops=4 * 10**9, bytes_accessed=10**7, transcendentals=0),
        name="spectral_step",
    )(waves, coeffs, hbm(table0), hbm(table1), gain)


def per_device(
    state, conv_in, bias_in, conv_out, bias_out, spectral_gain, mix_in, blend_bias, mix_out, mix_out_bias, level_order, wave_order
):
    trig, quad, lat_rows, start = constants()
    band = lax.axis_index("lat")
    columns = state.reshape(VARS * LV, COLUMNS)

    tendency = first_conv(columns, conv_in.transpose(1, 2, 0), bias_in, conv_out.transpose(1, 0, 2), bias_out, level_order)
    tendency, wave_order, spectral_gain = lax.optimization_barrier((tendency, wave_order, spectral_gain))
    pieces = lax.all_to_all(tendency.reshape(N_LON, GROUP, TILES, 128), "lon", 0, 0, tiled=True)

    grouped = jnp.pad(wave_order.reshape(N_LAT, OWNED), ((0, 0), (0, MP - OWNED)), constant_values=-1)
    chosen = (grouped.reshape(N_LAT * MP)[:, None] == jnp.arange(M, dtype=jnp.int32)[None, :]).astype(BF)
    tables = dot(chosen, jnp.asarray(trig[:, : 2 * NLON])).astype(BF)
    owned = lax.dynamic_slice_in_dim(grouped, band, 1, 0)[0]
    waves_f = jnp.where(owned < 0, 1000, owned).astype(F32)[:, None]
    lat_rows, start = jnp.asarray(lat_rows), jnp.asarray(start)
    band_quad = lax.dynamic_slice_in_dim(jnp.asarray(quad), band, 1, 0)[0]
    gain = jnp.broadcast_to(jnp.pad(spectral_gain, (0, 768 - M))[None], (8, 768))
    owned = jnp.maximum(owned, 0)
    table0 = legendre_table(waves_f[:MH], lat_rows, start)
    pieces, table0, tables, gain, owned = lax.optimization_barrier((pieces, table0, tables, gain, owned))

    coeffs = forward_fourier(pieces, tables, band_quad)
    coeffs, waves_late = lax.optimization_barrier((coeffs, waves_f[MH:]))
    coeffs = lax.all_to_all(coeffs, "lat", 0, 0, tiled=True)
    table1 = legendre_table(waves_late, lat_rows, start)
    coeffs, table1 = lax.optimization_barrier((coeffs, table1))

    spectrum, returned = spectral_step(owned, coeffs, table0, table1, gain)
    returned, mix_in, blend_bias, mix_out, mix_out_bias, level_order, chosen = lax.optimization_barrier(
        (returned, mix_in, blend_bias, mix_out, mix_out_bias, level_order, chosen)
    )
    returned = lax.all_to_all(returned, "lat", 0, 0, tiled=True)
    m1, m2, mb = second_weights(mix_in.transpose(1, 2, 0), blend_bias, mix_out.transpose(1, 0, 2), mix_out_bias, level_order)
    inverse_tables = dot(chosen, jnp.asarray(trig[:, 2 * NLON :])).astype(BF)
    returned, m1, m2, mb, inverse_tables = lax.optimization_barrier((returned, m1, m2, mb, inverse_tables))
    grid_values = inverse_fourier(returned.reshape(N_LAT * MP, 384), inverse_tables)
    filtered = lax.all_to_all(grid_values, "lon", 0, 0, tiled=True)
    increment = second_conv(columns, filtered.reshape(ITEMS, TILES, 128), m1, m2, mb)
    return spectrum, increment.reshape(1, VARS, LV, COLUMNS)


def solution(mesh):
    return jax.shard_map(
        per_device,
        mesh=mesh,
        in_specs=(P(None, None, None, ("lat", "lon")),) + (P(),) * 11,
        out_specs=(P("lon", "lat", None), P(None, None, None, ("lat", "lon"))),
        check_vma=False,
    )
```

```python
import functools
import math

import jax
import jax.numpy as jnp
import ml_dtypes
import numpy as np
from jax import lax
from jax.experimental import pallas as pl
from jax.experimental.pallas import tpu as pltpu
from jax.sharding import PartitionSpec as P

NLAT, NLON, M = 512, 1024, 344
LV, VARS, CH, FIELDS = 24, 6, 64, 2
N_LAT, N_LON = 8, 16
ROWS, COLS = NLAT // N_LAT, NLON // N_LON
COLUMNS = ROWS * COLS
TILES = COLUMNS // 128
ITEMS = FIELDS * LV
GROUP = ITEMS // N_LON
OWNED = M // N_LAT
MP = 48
MH = MP // 2
KP = 352
HALF = NLAT // 2
HID = CH * LV
BAND = 8
SLAB = 49
BF, F32 = jnp.bfloat16, jnp.float32
NT = (((1,), (1,)), ((), ()))

BLOCKS = {(0, 0): (0, 0), (0, 1): (0, 1), (1, 0): (0, 2), (1, 1): (1, 2), (2, 0): (1, 0), (2, 1): (1, 1)}


def slab_of(tile, half):
    part, item = BLOCKS[(tile, half)]
    return part * GROUP + item


def iota(shape, dim):
    return lax.broadcasted_iota(jnp.int32, shape, dim)


def over_levels(index):
    return jnp.floor((index.astype(F32) + 0.5) * (1.0 / LV)).astype(jnp.int32)


def hbm(x):
    return pltpu.with_memory_space_constraint(x, pltpu.HBM)


def dot(a, b):
    return jnp.dot(a, b, preferred_element_type=F32)


def row_order():
    slots = np.arange(ROWS)
    return 2 * (slots % (ROWS // 2)) + slots // (ROWS // 2)


@functools.lru_cache(None)
def constants():
    n = np.arange(M)[:, None]
    angle = 2 * np.pi * ((n * np.arange(NLON)[None, :]) % NLON) / NLON
    factor = np.where(n == 0, 1.0, 2.0) / math.sqrt(NLAT * NLON)
    trig = np.concatenate(
        [np.cos(angle) / math.sqrt(NLON), np.sin(angle) / math.sqrt(NLON), np.cos(angle) * factor, np.sin(angle) * factor],
        axis=1,
    ).astype(ml_dtypes.bfloat16)
    slots = np.arange(NLAT)
    lat = (slots // ROWS) * ROWS + row_order()[slots % ROWS]
    phi = np.pi * (lat + 0.5) / NLAT - np.pi / 2
    sine, cosine = np.sin(phi), np.cos(phi)
    quad = (np.pi * cosine / math.sqrt(NLAT)).reshape(N_LAT, 1, ROWS)
    quad = np.tile(quad, (1, 1, 2 * GROUP)).astype(np.float32)
    lat_rows = np.zeros((8, HALF), np.float32)
    lat_rows[0], lat_rows[1] = sine[:HALF], np.log(cosine[:HALF])
    start = np.zeros((1, 384), np.float32)
    start[0, :M] = [
        0.5 * math.log(0.5) + 0.5 * (math.lgamma(m + 1.5) - math.lgamma(m + 1.0) - math.lgamma(1.5)) for m in range(M)
    ]
    return trig, quad, lat_rows, start


def to_column(row):
    n = row.shape[1]
    return jnp.sum(jnp.where(iota((n, n), 0) == iota((n, n), 1), row, jnp.zeros_like(row)), axis=1, keepdims=True)


def make_weights(w1_ref, bias1_ref, w2_ref, order_ref, bias2_ref, slots_in, o1_ref, o2_ref, ob_ref):
    width, rows = o1_ref.shape[1], o2_ref.shape[0]
    variables, fields = w1_ref.shape[1], bias2_ref.shape[1]
    order = order_ref[...]
    base = VARS * LV
    column = iota((1, width), 1)
    var_col = over_levels(column)
    level_col = column - LV * var_col
    if slots_in:
        wide_order = jnp.concatenate([jnp.zeros((1, base), jnp.int32), order, jnp.zeros((1, width - base - ITEMS), jnp.int32)], axis=1)
        slot_field = (wide_order >= LV).astype(jnp.int32)
        var_col = jnp.where(column < base, var_col + FIELDS, slot_field)
        level_col = jnp.where(column < base, level_col, wide_order - LV * slot_field)
    level_col = jnp.where(column < width - 16, level_col, -100)
    pick = (iota((variables, width), 0) == var_col).astype(F32).astype(BF)
    same = (iota((CH, CH), 0) == iota((CH, CH), 1)).astype(F32).astype(BF)
    blocks = []
    for tap in range(3):
        turned = lax.dot_general(same, w1_ref[tap], NT, preferred_element_type=F32)
        blocks.append(dot((0.5 * turned).astype(BF), pick))
    bias = 0.5 * to_column(bias1_ref[...])
    high = bias.astype(BF).astype(F32)
    low = bias - high
    bias_block = jnp.where(column == width - 16, high, jnp.where(column == width - 15, low, 0.0))
    for level in range(LV):
        block = bias_block
        for tap in range(3):
            block = jnp.where(level_col == level + 2 * (tap - 1), blocks[tap], block)
        o1_ref[level * CH : (level + 1) * CH, :] = block.astype(BF)
    hidden = o2_ref.shape[1]
    if slots_in:
        row = iota((rows, 1), 0)
        level_out = (row >> 3) - 2
        field_row = row & 7
    else:
        row = to_column(order.astype(F32)).astype(jnp.int32)
        field_row = (row >= LV).astype(jnp.int32)
        level_out = row - LV * field_row
    spread2 = ((iota((CH, hidden), 1) & (CH - 1)) == iota((CH, hidden), 0)).astype(F32).astype(BF)
    level_hid = iota((1, hidden), 1) >> 6
    total2 = jnp.zeros((rows, hidden), F32)
    bias2 = jnp.zeros((rows, 128), F32)
    for tap in range(3):
        block = jnp.zeros((rows, CH), F32)
        for field in range(fields):
            taps = w2_ref[field].astype(F32)[tap : tap + 1] if slots_in else w2_ref[tap].astype(F32)[field : field + 1]
            block = jnp.where(field_row == field, taps, block)
        wide = dot(block.astype(BF), spread2)
        total2 = jnp.where(level_hid == level_out + 2 * (tap - 1), wide, total2)
    o2_ref[...] = total2.astype(BF)
    for field in range(fields):
        bias2 = jnp.where(field_row == field, bias2_ref[0:1, field : field + 1], bias2)
    ob_ref[...] = bias2


def weights_kernel(w1_ref, bias1_ref, w2_ref, order_ref, bias2_ref, o1_ref, o2_ref, ob_ref):
    make_weights(w1_ref, bias1_ref, w2_ref, order_ref, bias2_ref, True, o1_ref, o2_ref, ob_ref)


def second_weights(w1, bias1, w2, bias2, order):
    full = lambda *shape: pl.BlockSpec(shape, lambda i: (0,) * len(shape))
    width, rows = VARS * LV + ITEMS + 16, 8 * BAND
    return pl.pallas_call(
        weights_kernel,
        out_shape=(
            pltpu.HBM((HID, width), BF),
            pltpu.HBM((rows, 4 * CH), BF),
            pltpu.HBM((rows, 128), F32),
        ),
        grid=(1,),
        in_specs=[full(*w1.shape), full(1, CH), full(*w2.shape), full(1, ITEMS), full(1, bias2.shape[0])],
        out_specs=(full(HID, width), full(rows, 4 * CH), full(rows, 128)),
        compiler_params=pltpu.CompilerParams(vmem_limit_bytes=20 * 2**20),
        cost_estimate=pl.CostEstimate(flops=2 * 10**8, bytes_accessed=2 * 10**6, transcendentals=0),
        name="second_weights",
    )(hbm(w1), hbm(bias1.reshape(1, CH)), hbm(w2), hbm(order.reshape(1, ITEMS)), hbm(bias2.reshape(1, -1)))


def hidden_layer(w1_ref, v_ref, h_ref, cols):
    tall = HID // 2
    c1, c2 = 2 * math.sqrt(2 / math.pi), 8 * 0.044715 * math.sqrt(2 / math.pi)
    for row in range(0, HID, tall):
        y = dot(w1_ref[row : row + tall, :], v_ref[:, cols])
        u = y * (c1 + c2 * (y * y))
        h_ref[row : row + tall, cols] = (y + y * jnp.tanh(u)).astype(BF)


def first_kernel(
    block, state_ref, c1_ref, bias1_ref, c2_ref, order_ref, bias2_ref, out_ref, w1_ref, w2_ref, b2_ref, v_ref, h_ref, o_ref
):
    step = pl.program_id(0)

    @pl.when(step == 0)
    def _():
        make_weights(c1_ref, bias1_ref, c2_ref, order_ref, bias2_ref, False, w1_ref, w2_ref, b2_ref)
        v_ref[VARS * LV :, :] = jnp.ones((16, block), BF)

    v_ref[: VARS * LV, :] = state_ref[...]
    bias = b2_ref[...]
    for col in range(0, block, 256):
        hidden_layer(w1_ref, v_ref, h_ref, slice(col, col + 256))
        result = dot(w2_ref[...], h_ref[:, col : col + 256])
        for half in range(2):
            tile = step * (block // 128) + col // 128 + half
            o_ref[pl.ds(tile, ITEMS, stride=TILES + 1), :] = result[:, half * 128 : (half + 1) * 128] + bias

    @pl.when(step == pl.num_programs(0) - 1)
    def _():
        for item in range(ITEMS):
            out_ref[item] = o_ref[item * (TILES + 1) : item * (TILES + 1) + TILES, :].astype(BF)


def first_conv(state, w1, bias1, w2, bias2, order, block=1024):
    full = lambda *shape: pl.BlockSpec(shape, lambda i: (0,) * len(shape))
    return pl.pallas_call(
        functools.partial(first_kernel, block),
        grid=(COLUMNS // block,),
        out_shape=pltpu.HBM((ITEMS, TILES, 128), BF),
        in_specs=[
            pl.BlockSpec((VARS * LV, block), lambda i: (0, i)),
            full(*w1.shape),
            full(1, CH),
            full(*w2.shape),
            full(1, ITEMS),
            full(1, bias2.shape[0]),
        ],
        out_specs=full(ITEMS, TILES, 128),
        scratch_shapes=[
            pltpu.VMEM((HID, VARS * LV + 16), BF),
            pltpu.VMEM((ITEMS, HID), BF),
            pltpu.VMEM((ITEMS, 128), F32),
            pltpu.VMEM((VARS * LV + 16, block), BF),
            pltpu.VMEM((HID, block), BF),
            pltpu.VMEM((ITEMS * (TILES + 1), 128), F32),
        ],
        compiler_params=pltpu.CompilerParams(vmem_limit_bytes=24 * 2**20),
        cost_estimate=pl.CostEstimate(flops=3 * 10**9, bytes_accessed=2 * 10**6, transcendentals=HID * COLUMNS),
        name="first_conv",
    )(hbm(state), hbm(w1), hbm(bias1.reshape(1, CH)), hbm(w2), hbm(order.reshape(1, ITEMS)), hbm(bias2.reshape(1, -1)))


def second_kernel(block, state_ref, filt_ref, w1_ref, w2_ref, b2_ref, out_ref, v_ref, h_ref, f_ref, e_ref):
    step = pl.program_id(0)
    base = VARS * LV

    @pl.when(step == 0)
    def _():
        v_ref[base + ITEMS :, :] = jnp.ones((16, block), BF)
        for item in range(ITEMS):
            f_ref[item * (TILES + 1) : item * (TILES + 1) + TILES, :] = filt_ref[item].astype(F32)

    v_ref[:base, :] = state_ref[...]
    for tile in range(block // 128):
        piece = f_ref[pl.ds(step * (block // 128) + tile, ITEMS, stride=TILES + 1), :]
        v_ref[base : base + ITEMS, tile * 128 : (tile + 1) * 128] = piece.astype(BF)
    bias = b2_ref[0:8, :]
    for col in range(0, block, 256):
        hidden_layer(w1_ref, v_ref, h_ref, slice(col, col + 256))
        levels = [None] * LV
        for group in range(LV // 4):
            part = dot(w2_ref[...], h_ref[group * 4 * CH : (group + 1) * 4 * CH, col : col + 256])
            for at in range(BAND):
                level = 4 * group - 2 + at
                if 0 <= level < LV:
                    piece = part[8 * at : 8 * at + 8]
                    levels[level] = piece if levels[level] is None else levels[level] + piece
        for half in range(2):
            lanes = slice(col + half * 128, col + half * 128 + 128)
            for level in range(LV):
                e_ref[half, 9 * level : 9 * level + 8, :] = levels[level][:, half * 128 : (half + 1) * 128] + bias
            for variable in range(VARS):
                out_ref[variable * LV : (variable + 1) * LV, lanes] = e_ref[half, pl.ds(variable, LV, stride=9), :]


def second_conv(state, filtered, w1, w2, b2, block=1024):
    full = lambda *shape: pl.BlockSpec(shape, lambda i: (0,) * len(shape))
    width = VARS * LV + ITEMS + 16
    return pl.pallas_call(
        functools.partial(second_kernel, block),
        grid=(COLUMNS // block,),
        out_shape=pltpu.HBM((VARS * LV, COLUMNS), F32),
        in_specs=[
            pl.BlockSpec((VARS * LV, block), lambda i: (0, i)),
            full(ITEMS, TILES, 128),
            full(HID, width),
            full(8 * BAND, 4 * CH),
            full(8 * BAND, 128),
        ],
        out_specs=pl.BlockSpec((VARS * LV, block), lambda i: (0, i)),
        scratch_shapes=[
            pltpu.VMEM((width, block), BF),
            pltpu.VMEM((HID, block), BF),
            pltpu.VMEM((ITEMS * (TILES + 1), 128), F32),
            pltpu.VMEM((2, 9 * LV, 128), F32),
        ],
        compiler_params=pltpu.CompilerParams(vmem_limit_bytes=24 * 2**20),
        cost_estimate=pl.CostEstimate(flops=4 * 10**9, bytes_accessed=4 * 10**6, transcendentals=HID * COLUMNS),
        name="second_conv",
    )(hbm(state), filtered, w1, w2, b2)


CHUNK = 176
STRIDE = CHUNK + 1
LANES = -(-CHUNK // 128) * 128


def table_kernel(wave_ref, lat_ref, start_ref, out_ref, now_ref, old_ref, log_ref, ratio_ref, s_ref):
    step = pl.program_id(0)
    wave = jnp.broadcast_to(wave_ref[...], (MH, 128))
    sine = [lat_ref[0:1, 128 * h : 128 * h + 128] for h in range(2)]

    @pl.when(step == 0)
    def _():
        match = iota((MH, 384), 1).astype(F32) == wave_ref[...]
        start = jnp.sum(jnp.where(match, start_ref[...], 0.0), axis=1, keepdims=True)
        for h in range(2):
            log_cos = lat_ref[1:2, 128 * h : 128 * h + 128]
            log_ref[h] = jnp.where(wave > 500.0, -1e4, start + wave * log_cos)
            now_ref[h] = jnp.zeros((MH, 128), F32)
            old_ref[h] = jnp.zeros((MH, 128), F32)
        ratio_ref[...] = jnp.zeros((MH, 128), F32)

    now = [now_ref[h] for h in range(2)]
    old = [old_ref[h] for h in range(2)]
    log_scale = [log_ref[h] for h in range(2)]
    ratio = ratio_ref[...]
    scale = [None, None]
    k = (step * CHUNK).astype(F32) + iota((MH, LANES), 1).astype(F32)
    m = jnp.broadcast_to(wave_ref[...], (MH, LANES))
    n = m + k
    top = 4.0 * (n * n) - 1.0
    bottom = k * (m + n)
    root = lax.rsqrt(jnp.maximum(top * bottom, 1e-30))
    ups = jnp.where(n <= M - 1.0, top * root, 0.0)
    ratios = bottom * root
    for kk in range(CHUNK):
        if kk % 8 == 0:
            for h in range(2):
                big = jnp.abs(now[h]) > 1e8
                shrink = jnp.where(big, 1e-12, 1.0)
                now[h] = now[h] * shrink
                old[h] = old[h] * shrink
                log_scale[h] = log_scale[h] + jnp.where(big, math.log(1e12), 0.0)
                scale[h] = jnp.exp(log_scale[h])
        up = jnp.broadcast_to(ups[:, kk : kk + 1], (MH, 128))
        for h in range(2):
            stepped = up * (sine[h] * now[h] - ratio * old[h])
            if kk == 0:
                stepped = jnp.where(step == 0, 1.0, stepped)
            old[h], now[h] = now[h], stepped
            s_ref[h, pl.ds(kk, MH, stride=STRIDE), :] = stepped * scale[h]
        ratio = jnp.broadcast_to(ratios[:, kk : kk + 1], (MH, 128))
    for h in range(2):
        now_ref[h], old_ref[h], log_ref[h] = now[h], old[h], log_scale[h]
    ratio_ref[...] = ratio
    for m in range(MH):
        for h in range(2):
            out_ref[m, :, 128 * h : 128 * h + 128] = s_ref[h, m * STRIDE : m * STRIDE + CHUNK, :].astype(BF)


def legendre_table(waves_f, lat_rows, start):
    full = lambda *shape: pl.BlockSpec(shape, lambda i: (0,) * len(shape))
    return pl.pallas_call(
        table_kernel,
        grid=(KP // CHUNK,),
        out_shape=pltpu.HBM((MH, KP, HALF), BF),
        in_specs=[full(MH, 1), full(8, HALF), full(1, 384)],
        out_specs=pl.BlockSpec((MH, CHUNK, HALF), lambda i: (0, i, 0)),
        scratch_shapes=[pltpu.VMEM((2, MH, 128), F32)] * 3
        + [pltpu.VMEM((MH, 128), F32), pltpu.VMEM((2, MH * STRIDE, 128), F32)],
        compiler_params=pltpu.CompilerParams(vmem_limit_bytes=20 * 2**20),
        cost_estimate=pl.CostEstimate(flops=2 * 10**8, bytes_accessed=9 * 10**6, transcendentals=0),
        name="legendre_table",
    )(waves_f, lat_rows, start)


def swap_halves(x):
    return pltpu.roll(x, 64, 1)


def forward_kernel(band_ref, y_ref, f_ref, g_ref, q_ref, out_ref, x0_ref, x1_ref):
    low = iota((TILES, 128), 1) < 64
    x0_ref[192:256, :] = jnp.zeros((64, NLON), BF)
    x1_ref[0:64, :] = jnp.zeros((64, NLON), BF)
    place0, place1 = (0, 64, 128), (128, 192, 64)
    for pair in range(N_LON // 2):
        for item in range(GROUP):
            a = y_ref[2 * pair, item].astype(F32)
            b = y_ref[2 * pair + 1, item].astype(F32)
            even = jnp.where(low, a, swap_halves(b)).astype(BF)
            odd = jnp.where(low, swap_halves(a), b).astype(BF)
            lanes = slice(128 * pair, 128 * pair + 128)
            for ref, place in ((x0_ref, place0), (x1_ref, place1)):
                ref[place[item] : place[item] + 32, lanes] = even
                ref[place[item] + 32 : place[item] + 64, lanes] = odd
    quad = q_ref[pl.ds(band_ref[0], 1), :]
    cosines = lax.dot_general(f_ref[...], x0_ref[...], NT, preferred_element_type=F32)
    sines = lax.dot_general(g_ref[...], x1_ref[...], NT, preferred_element_type=F32)
    tiles = (cosines[:, :128], cosines[:, 128:] + sines[:, :128], sines[:, 128:])
    for t, value in enumerate(tiles):
        value = (value * quad[:, 128 * t : 128 * t + 128]).astype(BF)
        for group in range(N_LAT):
            out_ref[group, :, 128 * t : 128 * t + 128] = value[group * MP : (group + 1) * MP]


def forward_fourier(band, pieces, tables, quad):
    full = lambda *shape: pl.BlockSpec(shape, lambda i: (0,) * len(shape))
    return pl.pallas_call(
        forward_kernel,
        grid=(1,),
        out_shape=pltpu.HBM((N_LAT, MP, 384), BF),
        in_specs=[
            pl.BlockSpec(memory_space=pltpu.SMEM),
            full(N_LON, GROUP, TILES, 128),
            pl.BlockSpec((N_LAT * MP, NLON), lambda i: (0, 0)),
            pl.BlockSpec((N_LAT * MP, NLON), lambda i: (0, 1)),
            full(N_LAT, 384),
        ],
        out_specs=full(N_LAT, MP, 384),
        scratch_shapes=[pltpu.VMEM((256, NLON), BF)] * 2,
        compiler_params=pltpu.CompilerParams(vmem_limit_bytes=20 * 2**20),
        cost_estimate=pl.CostEstimate(flops=4 * 10**8, bytes_accessed=3 * 10**6, transcendentals=0),
        name="forward_fourier",
    )(band, pieces, tables, tables, hbm(quad))


def inverse_kernel(r_ref, f_ref, g_ref, out_ref):
    turned = [r_ref[:, 128 * t : 128 * t + 128].astype(F32).T.astype(BF) for t in range(3)]
    cosines = jnp.concatenate([turned[0], turned[1][:64]], axis=0)
    sines = jnp.concatenate([turned[2], turned[1][64:]], axis=0)
    grid = dot(cosines, f_ref[...]) + dot(sines, g_ref[...])
    low = iota((TILES, 128), 1) < 64
    for pair in range(N_LON // 2):
        for item in range(GROUP):
            lanes = slice(128 * pair, 128 * pair + 128)
            even = grid[64 * item : 64 * item + 32, lanes]
            odd = grid[64 * item + 32 : 64 * item + 64, lanes]
            out_ref[2 * pair, item] = jnp.where(low, even, swap_halves(odd)).astype(BF)
            out_ref[2 * pair + 1, item] = jnp.where(low, swap_halves(even), odd).astype(BF)


def inverse_fourier(returned, tables):
    full = lambda *shape: pl.BlockSpec(shape, lambda i: (0,) * len(shape))
    return pl.pallas_call(
        inverse_kernel,
        grid=(1,),
        out_shape=pltpu.HBM((N_LON, GROUP, TILES, 128), BF),
        in_specs=[
            full(N_LAT * MP, 384),
            pl.BlockSpec((N_LAT * MP, NLON), lambda i: (0, 0)),
            pl.BlockSpec((N_LAT * MP, NLON), lambda i: (0, 1)),
        ],
        out_specs=full(N_LON, GROUP, TILES, 128),
        compiler_params=pltpu.CompilerParams(vmem_limit_bytes=20 * 2**20),
        cost_estimate=pl.CostEstimate(flops=4 * 10**8, bytes_accessed=3 * 10**6, transcendentals=0),
        name="inverse_fourier",
    )(returned, tables, tables)


WAVES = 8
GROUPS = -(-OWNED // WAVES)
LAST = OWNED - (GROUPS - 1) * WAVES


def spectral_kernel(wave_ref, x_ref, t0_ref, t1_ref, gain_ref, spec_ref, out_ref, c_ref, n_ref, r_ref, m_ref, t_ref, sems):
    step = pl.program_id(0)
    low = iota((MP, 128), 1) < 64

    def table_copy(group):
        first, count = group * WAVES, LAST if group == GROUPS - 1 else WAVES
        source, at = (t0_ref, first) if first < MH else (t1_ref, first - MH)
        return pltpu.make_async_copy(source.at[pl.ds(at, count)], t_ref.at[pl.ds(first, count)], sems.at[group])

    @pl.when(step == 0)
    def _():
        for group in range(GROUPS):
            table_copy(group).start()

    mirror = (iota((HALF, HALF), 0) + iota((HALF, HALF), 1) == HALF - 1).astype(F32).astype(BF)

    @pl.when(step == 0)
    def _():
        for slab in (6, 7, 14, 15):
            for h in range(2):
                c_ref[h, slab * SLAB : slab * SLAB + MP, :] = jnp.zeros((MP, 128), F32)
        for slab in range(6):
            for h in range(4):
                r_ref[h, slab * SLAB + OWNED : slab * SLAB + MP, :] = jnp.zeros((MP - OWNED, 128), F32)
        for pair in range(N_LAT // 2):
            for tile in range(3):
                a = x_ref[2 * pair, :, 128 * tile : 128 * tile + 128].astype(F32)
                b = x_ref[2 * pair + 1, :, 128 * tile : 128 * tile + 128].astype(F32)
                both = jnp.where(low, a, swap_halves(b)), jnp.where(low, swap_halves(a), b)
                for half in range(2):
                    slab = slab_of(tile, half)
                    if pair < 2:
                        c_ref[pair, slab * SLAB : slab * SLAB + MP, :] = both[half]
                    else:
                        m_ref[slab * MP : slab * MP + MP, 128 * (pair - 2) : 128 * (pair - 2) + 128] = both[half].astype(BF)
        turned = dot(m_ref[...], mirror)
        for slab in range(6):
            for h in range(2):
                a = c_ref[h, slab * SLAB : slab * SLAB + MP, :]
                b = turned[slab * MP : slab * MP + MP, 128 * h : 128 * h + 128]
                c_ref[h, slab * SLAB : slab * SLAB + MP, :] = a + b
                c_ref[h, (8 + slab) * SLAB : (8 + slab) * SLAB + MP, :] = a - b

    even = iota((8, KP), 1) % 2 == 0
    gain = gain_ref[...]

    def waves(count):
        boths = []
        for mm in range(count):
            m = step * WAVES + mm
            left = jnp.concatenate([c_ref[h, pl.ds(m, 16, stride=SLAB), :] for h in range(2)], axis=1).astype(BF)
            boths.append(lax.dot_general(left, t_ref[m], NT, preferred_element_type=F32))
        rights = []
        for mm in range(count):
            m = step * WAVES + mm
            natural = jnp.where(even, boths[mm][:8], boths[mm][8:])
            n_ref[0, pl.ds(m, 8, stride=SLAB), :] = natural[:, :128]
            n_ref[1, pl.ds(m, 8, stride=SLAB), :] = natural[:, 128:256]
            n_ref[2, pl.ds(m, 8, stride=SLAB), :] = jnp.concatenate([natural[:, 256:], jnp.zeros((8, 384 - KP), F32)], axis=1)
            scaled = natural * pltpu.roll(gain, 768 - wave_ref[m], 1)[:, :KP]
            rights.append(jnp.concatenate([jnp.where(even, scaled, 0.0), jnp.where(even, 0.0, scaled)], axis=0).astype(BF))
        for mm in range(count):
            m = step * WAVES + mm
            back = dot(rights[mm], t_ref[m])
            north, south = back[:8] + back[8:], back[:8] - back[8:]
            for h in range(2):
                r_ref[h, pl.ds(m, 8, stride=SLAB), :] = north[:, 128 * h : 128 * h + 128]
                r_ref[2 + h, pl.ds(m, 8, stride=SLAB), :] = south[:, 128 * h : 128 * h + 128]

    for group in range(GROUPS):

        @pl.when(step == group)
        def _():
            table_copy(group).wait()

    pl.when(step < GROUPS - 1)(lambda: waves(WAVES))
    pl.when(step == GROUPS - 1)(lambda: waves(LAST))

    @pl.when(step == pl.num_programs(0) - 1)
    def _():
        for slab in range(6):
            for h in range(2):
                m_ref[slab * MP : slab * MP + MP, 128 * h : 128 * h + 128] = r_ref[2 + h, slab * SLAB : slab * SLAB + MP, :].astype(BF)
        turned = dot(m_ref[...], mirror)

        def tile_of(slab, j):
            if j < 2:
                return r_ref[j, slab * SLAB : slab * SLAB + MP, :]
            return turned[slab * MP : slab * MP + MP, 128 * (j - 2) : 128 * (j - 2) + 128]

        for pair in range(N_LAT // 2):
            for tile in range(3):
                a = tile_of(slab_of(tile, 0), pair)
                b = tile_of(slab_of(tile, 1), pair)
                lanes = slice(128 * tile, 128 * tile + 128)
                out_ref[2 * pair, :, lanes] = jnp.where(low, a, swap_halves(b)).astype(BF)
                out_ref[2 * pair + 1, :, lanes] = jnp.where(low, swap_halves(a), b).astype(BF)
        wide = iota((MP, 768), 1) < M
        zeros = jnp.zeros((MP, 384), F32)
        for item in range(GROUP):
            parts = []
            for part in range(2):
                at = (part * GROUP + item) * SLAB
                parts.append(jnp.concatenate([n_ref[h, at : at + MP, :] for h in range(3)] + [zeros], axis=1))
            value = jnp.where(wide, parts[0], pltpu.roll(parts[1], M, 1))
            spec_ref[item] = value[:OWNED, : 2 * M]


def spectral_step(waves, coeffs, table0, table1, gain):
    full = lambda *shape: pl.BlockSpec(shape, lambda i, w: (0,) * len(shape))
    return pl.pallas_call(
        spectral_kernel,
        grid_spec=pltpu.PrefetchScalarGridSpec(
            num_scalar_prefetch=1,
            grid=(GROUPS,),
            in_specs=[
                full(N_LAT, MP, 384),
                pl.BlockSpec(memory_space=pltpu.HBM),
                pl.BlockSpec(memory_space=pltpu.HBM),
                full(8, 768),
            ],
            out_specs=(full(GROUP, OWNED, 2 * M), full(N_LAT, MP, 384)),
            scratch_shapes=[
                pltpu.VMEM((2, 16 * SLAB, 128), F32),
                pltpu.VMEM((3, 8 * SLAB, 128), F32),
                pltpu.VMEM((4, 8 * SLAB, 128), F32),
                pltpu.VMEM((6 * MP, HALF), BF),
                pltpu.VMEM((OWNED, KP, HALF), BF),
                pltpu.SemaphoreType.DMA((GROUPS,)),
            ],
        ),
        out_shape=(
            pltpu.HBM((GROUP, OWNED, 2 * M), F32),
            pltpu.HBM((N_LAT, MP, 384), BF),
        ),
        compiler_params=pltpu.CompilerParams(vmem_limit_bytes=24 * 2**20),
        cost_estimate=pl.CostEstimate(flops=4 * 10**9, bytes_accessed=10**7, transcendentals=0),
        name="spectral_step",
    )(waves, coeffs, hbm(table0), hbm(table1), gain)


def one_hot(grouped):
    return (grouped.reshape(N_LAT * MP)[:, None] == jnp.arange(M, dtype=jnp.int32)[None, :]).astype(BF)


def per_device(
    state, conv_in, bias_in, conv_out, bias_out, spectral_gain, mix_in, blend_bias, mix_out, mix_out_bias, level_order, wave_order
):
    trig, quad, lat_rows, start = constants()
    band = lax.axis_index("lat")
    columns = state.reshape(VARS * LV, COLUMNS)

    tendency = first_conv(columns, conv_in.transpose(1, 2, 0), bias_in, conv_out.transpose(1, 0, 2), bias_out, level_order)
    tendency, wave_order, spectral_gain = lax.optimization_barrier((tendency, wave_order, spectral_gain))
    pieces = lax.all_to_all(tendency.reshape(N_LON, GROUP, TILES, 128), "lon", 0, 0, tiled=True)

    grouped = jnp.pad(wave_order.reshape(N_LAT, OWNED), ((0, 0), (0, MP - OWNED)), constant_values=-1)
    tables = dot(one_hot(grouped), jnp.asarray(trig[:, : 2 * NLON])).astype(BF)
    owned = lax.dynamic_slice_in_dim(grouped, band, 1, 0)[0]
    waves_f = jnp.where(owned < 0, 1000, owned).astype(F32)[:, None]
    lat_rows, start = jnp.asarray(lat_rows), jnp.asarray(start)
    gain = jnp.broadcast_to(jnp.pad(spectral_gain, (0, 768 - M))[None], (8, 768))
    owned = jnp.maximum(owned, 0)
    table0 = legendre_table(waves_f[:MH], lat_rows, start)
    pieces, table0, tables, gain, owned = lax.optimization_barrier((pieces, table0, tables, gain, owned))

    coeffs = forward_fourier(band.reshape(1), pieces, tables, jnp.asarray(quad[:, 0]))
    coeffs, waves_late = lax.optimization_barrier((coeffs, waves_f[MH:]))
    coeffs = lax.all_to_all(coeffs, "lat", 0, 0, tiled=True)
    table1 = legendre_table(waves_late, lat_rows, start)
    coeffs, table1 = lax.optimization_barrier((coeffs, table1))

    spectrum, returned = spectral_step(owned, coeffs, table0, table1, gain)
    returned, mix_in, blend_bias, mix_out, mix_out_bias, level_order, grouped = lax.optimization_barrier(
        (returned, mix_in, blend_bias, mix_out, mix_out_bias, level_order, grouped)
    )
    returned = lax.all_to_all(returned, "lat", 0, 0, tiled=True)
    m1, m2, mb = second_weights(mix_in.transpose(1, 2, 0), blend_bias, mix_out, mix_out_bias, level_order)
    inverse_tables = dot(one_hot(grouped), jnp.asarray(trig[:, 2 * NLON :])).astype(BF)
    returned, m1, m2, mb, inverse_tables = lax.optimization_barrier((returned, m1, m2, mb, inverse_tables))
    grid_values = inverse_fourier(returned.reshape(N_LAT * MP, 384), inverse_tables)
    filtered = lax.all_to_all(grid_values, "lon", 0, 0, tiled=True)
    increment = second_conv(columns, filtered.reshape(ITEMS, TILES, 128), m1, m2, mb)
    return spectrum, increment.reshape(1, VARS, LV, COLUMNS)


def solution(mesh):
    return jax.shard_map(
        per_device,
        mesh=mesh,
        in_specs=(P(None, None, None, ("lat", "lon")),) + (P(),) * 11,
        out_specs=(P("lon", "lat", None), P(None, None, None, ("lat", "lon"))),
        check_vma=False,
    )
```

```python
import functools
import math

import jax
import jax.numpy as jnp
import ml_dtypes
import numpy as np
from jax import lax
from jax.experimental import pallas as pl
from jax.experimental.pallas import tpu as pltpu
from jax.sharding import PartitionSpec as P

NLAT, NLON, M = 512, 1024, 344
LV, VARS, CH, FIELDS = 24, 6, 64, 2
N_LAT, N_LON = 8, 16
ROWS, COLS = NLAT // N_LAT, NLON // N_LON
COLUMNS = ROWS * COLS
TILES = COLUMNS // 128
ITEMS = FIELDS * LV
GROUP = ITEMS // N_LON
OWNED = M // N_LAT
MP = 48
MH = MP // 2
KP = 352
HALF = NLAT // 2
HID = CH * LV
BAND = 8
SLAB = 49
BF, F32 = jnp.bfloat16, jnp.float32
NT = (((1,), (1,)), ((), ()))

BLOCKS = {(0, 0): (0, 0), (0, 1): (0, 1), (1, 0): (0, 2), (1, 1): (1, 2), (2, 0): (1, 0), (2, 1): (1, 1)}


def slab_of(tile, half):
    part, item = BLOCKS[(tile, half)]
    return part * GROUP + item


def iota(shape, dim):
    return lax.broadcasted_iota(jnp.int32, shape, dim)


def over_levels(index):
    return jnp.floor((index.astype(F32) + 0.5) * (1.0 / LV)).astype(jnp.int32)


def hbm(x):
    return pltpu.with_memory_space_constraint(x, pltpu.HBM)


def dot(a, b):
    return jnp.dot(a, b, preferred_element_type=F32)


def row_order():
    slots = np.arange(ROWS)
    return 2 * (slots % (ROWS // 2)) + slots // (ROWS // 2)


@functools.lru_cache(None)
def constants():
    n = np.arange(M)[:, None]
    angle = 2 * np.pi * ((n * np.arange(NLON)[None, :]) % NLON) / NLON
    factor = np.where(n == 0, 1.0, 2.0) / math.sqrt(NLAT * NLON)
    trig = np.concatenate(
        [np.cos(angle) / math.sqrt(NLON), np.sin(angle) / math.sqrt(NLON), np.cos(angle) * factor, np.sin(angle) * factor],
        axis=1,
    ).astype(ml_dtypes.bfloat16)
    slots = np.arange(NLAT)
    lat = (slots // ROWS) * ROWS + row_order()[slots % ROWS]
    phi = np.pi * (lat + 0.5) / NLAT - np.pi / 2
    sine, cosine = np.sin(phi), np.cos(phi)
    quad = (np.pi * cosine / math.sqrt(NLAT)).reshape(N_LAT, 1, ROWS)
    quad = np.tile(quad, (1, 1, 2 * GROUP)).astype(np.float32)
    lat_rows = np.zeros((8, HALF), np.float32)
    lat_rows[0], lat_rows[1] = sine[:HALF], np.log(cosine[:HALF])
    start = np.zeros((1, 384), np.float32)
    start[0, :M] = [
        0.5 * math.log(0.5) + 0.5 * (math.lgamma(m + 1.5) - math.lgamma(m + 1.0) - math.lgamma(1.5)) for m in range(M)
    ]
    return trig, quad, lat_rows, start


def to_column(row):
    n = row.shape[1]
    return jnp.sum(jnp.where(iota((n, n), 0) == iota((n, n), 1), row, jnp.zeros_like(row)), axis=1, keepdims=True)


def make_weights(w1_ref, bias1_ref, w2_ref, order_ref, bias2_ref, slots_in, o1_ref, o2_ref, ob_ref):
    width, rows = o1_ref.shape[1], o2_ref.shape[0]
    variables, fields = w1_ref.shape[1], bias2_ref.shape[1]
    order = order_ref[...]
    base = VARS * LV
    column = iota((1, width), 1)
    var_col = over_levels(column)
    level_col = column - LV * var_col
    if slots_in:
        wide_order = jnp.concatenate([jnp.zeros((1, base), jnp.int32), order, jnp.zeros((1, width - base - ITEMS), jnp.int32)], axis=1)
        slot_field = (wide_order >= LV).astype(jnp.int32)
        var_col = jnp.where(column < base, var_col + FIELDS, slot_field)
        level_col = jnp.where(column < base, level_col, wide_order - LV * slot_field)
    level_col = jnp.where(column < width - 16, level_col, -100)
    pick = (iota((variables, width), 0) == var_col).astype(F32).astype(BF)
    same = (iota((CH, CH), 0) == iota((CH, CH), 1)).astype(F32).astype(BF)
    blocks = []
    for tap in range(3):
        turned = lax.dot_general(same, w1_ref[tap], NT, preferred_element_type=F32)
        blocks.append(dot((0.5 * turned).astype(BF), pick))
    bias = 0.5 * to_column(bias1_ref[...])
    high = bias.astype(BF).astype(F32)
    low = bias - high
    bias_block = jnp.where(column == width - 16, high, jnp.where(column == width - 15, low, 0.0))
    for level in range(LV):
        block = bias_block
        for tap in range(3):
            block = jnp.where(level_col == level + 2 * (tap - 1), blocks[tap], block)
        o1_ref[level * CH : (level + 1) * CH, :] = block.astype(BF)
    hidden = o2_ref.shape[1]
    if slots_in:
        row = iota((rows, 1), 0)
        level_out = (row >> 3) - 2
        field_row = row & 7
    else:
        row = to_column(order.astype(F32)).astype(jnp.int32)
        field_row = (row >= LV).astype(jnp.int32)
        level_out = row - LV * field_row
    spread2 = ((iota((CH, hidden), 1) & (CH - 1)) == iota((CH, hidden), 0)).astype(F32).astype(BF)
    level_hid = iota((1, hidden), 1) >> 6
    total2 = jnp.zeros((rows, hidden), F32)
    bias2 = jnp.zeros((rows, 128), F32)
    for tap in range(3):
        block = jnp.zeros((rows, CH), F32)
        for field in range(fields):
            taps = w2_ref[field].astype(F32)[tap : tap + 1] if slots_in else w2_ref[tap].astype(F32)[field : field + 1]
            block = jnp.where(field_row == field, taps, block)
        wide = dot(block.astype(BF), spread2)
        total2 = jnp.where(level_hid == level_out + 2 * (tap - 1), wide, total2)
    o2_ref[...] = total2.astype(BF)
    for field in range(fields):
        bias2 = jnp.where(field_row == field, bias2_ref[0:1, field : field + 1], bias2)
    ob_ref[...] = bias2


def weights_kernel(w1_ref, bias1_ref, w2_ref, order_ref, bias2_ref, o1_ref, o2_ref, ob_ref):
    make_weights(w1_ref, bias1_ref, w2_ref, order_ref, bias2_ref, True, o1_ref, o2_ref, ob_ref)


def second_weights(w1, bias1, w2, bias2, order):
    full = lambda *shape: pl.BlockSpec(shape, lambda i: (0,) * len(shape))
    width, rows = VARS * LV + ITEMS + 16, 8 * BAND
    return pl.pallas_call(
        weights_kernel,
        out_shape=(
            pltpu.HBM((HID, width), BF),
            pltpu.HBM((rows, 4 * CH), BF),
            pltpu.HBM((rows, 128), F32),
        ),
        grid=(1,),
        in_specs=[full(*w1.shape), full(1, CH), full(*w2.shape), full(1, ITEMS), full(1, bias2.shape[0])],
        out_specs=(full(HID, width), full(rows, 4 * CH), full(rows, 128)),
        compiler_params=pltpu.CompilerParams(vmem_limit_bytes=20 * 2**20),
        cost_estimate=pl.CostEstimate(flops=2 * 10**8, bytes_accessed=2 * 10**6, transcendentals=0),
        name="second_weights",
    )(hbm(w1), hbm(bias1.reshape(1, CH)), hbm(w2), hbm(order.reshape(1, ITEMS)), hbm(bias2.reshape(1, -1)))


def hidden_layer(w1_ref, v_ref, h_ref, cols):
    tall = HID // 2
    c1, c2 = 2 * math.sqrt(2 / math.pi), 8 * 0.044715 * math.sqrt(2 / math.pi)
    for row in range(0, HID, tall):
        y = dot(w1_ref[row : row + tall, :], v_ref[:, cols])
        u = y * (c1 + c2 * (y * y))
        h_ref[row : row + tall, cols] = (y + y * jnp.tanh(u)).astype(BF)


def first_kernel(
    block, state_ref, c1_ref, bias1_ref, c2_ref, order_ref, bias2_ref, out_ref, w1_ref, w2_ref, b2_ref, v_ref, h_ref, o_ref
):
    step = pl.program_id(0)

    @pl.when(step == 0)
    def _():
        make_weights(c1_ref, bias1_ref, c2_ref, order_ref, bias2_ref, False, w1_ref, w2_ref, b2_ref)
        v_ref[VARS * LV :, :] = jnp.ones((16, block), BF)

    v_ref[: VARS * LV, :] = state_ref[...]
    bias = b2_ref[...]
    for col in range(0, block, 256):
        hidden_layer(w1_ref, v_ref, h_ref, slice(col, col + 256))
        result = dot(w2_ref[...], h_ref[:, col : col + 256])
        for half in range(2):
            tile = step * (block // 128) + col // 128 + half
            o_ref[pl.ds(tile, ITEMS, stride=TILES + 1), :] = result[:, half * 128 : (half + 1) * 128] + bias

    @pl.when(step == pl.num_programs(0) - 1)
    def _():
        for item in range(ITEMS):
            out_ref[item] = o_ref[item * (TILES + 1) : item * (TILES + 1) + TILES, :].astype(BF)


def first_conv(state, w1, bias1, w2, bias2, order, block=1024):
    full = lambda *shape: pl.BlockSpec(shape, lambda i: (0,) * len(shape))
    return pl.pallas_call(
        functools.partial(first_kernel, block),
        grid=(COLUMNS // block,),
        out_shape=pltpu.HBM((ITEMS, TILES, 128), BF),
        in_specs=[
            pl.BlockSpec((VARS * LV, block), lambda i: (0, i)),
            full(*w1.shape),
            full(1, CH),
            full(*w2.shape),
            full(1, ITEMS),
            full(1, bias2.shape[0]),
        ],
        out_specs=full(ITEMS, TILES, 128),
        scratch_shapes=[
            pltpu.VMEM((HID, VARS * LV + 16), BF),
            pltpu.VMEM((ITEMS, HID), BF),
            pltpu.VMEM((ITEMS, 128), F32),
            pltpu.VMEM((VARS * LV + 16, block), BF),
            pltpu.VMEM((HID, block), BF),
            pltpu.VMEM((ITEMS * (TILES + 1), 128), F32),
        ],
        compiler_params=pltpu.CompilerParams(vmem_limit_bytes=24 * 2**20),
        cost_estimate=pl.CostEstimate(flops=3 * 10**9, bytes_accessed=2 * 10**6, transcendentals=HID * COLUMNS),
        name="first_conv",
    )(hbm(state), hbm(w1), hbm(bias1.reshape(1, CH)), hbm(w2), hbm(order.reshape(1, ITEMS)), hbm(bias2.reshape(1, -1)))


def second_kernel(block, state_ref, filt_ref, w1_ref, w2_ref, b2_ref, out_ref, v_ref, h_ref, f_ref, e_ref):
    step = pl.program_id(0)
    base = VARS * LV

    @pl.when(step == 0)
    def _():
        v_ref[base + ITEMS :, :] = jnp.ones((16, block), BF)
        for item in range(ITEMS):
            f_ref[item * (TILES + 1) : item * (TILES + 1) + TILES, :] = filt_ref[item].astype(F32)

    v_ref[:base, :] = state_ref[...]
    for tile in range(block // 128):
        piece = f_ref[pl.ds(step * (block // 128) + tile, ITEMS, stride=TILES + 1), :]
        v_ref[base : base + ITEMS, tile * 128 : (tile + 1) * 128] = piece.astype(BF)
    bias = b2_ref[0:8, :]
    for col in range(0, block, 256):
        hidden_layer(w1_ref, v_ref, h_ref, slice(col, col + 256))
        levels = [None] * LV
        for group in range(LV // 4):
            part = dot(w2_ref[...], h_ref[group * 4 * CH : (group + 1) * 4 * CH, col : col + 256])
            for at in range(BAND):
                level = 4 * group - 2 + at
                if 0 <= level < LV:
                    piece = part[8 * at : 8 * at + 8]
                    levels[level] = piece if levels[level] is None else levels[level] + piece
        for half in range(2):
            lanes = slice(col + half * 128, col + half * 128 + 128)
            for level in range(LV):
                e_ref[half, 9 * level : 9 * level + 8, :] = levels[level][:, half * 128 : (half + 1) * 128] + bias
            for variable in range(VARS):
                out_ref[variable * LV : (variable + 1) * LV, lanes] = e_ref[half, pl.ds(variable, LV, stride=9), :]


def second_conv(state, filtered, w1, w2, b2, block=1024):
    full = lambda *shape: pl.BlockSpec(shape, lambda i: (0,) * len(shape))
    width = VARS * LV + ITEMS + 16
    return pl.pallas_call(
        functools.partial(second_kernel, block),
        grid=(COLUMNS // block,),
        out_shape=pltpu.HBM((VARS * LV, COLUMNS), F32),
        in_specs=[
            pl.BlockSpec((VARS * LV, block), lambda i: (0, i)),
            pl.BlockSpec(memory_space=pltpu.VMEM),
            pl.BlockSpec(memory_space=pltpu.VMEM),
            pl.BlockSpec(memory_space=pltpu.VMEM),
            pl.BlockSpec(memory_space=pltpu.VMEM),
        ],
        out_specs=pl.BlockSpec((VARS * LV, block), lambda i: (0, i)),
        scratch_shapes=[
            pltpu.VMEM((width, block), BF),
            pltpu.VMEM((HID, block), BF),
            pltpu.VMEM((ITEMS * (TILES + 1), 128), F32),
            pltpu.VMEM((2, 9 * LV, 128), F32),
        ],
        compiler_params=pltpu.CompilerParams(vmem_limit_bytes=24 * 2**20),
        cost_estimate=pl.CostEstimate(flops=4 * 10**9, bytes_accessed=4 * 10**6, transcendentals=HID * COLUMNS),
        name="second_conv",
    )(hbm(state), filtered, w1, w2, b2)


CHUNK = 176
STRIDE = CHUNK + 1
LANES = -(-CHUNK // 128) * 128


def table_kernel(wave_ref, lat_ref, start_ref, out_ref, now_ref, old_ref, log_ref, ratio_ref, s_ref):
    step = pl.program_id(0)
    wave = jnp.broadcast_to(wave_ref[...], (MH, 128))
    sine = [lat_ref[0:1, 128 * h : 128 * h + 128] for h in range(2)]

    @pl.when(step == 0)
    def _():
        match = iota((MH, 384), 1).astype(F32) == wave_ref[...]
        start = jnp.sum(jnp.where(match, start_ref[...], 0.0), axis=1, keepdims=True)
        for h in range(2):
            log_cos = lat_ref[1:2, 128 * h : 128 * h + 128]
            log_ref[h] = jnp.where(wave > 500.0, -1e4, start + wave * log_cos)
            now_ref[h] = jnp.zeros((MH, 128), F32)
            old_ref[h] = jnp.zeros((MH, 128), F32)
        ratio_ref[...] = jnp.zeros((MH, 128), F32)

    now = [now_ref[h] for h in range(2)]
    old = [old_ref[h] for h in range(2)]
    log_scale = [log_ref[h] for h in range(2)]
    ratio = ratio_ref[...]
    scale = [None, None]
    k = (step * CHUNK).astype(F32) + iota((MH, LANES), 1).astype(F32)
    m = jnp.broadcast_to(wave_ref[...], (MH, LANES))
    n = m + k
    top = 4.0 * (n * n) - 1.0
    bottom = k * (m + n)
    root = lax.rsqrt(jnp.maximum(top * bottom, 1e-30))
    ups = jnp.where(n <= M - 1.0, top * root, 0.0)
    ratios = bottom * root
    for kk in range(CHUNK):
        if kk % 8 == 0:
            for h in range(2):
                big = jnp.abs(now[h]) > 1e8
                shrink = jnp.where(big, 1e-12, 1.0)
                now[h] = now[h] * shrink
                old[h] = old[h] * shrink
                log_scale[h] = log_scale[h] + jnp.where(big, math.log(1e12), 0.0)
                scale[h] = jnp.exp(log_scale[h])
        up = jnp.broadcast_to(ups[:, kk : kk + 1], (MH, 128))
        for h in range(2):
            stepped = up * (sine[h] * now[h] - ratio * old[h])
            if kk == 0:
                stepped = jnp.where(step == 0, 1.0, stepped)
            old[h], now[h] = now[h], stepped
            s_ref[h, pl.ds(kk, MH, stride=STRIDE), :] = stepped * scale[h]
        ratio = jnp.broadcast_to(ratios[:, kk : kk + 1], (MH, 128))
    for h in range(2):
        now_ref[h], old_ref[h], log_ref[h] = now[h], old[h], log_scale[h]
    ratio_ref[...] = ratio
    for m in range(MH):
        for h in range(2):
            out_ref[m, :, 128 * h : 128 * h + 128] = s_ref[h, m * STRIDE : m * STRIDE + CHUNK, :].astype(BF)


def legendre_table(waves_f, lat_rows, start):
    full = lambda *shape: pl.BlockSpec(shape, lambda i: (0,) * len(shape))
    return pl.pallas_call(
        table_kernel,
        grid=(KP // CHUNK,),
        out_shape=pltpu.HBM((MH, KP, HALF), BF),
        in_specs=[full(MH, 1), full(8, HALF), full(1, 384)],
        out_specs=pl.BlockSpec((MH, CHUNK, HALF), lambda i: (0, i, 0)),
        scratch_shapes=[pltpu.VMEM((2, MH, 128), F32)] * 3
        + [pltpu.VMEM((MH, 128), F32), pltpu.VMEM((2, MH * STRIDE, 128), F32)],
        compiler_params=pltpu.CompilerParams(vmem_limit_bytes=20 * 2**20),
        cost_estimate=pl.CostEstimate(flops=2 * 10**8, bytes_accessed=9 * 10**6, transcendentals=0),
        name="legendre_table",
    )(waves_f, lat_rows, start)


def swap_halves(x):
    return pltpu.roll(x, 64, 1)


def forward_kernel(y_ref, f_ref, q_ref, out_ref, x0_ref, x1_ref):
    low = iota((TILES, 128), 1) < 64
    x0_ref[192:256, :] = jnp.zeros((64, NLON), BF)
    x1_ref[0:64, :] = jnp.zeros((64, NLON), BF)
    place0, place1 = (0, 64, 128), (128, 192, 64)
    for pair in range(N_LON // 2):
        for item in range(GROUP):
            a = y_ref[2 * pair, item].astype(F32)
            b = y_ref[2 * pair + 1, item].astype(F32)
            even = jnp.where(low, a, swap_halves(b)).astype(BF)
            odd = jnp.where(low, swap_halves(a), b).astype(BF)
            lanes = slice(128 * pair, 128 * pair + 128)
            for ref, place in ((x0_ref, place0), (x1_ref, place1)):
                ref[place[item] : place[item] + 32, lanes] = even
                ref[place[item] + 32 : place[item] + 64, lanes] = odd
    quad = q_ref[...]
    cosines = lax.dot_general(f_ref[:, :NLON], x0_ref[...], NT, preferred_element_type=F32)
    sines = lax.dot_general(f_ref[:, NLON:], x1_ref[...], NT, preferred_element_type=F32)
    tiles = (cosines[:, :128], cosines[:, 128:] + sines[:, :128], sines[:, 128:])
    for t, value in enumerate(tiles):
        value = (value * quad[:, 128 * t : 128 * t + 128]).astype(BF)
        for group in range(N_LAT):
            out_ref[group, :, 128 * t : 128 * t + 128] = value[group * MP : (group + 1) * MP]


def forward_fourier(pieces, tables, quad):
    full = lambda *shape: pl.BlockSpec(shape, lambda i: (0,) * len(shape))
    return pl.pallas_call(
        forward_kernel,
        grid=(1,),
        out_shape=pltpu.HBM((N_LAT, MP, 384), BF),
        in_specs=[pl.BlockSpec(memory_space=pltpu.VMEM)] * 3,
        out_specs=full(N_LAT, MP, 384),
        scratch_shapes=[pltpu.VMEM((256, NLON), BF)] * 2,
        compiler_params=pltpu.CompilerParams(vmem_limit_bytes=20 * 2**20),
        cost_estimate=pl.CostEstimate(flops=4 * 10**8, bytes_accessed=3 * 10**6, transcendentals=0),
        name="forward_fourier",
    )(pieces, tables, quad)


def inverse_kernel(r_ref, f_ref, out_ref):
    turned = [r_ref[:, 128 * t : 128 * t + 128].astype(F32).T.astype(BF) for t in range(3)]
    cosines = jnp.concatenate([turned[0], turned[1][:64]], axis=0)
    sines = jnp.concatenate([turned[2], turned[1][64:]], axis=0)
    grid = dot(cosines, f_ref[:, :NLON]) + dot(sines, f_ref[:, NLON:])
    low = iota((TILES, 128), 1) < 64
    for pair in range(N_LON // 2):
        for item in range(GROUP):
            lanes = slice(128 * pair, 128 * pair + 128)
            even = grid[64 * item : 64 * item + 32, lanes]
            odd = grid[64 * item + 32 : 64 * item + 64, lanes]
            out_ref[2 * pair, item] = jnp.where(low, even, swap_halves(odd)).astype(BF)
            out_ref[2 * pair + 1, item] = jnp.where(low, swap_halves(even), odd).astype(BF)


def inverse_fourier(returned, tables):
    full = lambda *shape: pl.BlockSpec(shape, lambda i: (0,) * len(shape))
    return pl.pallas_call(
        inverse_kernel,
        grid=(1,),
        out_shape=pltpu.HBM((N_LON, GROUP, TILES, 128), BF),
        in_specs=[pl.BlockSpec(memory_space=pltpu.VMEM)] * 2,
        out_specs=full(N_LON, GROUP, TILES, 128),
        compiler_params=pltpu.CompilerParams(vmem_limit_bytes=20 * 2**20),
        cost_estimate=pl.CostEstimate(flops=4 * 10**8, bytes_accessed=3 * 10**6, transcendentals=0),
        name="inverse_fourier",
    )(returned, tables)


WAVES = 8
GROUPS = -(-OWNED // WAVES)
LAST = OWNED - (GROUPS - 1) * WAVES


def spectral_kernel(wave_ref, x_ref, t0_ref, t1_ref, gain_ref, spec_ref, out_ref, c_ref, n_ref, r_ref, m_ref, t_ref, sems):
    step = pl.program_id(0)
    low = iota((MP, 128), 1) < 64

    def table_copy(group):
        first, count = group * WAVES, LAST if group == GROUPS - 1 else WAVES
        source, at = (t0_ref, first) if first < MH else (t1_ref, first - MH)
        return pltpu.make_async_copy(source.at[pl.ds(at, count)], t_ref.at[pl.ds(first, count)], sems.at[group])

    @pl.when(step == 0)
    def _():
        for group in range(GROUPS):
            table_copy(group).start()

    mirror = (iota((HALF, HALF), 0) + iota((HALF, HALF), 1) == HALF - 1).astype(F32).astype(BF)

    @pl.when(step == 0)
    def _():
        for slab in (6, 7, 14, 15):
            for h in range(2):
                c_ref[h, slab * SLAB : slab * SLAB + MP, :] = jnp.zeros((MP, 128), F32)
        for slab in range(6):
            for h in range(4):
                r_ref[h, slab * SLAB + OWNED : slab * SLAB + MP, :] = jnp.zeros((MP - OWNED, 128), F32)
        for pair in range(N_LAT // 2):
            for tile in range(3):
                a = x_ref[2 * pair, :, 128 * tile : 128 * tile + 128].astype(F32)
                b = x_ref[2 * pair + 1, :, 128 * tile : 128 * tile + 128].astype(F32)
                both = jnp.where(low, a, swap_halves(b)), jnp.where(low, swap_halves(a), b)
                for half in range(2):
                    slab = slab_of(tile, half)
                    if pair < 2:
                        c_ref[pair, slab * SLAB : slab * SLAB + MP, :] = both[half]
                    else:
                        m_ref[slab * MP : slab * MP + MP, 128 * (pair - 2) : 128 * (pair - 2) + 128] = both[half].astype(BF)
        turned = dot(m_ref[...], mirror)
        for slab in range(6):
            for h in range(2):
                a = c_ref[h, slab * SLAB : slab * SLAB + MP, :]
                b = turned[slab * MP : slab * MP + MP, 128 * h : 128 * h + 128]
                c_ref[h, slab * SLAB : slab * SLAB + MP, :] = a + b
                c_ref[h, (8 + slab) * SLAB : (8 + slab) * SLAB + MP, :] = a - b

    even = iota((8, KP), 1) % 2 == 0
    gain = gain_ref[...]

    def waves(count):
        boths = []
        for mm in range(count):
            m = step * WAVES + mm
            left = jnp.concatenate([c_ref[h, pl.ds(m, 16, stride=SLAB), :] for h in range(2)], axis=1).astype(BF)
            boths.append(lax.dot_general(left, t_ref[m], NT, preferred_element_type=F32))
        rights = []
        for mm in range(count):
            m = step * WAVES + mm
            natural = jnp.where(even, boths[mm][:8], boths[mm][8:])
            n_ref[0, pl.ds(m, 8, stride=SLAB), :] = natural[:, :128]
            n_ref[1, pl.ds(m, 8, stride=SLAB), :] = natural[:, 128:256]
            n_ref[2, pl.ds(m, 8, stride=SLAB), :] = jnp.concatenate([natural[:, 256:], jnp.zeros((8, 384 - KP), F32)], axis=1)
            scaled = natural * pltpu.roll(gain, 768 - wave_ref[m], 1)[:, :KP]
            rights.append(jnp.concatenate([jnp.where(even, scaled, 0.0), jnp.where(even, 0.0, scaled)], axis=0).astype(BF))
        for mm in range(count):
            m = step * WAVES + mm
            back = dot(rights[mm], t_ref[m])
            north, south = back[:8] + back[8:], back[:8] - back[8:]
            for h in range(2):
                r_ref[h, pl.ds(m, 8, stride=SLAB), :] = north[:, 128 * h : 128 * h + 128]
                r_ref[2 + h, pl.ds(m, 8, stride=SLAB), :] = south[:, 128 * h : 128 * h + 128]

    for group in range(GROUPS):

        @pl.when(step == group)
        def _():
            table_copy(group).wait()

    pl.when(step < GROUPS - 1)(lambda: waves(WAVES))
    pl.when(step == GROUPS - 1)(lambda: waves(LAST))

    @pl.when(step == pl.num_programs(0) - 1)
    def _():
        for slab in range(6):
            for h in range(2):
                m_ref[slab * MP : slab * MP + MP, 128 * h : 128 * h + 128] = r_ref[2 + h, slab * SLAB : slab * SLAB + MP, :].astype(BF)
        turned = dot(m_ref[...], mirror)

        def tile_of(slab, j):
            if j < 2:
                return r_ref[j, slab * SLAB : slab * SLAB + MP, :]
            return turned[slab * MP : slab * MP + MP, 128 * (j - 2) : 128 * (j - 2) + 128]

        for pair in range(N_LAT // 2):
            for tile in range(3):
                a = tile_of(slab_of(tile, 0), pair)
                b = tile_of(slab_of(tile, 1), pair)
                lanes = slice(128 * tile, 128 * tile + 128)
                out_ref[2 * pair, :, lanes] = jnp.where(low, a, swap_halves(b)).astype(BF)
                out_ref[2 * pair + 1, :, lanes] = jnp.where(low, swap_halves(a), b).astype(BF)
        wide = iota((MP, 768), 1) < M
        zeros = jnp.zeros((MP, 384), F32)
        for item in range(GROUP):
            parts = []
            for part in range(2):
                at = (part * GROUP + item) * SLAB
                parts.append(jnp.concatenate([n_ref[h, at : at + MP, :] for h in range(3)] + [zeros], axis=1))
            value = jnp.where(wide, parts[0], pltpu.roll(parts[1], M, 1))
            spec_ref[item] = value[:OWNED, : 2 * M]


def spectral_step(waves, coeffs, table0, table1, gain):
    full = lambda *shape: pl.BlockSpec(shape, lambda i, w: (0,) * len(shape))
    return pl.pallas_call(
        spectral_kernel,
        grid_spec=pltpu.PrefetchScalarGridSpec(
            num_scalar_prefetch=1,
            grid=(GROUPS,),
            in_specs=[
                pl.BlockSpec(memory_space=pltpu.VMEM),
                pl.BlockSpec(memory_space=pltpu.HBM),
                pl.BlockSpec(memory_space=pltpu.HBM),
                pl.BlockSpec(memory_space=pltpu.VMEM),
            ],
            out_specs=(full(GROUP, OWNED, 2 * M), full(N_LAT, MP, 384)),
            scratch_shapes=[
                pltpu.VMEM((2, 16 * SLAB, 128), F32),
                pltpu.VMEM((3, 8 * SLAB, 128), F32),
                pltpu.VMEM((4, 8 * SLAB, 128), F32),
                pltpu.VMEM((6 * MP, HALF), BF),
                pltpu.VMEM((OWNED, KP, HALF), BF),
                pltpu.SemaphoreType.DMA((GROUPS,)),
            ],
        ),
        out_shape=(
            pltpu.HBM((GROUP, OWNED, 2 * M), F32),
            pltpu.HBM((N_LAT, MP, 384), BF),
        ),
        compiler_params=pltpu.CompilerParams(vmem_limit_bytes=24 * 2**20),
        cost_estimate=pl.CostEstimate(flops=4 * 10**9, bytes_accessed=10**7, transcendentals=0),
        name="spectral_step",
    )(waves, coeffs, hbm(table0), hbm(table1), gain)


def one_hot(grouped):
    return (grouped.reshape(N_LAT * MP)[:, None] == jnp.arange(M, dtype=jnp.int32)[None, :]).astype(BF)


def per_device(
    state, conv_in, bias_in, conv_out, bias_out, spectral_gain, mix_in, blend_bias, mix_out, mix_out_bias, level_order, wave_order
):
    trig, quad, lat_rows, start = constants()
    band = lax.axis_index("lat")
    columns = state.reshape(VARS * LV, COLUMNS)

    tendency = first_conv(columns, conv_in.transpose(1, 2, 0), bias_in, conv_out.transpose(1, 0, 2), bias_out, level_order)
    tendency, wave_order, spectral_gain = lax.optimization_barrier((tendency, wave_order, spectral_gain))
    pieces = lax.all_to_all(tendency.reshape(N_LON, GROUP, TILES, 128), "lon", 0, 0, tiled=True)

    grouped = jnp.pad(wave_order.reshape(N_LAT, OWNED), ((0, 0), (0, MP - OWNED)), constant_values=-1)
    tables = dot(one_hot(grouped), jnp.asarray(trig[:, : 2 * NLON])).astype(BF)
    owned = lax.dynamic_slice_in_dim(grouped, band, 1, 0)[0]
    waves_f = jnp.where(owned < 0, 1000, owned).astype(F32)[:, None]
    lat_rows, start = jnp.asarray(lat_rows), jnp.asarray(start)
    band_quad = lax.dynamic_slice_in_dim(jnp.asarray(quad), band, 1, 0)[0]
    gain = jnp.broadcast_to(jnp.pad(spectral_gain, (0, 768 - M))[None], (8, 768))
    owned = jnp.maximum(owned, 0)
    table0 = legendre_table(waves_f[:MH], lat_rows, start)
    pieces, table0, tables, gain, owned, band_quad = lax.optimization_barrier(
        (pieces, table0, tables, gain, owned, band_quad)
    )

    coeffs = forward_fourier(pieces, tables, band_quad)
    coeffs, waves_late = lax.optimization_barrier((coeffs, waves_f[MH:]))
    coeffs = lax.all_to_all(coeffs, "lat", 0, 0, tiled=True)
    table1 = legendre_table(waves_late, lat_rows, start)
    coeffs, table1 = lax.optimization_barrier((coeffs, table1))

    spectrum, returned = spectral_step(owned, coeffs, table0, table1, gain)
    returned, mix_in, blend_bias, mix_out, mix_out_bias, level_order, grouped = lax.optimization_barrier(
        (returned, mix_in, blend_bias, mix_out, mix_out_bias, level_order, grouped)
    )
    returned = lax.all_to_all(returned, "lat", 0, 0, tiled=True)
    m1, m2, mb = second_weights(mix_in.transpose(1, 2, 0), blend_bias, mix_out, mix_out_bias, level_order)
    inverse_tables = dot(one_hot(grouped), jnp.asarray(trig[:, 2 * NLON :])).astype(BF)
    returned, m1, m2, mb, inverse_tables = lax.optimization_barrier((returned, m1, m2, mb, inverse_tables))
    grid_values = inverse_fourier(returned.reshape(N_LAT * MP, 384), inverse_tables)
    filtered = lax.all_to_all(grid_values, "lon", 0, 0, tiled=True)
    increment = second_conv(columns, filtered.reshape(ITEMS, TILES, 128), m1, m2, mb)
    return spectrum, increment.reshape(1, VARS, LV, COLUMNS)


def solution(mesh):
    return jax.shard_map(
        per_device,
        mesh=mesh,
        in_specs=(P(None, None, None, ("lat", "lon")),) + (P(),) * 11,
        out_specs=(P("lon", "lat", None), P(None, None, None, ("lat", "lon"))),
        check_vma=False,
    )
```

```python
import functools
import math

import jax
import jax.numpy as jnp
import ml_dtypes
import numpy as np
from jax import lax
from jax.experimental import pallas as pl
from jax.experimental.pallas import tpu as pltpu
from jax.sharding import PartitionSpec as P

NLAT, NLON, M = 512, 1024, 344
LV, VARS, CH, FIELDS = 24, 6, 64, 2
N_LAT, N_LON = 8, 16
ROWS, COLS = NLAT // N_LAT, NLON // N_LON
COLUMNS = ROWS * COLS
TILES = COLUMNS // 128
ITEMS = FIELDS * LV
GROUP = ITEMS // N_LON
OWNED = M // N_LAT
MP = 48
MH = MP // 2
KP = 352
HALF = NLAT // 2
HID = CH * LV
BAND = 8
SLAB = 49
BF, F32 = jnp.bfloat16, jnp.float32
NT = (((1,), (1,)), ((), ()))

BLOCKS = {(0, 0): (0, 0), (0, 1): (0, 1), (1, 0): (0, 2), (1, 1): (1, 2), (2, 0): (1, 0), (2, 1): (1, 1)}


def slab_of(tile, half):
    part, item = BLOCKS[(tile, half)]
    return part * GROUP + item


def iota(shape, dim):
    return lax.broadcasted_iota(jnp.int32, shape, dim)


def over_levels(index):
    return jnp.floor((index.astype(F32) + 0.5) * (1.0 / LV)).astype(jnp.int32)


def hbm(x):
    return pltpu.with_memory_space_constraint(x, pltpu.HBM)


def dot(a, b):
    return jnp.dot(a, b, preferred_element_type=F32)


def row_order():
    slots = np.arange(ROWS)
    return 2 * (slots % (ROWS // 2)) + slots // (ROWS // 2)


@functools.lru_cache(None)
def constants():
    n = np.arange(M)[:, None]
    angle = 2 * np.pi * ((n * np.arange(NLON)[None, :]) % NLON) / NLON
    factor = np.where(n == 0, 1.0, 2.0) / math.sqrt(NLAT * NLON)
    trig = np.concatenate(
        [np.cos(angle) / math.sqrt(NLON), np.sin(angle) / math.sqrt(NLON), np.cos(angle) * factor, np.sin(angle) * factor],
        axis=1,
    ).astype(ml_dtypes.bfloat16)
    slots = np.arange(NLAT)
    lat = (slots // ROWS) * ROWS + row_order()[slots % ROWS]
    phi = np.pi * (lat + 0.5) / NLAT - np.pi / 2
    sine, cosine = np.sin(phi), np.cos(phi)
    quad = (np.pi * cosine / math.sqrt(NLAT)).reshape(N_LAT, 1, ROWS)
    quad = np.tile(quad, (1, 1, 2 * GROUP)).astype(np.float32)
    lat_rows = np.zeros((8, HALF), np.float32)
    lat_rows[0], lat_rows[1] = sine[:HALF], np.log(cosine[:HALF])
    start = np.zeros((1, 384), np.float32)
    start[0, :M] = [
        0.5 * math.log(0.5) + 0.5 * (math.lgamma(m + 1.5) - math.lgamma(m + 1.0) - math.lgamma(1.5)) for m in range(M)
    ]
    return trig, quad, lat_rows, start


def to_column(row):
    n = row.shape[1]
    return jnp.sum(jnp.where(iota((n, n), 0) == iota((n, n), 1), row, jnp.zeros_like(row)), axis=1, keepdims=True)


def make_weights(w1_ref, bias1_ref, w2_ref, order_ref, bias2_ref, slots_in, o1_ref, o2_ref, ob_ref):
    width, rows = o1_ref.shape[1], o2_ref.shape[0]
    variables, fields = w1_ref.shape[1], bias2_ref.shape[1]
    order = order_ref[...]
    base = VARS * LV
    column = iota((1, width), 1)
    var_col = over_levels(column)
    level_col = column - LV * var_col
    if slots_in:
        wide_order = jnp.concatenate([jnp.zeros((1, base), jnp.int32), order, jnp.zeros((1, width - base - ITEMS), jnp.int32)], axis=1)
        slot_field = (wide_order >= LV).astype(jnp.int32)
        var_col = jnp.where(column < base, var_col + FIELDS, slot_field)
        level_col = jnp.where(column < base, level_col, wide_order - LV * slot_field)
    level_col = jnp.where(column < width - 16, level_col, -100)
    pick = (iota((variables, width), 0) == var_col).astype(F32).astype(BF)
    same = (iota((CH, CH), 0) == iota((CH, CH), 1)).astype(F32).astype(BF)
    blocks = []
    for tap in range(3):
        turned = lax.dot_general(same, w1_ref[tap], NT, preferred_element_type=F32)
        blocks.append(dot((0.5 * turned).astype(BF), pick))
    bias = 0.5 * to_column(bias1_ref[...])
    high = bias.astype(BF).astype(F32)
    low = bias - high
    bias_block = jnp.where(column == width - 16, high, jnp.where(column == width - 15, low, 0.0))
    for level in range(LV):
        block = bias_block
        for tap in range(3):
            block = jnp.where(level_col == level + 2 * (tap - 1), blocks[tap], block)
        o1_ref[level * CH : (level + 1) * CH, :] = block.astype(BF)
    hidden = o2_ref.shape[1]
    if slots_in:
        row = iota((rows, 1), 0)
        level_out = (row >> 3) - 2
        field_row = row & 7
    else:
        row = to_column(order.astype(F32)).astype(jnp.int32)
        field_row = (row >= LV).astype(jnp.int32)
        level_out = row - LV * field_row
    spread2 = ((iota((CH, hidden), 1) & (CH - 1)) == iota((CH, hidden), 0)).astype(F32).astype(BF)
    level_hid = iota((1, hidden), 1) >> 6
    total2 = jnp.zeros((rows, hidden), F32)
    bias2 = jnp.zeros((rows, 128), F32)
    for tap in range(3):
        block = jnp.zeros((rows, CH), F32)
        for field in range(fields):
            taps = w2_ref[field].astype(F32)[tap : tap + 1] if slots_in else w2_ref[tap].astype(F32)[field : field + 1]
            block = jnp.where(field_row == field, taps, block)
        wide = dot(block.astype(BF), spread2)
        total2 = jnp.where(level_hid == level_out + 2 * (tap - 1), wide, total2)
    o2_ref[...] = total2.astype(BF)
    for field in range(fields):
        bias2 = jnp.where(field_row == field, bias2_ref[0:1, field : field + 1], bias2)
    ob_ref[...] = bias2


def weights_kernel(w1_ref, bias1_ref, w2_ref, order_ref, bias2_ref, o1_ref, o2_ref, ob_ref):
    make_weights(w1_ref, bias1_ref, w2_ref, order_ref, bias2_ref, True, o1_ref, o2_ref, ob_ref)


def second_weights(w1, bias1, w2, bias2, order):
    full = lambda *shape: pl.BlockSpec(shape, lambda i: (0,) * len(shape))
    width, rows = VARS * LV + ITEMS + 16, 8 * BAND
    return pl.pallas_call(
        weights_kernel,
        out_shape=(
            pltpu.HBM((HID, width), BF),
            pltpu.HBM((rows, 4 * CH), BF),
            pltpu.HBM((rows, 128), F32),
        ),
        grid=(1,),
        in_specs=[full(*w1.shape), full(1, CH), full(*w2.shape), full(1, ITEMS), full(1, bias2.shape[0])],
        out_specs=(full(HID, width), full(rows, 4 * CH), full(rows, 128)),
        compiler_params=pltpu.CompilerParams(vmem_limit_bytes=20 * 2**20),
        cost_estimate=pl.CostEstimate(flops=2 * 10**8, bytes_accessed=2 * 10**6, transcendentals=0),
        name="second_weights",
    )(hbm(w1), hbm(bias1.reshape(1, CH)), hbm(w2), hbm(order.reshape(1, ITEMS)), hbm(bias2.reshape(1, -1)))


def hidden_layer(w1_ref, v_ref, h_ref, cols):
    tall = HID // 2
    c1, c2 = 2 * math.sqrt(2 / math.pi), 8 * 0.044715 * math.sqrt(2 / math.pi)
    for row in range(0, HID, tall):
        y = dot(w1_ref[row : row + tall, :], v_ref[:, cols])
        u = y * (c1 + c2 * (y * y))
        h_ref[row : row + tall, cols] = (y + y * jnp.tanh(u)).astype(BF)


def first_kernel(
    block, state_ref, c1_ref, bias1_ref, c2_ref, order_ref, bias2_ref, out_ref, w1_ref, w2_ref, b2_ref, v_ref, h_ref, o_ref
):
    step = pl.program_id(0)

    @pl.when(step == 0)
    def _():
        make_weights(c1_ref, bias1_ref, c2_ref, order_ref, bias2_ref, False, w1_ref, w2_ref, b2_ref)
        v_ref[VARS * LV :, :] = jnp.ones((16, block), BF)

    v_ref[: VARS * LV, :] = state_ref[...]
    bias = b2_ref[...]
    for col in range(0, block, 256):
        hidden_layer(w1_ref, v_ref, h_ref, slice(col, col + 256))
        result = dot(w2_ref[...], h_ref[:, col : col + 256])
        for half in range(2):
            tile = step * (block // 128) + col // 128 + half
            o_ref[pl.ds(tile, ITEMS, stride=TILES + 1), :] = result[:, half * 128 : (half + 1) * 128] + bias

    @pl.when(step == pl.num_programs(0) - 1)
    def _():
        for item in range(ITEMS):
            out_ref[item] = o_ref[item * (TILES + 1) : item * (TILES + 1) + TILES, :].astype(BF)


def first_conv(state, w1, bias1, w2, bias2, order, block=COLUMNS):
    full = lambda *shape: pl.BlockSpec(shape, lambda i: (0,) * len(shape))
    return pl.pallas_call(
        functools.partial(first_kernel, block),
        grid=(COLUMNS // block,),
        out_shape=pltpu.HBM((ITEMS, TILES, 128), BF),
        in_specs=[
            pl.BlockSpec((VARS * LV, block), lambda i: (0, i)),
            full(*w1.shape),
            full(1, CH),
            full(*w2.shape),
            full(1, ITEMS),
            full(1, bias2.shape[0]),
        ],
        out_specs=full(ITEMS, TILES, 128),
        scratch_shapes=[
            pltpu.VMEM((HID, VARS * LV + 16), BF),
            pltpu.VMEM((ITEMS, HID), BF),
            pltpu.VMEM((ITEMS, 128), F32),
            pltpu.VMEM((VARS * LV + 16, block), BF),
            pltpu.VMEM((HID, block), BF),
            pltpu.VMEM((ITEMS * (TILES + 1), 128), F32),
        ],
        compiler_params=pltpu.CompilerParams(vmem_limit_bytes=40 * 2**20),
        cost_estimate=pl.CostEstimate(flops=3 * 10**9, bytes_accessed=2 * 10**6, transcendentals=HID * COLUMNS),
        name="first_conv",
    )(hbm(state), hbm(w1), hbm(bias1.reshape(1, CH)), hbm(w2), hbm(order.reshape(1, ITEMS)), hbm(bias2.reshape(1, -1)))


def second_kernel(block, state_ref, filt_ref, w1_ref, w2_ref, b2_ref, out_ref, v_ref, h_ref, f_ref, e_ref):
    step = pl.program_id(0)
    base = VARS * LV

    @pl.when(step == 0)
    def _():
        v_ref[base + ITEMS :, :] = jnp.ones((16, block), BF)
        for item in range(ITEMS):
            f_ref[item * (TILES + 1) : item * (TILES + 1) + TILES, :] = filt_ref[item].astype(F32)

    v_ref[:base, :] = state_ref[...]
    for tile in range(block // 128):
        piece = f_ref[pl.ds(step * (block // 128) + tile, ITEMS, stride=TILES + 1), :]
        v_ref[base : base + ITEMS, tile * 128 : (tile + 1) * 128] = piece.astype(BF)
    bias = b2_ref[0:8, :]
    for col in range(0, block, 256):
        hidden_layer(w1_ref, v_ref, h_ref, slice(col, col + 256))
        levels = [None] * LV
        for group in range(LV // 4):
            part = dot(w2_ref[...], h_ref[group * 4 * CH : (group + 1) * 4 * CH, col : col + 256])
            for at in range(BAND):
                level = 4 * group - 2 + at
                if 0 <= level < LV:
                    piece = part[8 * at : 8 * at + 8]
                    levels[level] = piece if levels[level] is None else levels[level] + piece
        for half in range(2):
            lanes = slice(col + half * 128, col + half * 128 + 128)
            for level in range(LV):
                e_ref[half, 9 * level : 9 * level + 8, :] = levels[level][:, half * 128 : (half + 1) * 128] + bias
            for variable in range(VARS):
                out_ref[variable * LV : (variable + 1) * LV, lanes] = e_ref[half, pl.ds(variable, LV, stride=9), :]


def second_conv(state, filtered, w1, w2, b2, block=2048):
    full = lambda *shape: pl.BlockSpec(shape, lambda i: (0,) * len(shape))
    width = VARS * LV + ITEMS + 16
    return pl.pallas_call(
        functools.partial(second_kernel, block),
        grid=(COLUMNS // block,),
        out_shape=pltpu.HBM((VARS * LV, COLUMNS), F32),
        in_specs=[
            pl.BlockSpec((VARS * LV, block), lambda i: (0, i)),
            pl.BlockSpec(memory_space=pltpu.VMEM),
            pl.BlockSpec(memory_space=pltpu.VMEM),
            pl.BlockSpec(memory_space=pltpu.VMEM),
            pl.BlockSpec(memory_space=pltpu.VMEM),
        ],
        out_specs=pl.BlockSpec((VARS * LV, block), lambda i: (0, i)),
        scratch_shapes=[
            pltpu.VMEM((width, block), BF),
            pltpu.VMEM((HID, block), BF),
            pltpu.VMEM((ITEMS * (TILES + 1), 128), F32),
            pltpu.VMEM((2, 9 * LV, 128), F32),
        ],
        compiler_params=pltpu.CompilerParams(vmem_limit_bytes=40 * 2**20),
        cost_estimate=pl.CostEstimate(flops=4 * 10**9, bytes_accessed=4 * 10**6, transcendentals=HID * COLUMNS),
        name="second_conv",
    )(hbm(state), filtered, w1, w2, b2)


CHUNK = 176
STRIDE = CHUNK + 1
LANES = -(-CHUNK // 128) * 128


def table_kernel(wave_ref, lat_ref, start_ref, out_ref, now_ref, old_ref, log_ref, ratio_ref, s_ref):
    step = pl.program_id(0)
    wave = jnp.broadcast_to(wave_ref[...], (MH, 128))
    sine = [lat_ref[0:1, 128 * h : 128 * h + 128] for h in range(2)]

    @pl.when(step == 0)
    def _():
        match = iota((MH, 384), 1).astype(F32) == wave_ref[...]
        start = jnp.sum(jnp.where(match, start_ref[...], 0.0), axis=1, keepdims=True)
        for h in range(2):
            log_cos = lat_ref[1:2, 128 * h : 128 * h + 128]
            log_ref[h] = jnp.where(wave > 500.0, -1e4, start + wave * log_cos)
            now_ref[h] = jnp.zeros((MH, 128), F32)
            old_ref[h] = jnp.zeros((MH, 128), F32)
        ratio_ref[...] = jnp.zeros((MH, 128), F32)

    now = [now_ref[h] for h in range(2)]
    old = [old_ref[h] for h in range(2)]
    log_scale = [log_ref[h] for h in range(2)]
    ratio = ratio_ref[...]
    scale = [None, None]
    k = (step * CHUNK).astype(F32) + iota((MH, LANES), 1).astype(F32)
    m = jnp.broadcast_to(wave_ref[...], (MH, LANES))
    n = m + k
    top = 4.0 * (n * n) - 1.0
    bottom = k * (m + n)
    root = lax.rsqrt(jnp.maximum(top * bottom, 1e-30))
    ups = jnp.where(n <= M - 1.0, top * root, 0.0)
    ratios = bottom * root
    for kk in range(CHUNK):
        if kk % 8 == 0:
            for h in range(2):
                big = jnp.abs(now[h]) > 1e8
                shrink = jnp.where(big, 1e-12, 1.0)
                now[h] = now[h] * shrink
                old[h] = old[h] * shrink
                log_scale[h] = log_scale[h] + jnp.where(big, math.log(1e12), 0.0)
                scale[h] = jnp.exp(log_scale[h])
        up = jnp.broadcast_to(ups[:, kk : kk + 1], (MH, 128))
        for h in range(2):
            stepped = up * (sine[h] * now[h] - ratio * old[h])
            if kk == 0:
                stepped = jnp.where(step == 0, 1.0, stepped)
            old[h], now[h] = now[h], stepped
            s_ref[h, pl.ds(kk, MH, stride=STRIDE), :] = stepped * scale[h]
        ratio = jnp.broadcast_to(ratios[:, kk : kk + 1], (MH, 128))
    for h in range(2):
        now_ref[h], old_ref[h], log_ref[h] = now[h], old[h], log_scale[h]
    ratio_ref[...] = ratio
    for m in range(MH):
        for h in range(2):
            out_ref[m, :, 128 * h : 128 * h + 128] = s_ref[h, m * STRIDE : m * STRIDE + CHUNK, :].astype(BF)


def legendre_table(waves_f, lat_rows, start):
    full = lambda *shape: pl.BlockSpec(shape, lambda i: (0,) * len(shape))
    return pl.pallas_call(
        table_kernel,
        grid=(KP // CHUNK,),
        out_shape=pltpu.HBM((MH, KP, HALF), BF),
        in_specs=[full(MH, 1), full(8, HALF), full(1, 384)],
        out_specs=pl.BlockSpec((MH, CHUNK, HALF), lambda i: (0, i, 0)),
        scratch_shapes=[pltpu.VMEM((2, MH, 128), F32)] * 3
        + [pltpu.VMEM((MH, 128), F32), pltpu.VMEM((2, MH * STRIDE, 128), F32)],
        compiler_params=pltpu.CompilerParams(vmem_limit_bytes=20 * 2**20),
        cost_estimate=pl.CostEstimate(flops=2 * 10**8, bytes_accessed=9 * 10**6, transcendentals=0),
        name="legendre_table",
    )(waves_f, lat_rows, start)


def swap_halves(x):
    return pltpu.roll(x, 64, 1)


def forward_kernel(y_ref, f_ref, q_ref, out_ref, x0_ref, x1_ref):
    low = iota((TILES, 128), 1) < 64
    x0_ref[192:256, :] = jnp.zeros((64, NLON), BF)
    x1_ref[0:64, :] = jnp.zeros((64, NLON), BF)
    place0, place1 = (0, 64, 128), (128, 192, 64)
    for pair in range(N_LON // 2):
        for item in range(GROUP):
            a = y_ref[2 * pair, item].astype(F32)
            b = y_ref[2 * pair + 1, item].astype(F32)
            even = jnp.where(low, a, swap_halves(b)).astype(BF)
            odd = jnp.where(low, swap_halves(a), b).astype(BF)
            lanes = slice(128 * pair, 128 * pair + 128)
            for ref, place in ((x0_ref, place0), (x1_ref, place1)):
                ref[place[item] : place[item] + 32, lanes] = even
                ref[place[item] + 32 : place[item] + 64, lanes] = odd
    quad = q_ref[pl.ds(lax.axis_index("lat"), 1), :]
    cosines = lax.dot_general(f_ref[:, :NLON], x0_ref[...], NT, preferred_element_type=F32)
    sines = lax.dot_general(f_ref[:, NLON:], x1_ref[...], NT, preferred_element_type=F32)
    tiles = (cosines[:, :128], cosines[:, 128:] + sines[:, :128], sines[:, 128:])
    for t, value in enumerate(tiles):
        value = (value * quad[:, 128 * t : 128 * t + 128]).astype(BF)
        for group in range(N_LAT):
            out_ref[group, :, 128 * t : 128 * t + 128] = value[group * MP : (group + 1) * MP]


def forward_fourier(pieces, tables, quad):
    full = lambda *shape: pl.BlockSpec(shape, lambda i: (0,) * len(shape))
    return pl.pallas_call(
        forward_kernel,
        grid=(1,),
        out_shape=pltpu.HBM((N_LAT, MP, 384), BF),
        in_specs=[pl.BlockSpec(memory_space=pltpu.VMEM)] * 3,
        out_specs=full(N_LAT, MP, 384),
        scratch_shapes=[pltpu.VMEM((256, NLON), BF)] * 2,
        compiler_params=pltpu.CompilerParams(vmem_limit_bytes=20 * 2**20),
        cost_estimate=pl.CostEstimate(flops=4 * 10**8, bytes_accessed=3 * 10**6, transcendentals=0),
        name="forward_fourier",
    )(pieces, tables, quad)


def inverse_kernel(r_ref, f_ref, out_ref):
    turned = [r_ref[:, 128 * t : 128 * t + 128].astype(F32).T.astype(BF) for t in range(3)]
    cosines = jnp.concatenate([turned[0], turned[1][:64]], axis=0)
    sines = jnp.concatenate([turned[2], turned[1][64:]], axis=0)
    grid = dot(cosines, f_ref[:, :NLON]) + dot(sines, f_ref[:, NLON:])
    low = iota((TILES, 128), 1) < 64
    for pair in range(N_LON // 2):
        for item in range(GROUP):
            lanes = slice(128 * pair, 128 * pair + 128)
            even = grid[64 * item : 64 * item + 32, lanes]
            odd = grid[64 * item + 32 : 64 * item + 64, lanes]
            out_ref[2 * pair, item] = jnp.where(low, even, swap_halves(odd)).astype(BF)
            out_ref[2 * pair + 1, item] = jnp.where(low, swap_halves(even), odd).astype(BF)


def inverse_fourier(returned, tables):
    full = lambda *shape: pl.BlockSpec(shape, lambda i: (0,) * len(shape))
    return pl.pallas_call(
        inverse_kernel,
        grid=(1,),
        out_shape=pltpu.HBM((N_LON, GROUP, TILES, 128), BF),
        in_specs=[pl.BlockSpec(memory_space=pltpu.VMEM)] * 2,
        out_specs=full(N_LON, GROUP, TILES, 128),
        compiler_params=pltpu.CompilerParams(vmem_limit_bytes=20 * 2**20),
        cost_estimate=pl.CostEstimate(flops=4 * 10**8, bytes_accessed=3 * 10**6, transcendentals=0),
        name="inverse_fourier",
    )(returned, tables)


WAVES = 8
GROUPS = -(-OWNED // WAVES)
LAST = OWNED - (GROUPS - 1) * WAVES


def spectral_kernel(wave_ref, x_ref, t0_ref, t1_ref, gain_ref, spec_ref, out_ref, c_ref, n_ref, r_ref, m_ref, t_ref, sems):
    step = pl.program_id(0)
    low = iota((MP, 128), 1) < 64

    def table_copy(group):
        first, count = group * WAVES, LAST if group == GROUPS - 1 else WAVES
        source, at = (t0_ref, first) if first < MH else (t1_ref, first - MH)
        return pltpu.make_async_copy(source.at[pl.ds(at, count)], t_ref.at[pl.ds(first, count)], sems.at[group])

    @pl.when(step == 0)
    def _():
        for group in range(GROUPS):
            table_copy(group).start()

    mirror = (iota((HALF, HALF), 0) + iota((HALF, HALF), 1) == HALF - 1).astype(F32).astype(BF)

    @pl.when(step == 0)
    def _():
        for slab in (6, 7, 14, 15):
            for h in range(2):
                c_ref[h, slab * SLAB : slab * SLAB + MP, :] = jnp.zeros((MP, 128), F32)
        for slab in range(6):
            for h in range(4):
                r_ref[h, slab * SLAB + OWNED : slab * SLAB + MP, :] = jnp.zeros((MP - OWNED, 128), F32)
        for pair in range(N_LAT // 2):
            for tile in range(3):
                a = x_ref[2 * pair, :, 128 * tile : 128 * tile + 128].astype(F32)
                b = x_ref[2 * pair + 1, :, 128 * tile : 128 * tile + 128].astype(F32)
                both = jnp.where(low, a, swap_halves(b)), jnp.where(low, swap_halves(a), b)
                for half in range(2):
                    slab = slab_of(tile, half)
                    if pair < 2:
                        c_ref[pair, slab * SLAB : slab * SLAB + MP, :] = both[half]
                    else:
                        m_ref[slab * MP : slab * MP + MP, 128 * (pair - 2) : 128 * (pair - 2) + 128] = both[half].astype(BF)
        turned = dot(m_ref[...], mirror)
        for slab in range(6):
            for h in range(2):
                a = c_ref[h, slab * SLAB : slab * SLAB + MP, :]
                b = turned[slab * MP : slab * MP + MP, 128 * h : 128 * h + 128]
                c_ref[h, slab * SLAB : slab * SLAB + MP, :] = a + b
                c_ref[h, (8 + slab) * SLAB : (8 + slab) * SLAB + MP, :] = a - b

    even = iota((8, KP), 1) % 2 == 0
    gain = gain_ref[...]

    def waves(count):
        boths = []
        for mm in range(count):
            m = step * WAVES + mm
            left = jnp.concatenate([c_ref[h, pl.ds(m, 16, stride=SLAB), :] for h in range(2)], axis=1).astype(BF)
            boths.append(lax.dot_general(left, t_ref[m], NT, preferred_element_type=F32))
        rights = []
        for mm in range(count):
            m = step * WAVES + mm
            natural = jnp.where(even, boths[mm][:8], boths[mm][8:])
            n_ref[0, pl.ds(m, 8, stride=SLAB), :] = natural[:, :128]
            n_ref[1, pl.ds(m, 8, stride=SLAB), :] = natural[:, 128:256]
            n_ref[2, pl.ds(m, 8, stride=SLAB), :] = jnp.concatenate([natural[:, 256:], jnp.zeros((8, 384 - KP), F32)], axis=1)
            scaled = natural * pltpu.roll(gain, 768 - wave_ref[m], 1)[:, :KP]
            rights.append(jnp.concatenate([jnp.where(even, scaled, 0.0), jnp.where(even, 0.0, scaled)], axis=0).astype(BF))
        for mm in range(count):
            m = step * WAVES + mm
            back = dot(rights[mm], t_ref[m])
            north, south = back[:8] + back[8:], back[:8] - back[8:]
            for h in range(2):
                r_ref[h, pl.ds(m, 8, stride=SLAB), :] = north[:, 128 * h : 128 * h + 128]
                r_ref[2 + h, pl.ds(m, 8, stride=SLAB), :] = south[:, 128 * h : 128 * h + 128]

    for group in range(GROUPS):

        @pl.when(step == group)
        def _():
            table_copy(group).wait()

    pl.when(step < GROUPS - 1)(lambda: waves(WAVES))
    pl.when(step == GROUPS - 1)(lambda: waves(LAST))

    @pl.when(step == pl.num_programs(0) - 1)
    def _():
        for slab in range(6):
            for h in range(2):
                m_ref[slab * MP : slab * MP + MP, 128 * h : 128 * h + 128] = r_ref[2 + h, slab * SLAB : slab * SLAB + MP, :].astype(BF)
        turned = dot(m_ref[...], mirror)

        def tile_of(slab, j):
            if j < 2:
                return r_ref[j, slab * SLAB : slab * SLAB + MP, :]
            return turned[slab * MP : slab * MP + MP, 128 * (j - 2) : 128 * (j - 2) + 128]

        for pair in range(N_LAT // 2):
            for tile in range(3):
                a = tile_of(slab_of(tile, 0), pair)
                b = tile_of(slab_of(tile, 1), pair)
                lanes = slice(128 * tile, 128 * tile + 128)
                out_ref[2 * pair, :, lanes] = jnp.where(low, a, swap_halves(b)).astype(BF)
                out_ref[2 * pair + 1, :, lanes] = jnp.where(low, swap_halves(a), b).astype(BF)
        wide = iota((MP, 768), 1) < M
        zeros = jnp.zeros((MP, 384), F32)
        for item in range(GROUP):
            parts = []
            for part in range(2):
                at = (part * GROUP + item) * SLAB
                parts.append(jnp.concatenate([n_ref[h, at : at + MP, :] for h in range(3)] + [zeros], axis=1))
            value = jnp.where(wide, parts[0], pltpu.roll(parts[1], M, 1))
            spec_ref[item] = value[:OWNED, : 2 * M]


def spectral_step(waves, coeffs, table0, table1, gain):
    full = lambda *shape: pl.BlockSpec(shape, lambda i, w: (0,) * len(shape))
    return pl.pallas_call(
        spectral_kernel,
        grid_spec=pltpu.PrefetchScalarGridSpec(
            num_scalar_prefetch=1,
            grid=(GROUPS,),
            in_specs=[
                pl.BlockSpec(memory_space=pltpu.VMEM),
                pl.BlockSpec(memory_space=pltpu.HBM),
                pl.BlockSpec(memory_space=pltpu.HBM),
                pl.BlockSpec(memory_space=pltpu.VMEM),
            ],
            out_specs=(full(GROUP, OWNED, 2 * M), full(N_LAT, MP, 384)),
            scratch_shapes=[
                pltpu.VMEM((2, 16 * SLAB, 128), F32),
                pltpu.VMEM((3, 8 * SLAB, 128), F32),
                pltpu.VMEM((4, 8 * SLAB, 128), F32),
                pltpu.VMEM((6 * MP, HALF), BF),
                pltpu.VMEM((OWNED, KP, HALF), BF),
                pltpu.SemaphoreType.DMA((GROUPS,)),
            ],
        ),
        out_shape=(
            pltpu.HBM((GROUP, OWNED, 2 * M), F32),
            pltpu.HBM((N_LAT, MP, 384), BF),
        ),
        compiler_params=pltpu.CompilerParams(vmem_limit_bytes=24 * 2**20),
        cost_estimate=pl.CostEstimate(flops=4 * 10**9, bytes_accessed=10**7, transcendentals=0),
        name="spectral_step",
    )(waves, coeffs, hbm(table0), hbm(table1), gain)


def one_hot(grouped):
    return (grouped.reshape(N_LAT * MP)[:, None] == jnp.arange(M, dtype=jnp.int32)[None, :]).astype(BF)


def per_device(
    state, conv_in, bias_in, conv_out, bias_out, spectral_gain, mix_in, blend_bias, mix_out, mix_out_bias, level_order, wave_order
):
    trig, quad, lat_rows, start = constants()
    band = lax.axis_index("lat")
    columns = state.reshape(VARS * LV, COLUMNS)

    tendency = first_conv(columns, conv_in.transpose(1, 2, 0), bias_in, conv_out.transpose(1, 0, 2), bias_out, level_order)
    tendency, wave_order, spectral_gain = lax.optimization_barrier((tendency, wave_order, spectral_gain))
    pieces = lax.all_to_all(tendency.reshape(N_LON, GROUP, TILES, 128), "lon", 0, 0, tiled=True)

    grouped = jnp.pad(wave_order.reshape(N_LAT, OWNED), ((0, 0), (0, MP - OWNED)), constant_values=-1)
    tables = dot(one_hot(grouped), jnp.asarray(trig[:, : 2 * NLON])).astype(BF)
    owned = lax.dynamic_slice_in_dim(grouped, band, 1, 0)[0]
    waves_f = jnp.where(owned < 0, 1000, owned).astype(F32)[:, None]
    lat_rows, start = jnp.asarray(lat_rows), jnp.asarray(start)
    band_quad = jnp.asarray(quad[:, 0])
    gain = jnp.broadcast_to(jnp.pad(spectral_gain, (0, 768 - M))[None], (8, 768))
    owned = jnp.maximum(owned, 0)
    table0 = legendre_table(waves_f[:MH], lat_rows, start)
    pieces, table0, tables, gain, owned, band_quad = lax.optimization_barrier(
        (pieces, table0, tables, gain, owned, band_quad)
    )

    coeffs = forward_fourier(pieces, tables, band_quad)
    coeffs, waves_late = lax.optimization_barrier((coeffs, waves_f[MH:]))
    coeffs = lax.all_to_all(coeffs, "lat", 0, 0, tiled=True)
    table1 = legendre_table(waves_late, lat_rows, start)
    coeffs, table1 = lax.optimization_barrier((coeffs, table1))

    spectrum, returned = spectral_step(owned, coeffs, table0, table1, gain)
    returned, mix_in, blend_bias, mix_out, mix_out_bias, level_order, grouped = lax.optimization_barrier(
        (returned, mix_in, blend_bias, mix_out, mix_out_bias, level_order, grouped)
    )
    returned = lax.all_to_all(returned, "lat", 0, 0, tiled=True)
    m1, m2, mb = second_weights(mix_in.transpose(1, 2, 0), blend_bias, mix_out, mix_out_bias, level_order)
    inverse_tables = dot(one_hot(grouped), jnp.asarray(trig[:, 2 * NLON :])).astype(BF)
    returned, m1, m2, mb, inverse_tables = lax.optimization_barrier((returned, m1, m2, mb, inverse_tables))
    grid_values = inverse_fourier(returned.reshape(N_LAT * MP, 384), inverse_tables)
    filtered = lax.all_to_all(grid_values, "lon", 0, 0, tiled=True)
    increment = second_conv(columns, filtered.reshape(ITEMS, TILES, 128), m1, m2, mb)
    return spectrum, increment.reshape(1, VARS, LV, COLUMNS)


def solution(mesh):
    return jax.shard_map(
        per_device,
        mesh=mesh,
        in_specs=(P(None, None, None, ("lat", "lon")),) + (P(),) * 11,
        out_specs=(P("lon", "lat", None), P(None, None, None, ("lat", "lon"))),
        check_vma=False,
    )
```

```python
import functools
import math

import jax
import jax.numpy as jnp
import ml_dtypes
import numpy as np
from jax import lax
from jax.experimental import pallas as pl
from jax.experimental.pallas import tpu as pltpu
from jax.sharding import PartitionSpec as P

NLAT, NLON, M = 512, 1024, 344
LV, VARS, CH, FIELDS = 24, 6, 64, 2
N_LAT, N_LON = 8, 16
ROWS, COLS = NLAT // N_LAT, NLON // N_LON
COLUMNS = ROWS * COLS
TILES = COLUMNS // 128
ITEMS = FIELDS * LV
GROUP = ITEMS // N_LON
OWNED = M // N_LAT
MP = 48
MH = MP // 2
KP = 352
HALF = NLAT // 2
HID = CH * LV
BAND = 8
SLAB = 49
BF, F32 = jnp.bfloat16, jnp.float32
NT = (((1,), (1,)), ((), ()))

BLOCKS = {(0, 0): (0, 0), (0, 1): (0, 1), (1, 0): (0, 2), (1, 1): (1, 2), (2, 0): (1, 0), (2, 1): (1, 1)}


def slab_of(tile, half):
    part, item = BLOCKS[(tile, half)]
    return part * GROUP + item


def iota(shape, dim):
    return lax.broadcasted_iota(jnp.int32, shape, dim)


def over_levels(index):
    return jnp.floor((index.astype(F32) + 0.5) * (1.0 / LV)).astype(jnp.int32)


def hbm(x):
    return pltpu.with_memory_space_constraint(x, pltpu.HBM)


def dot(a, b):
    return jnp.dot(a, b, preferred_element_type=F32)


def row_order():
    slots = np.arange(ROWS)
    return 2 * (slots % (ROWS // 2)) + slots // (ROWS // 2)


@functools.lru_cache(None)
def constants():
    n = np.arange(M)[:, None]
    angle = 2 * np.pi * ((n * np.arange(NLON)[None, :]) % NLON) / NLON
    factor = np.where(n == 0, 1.0, 2.0) / math.sqrt(NLAT * NLON)
    trig = np.concatenate(
        [np.cos(angle) / math.sqrt(NLON), np.sin(angle) / math.sqrt(NLON), np.cos(angle) * factor, np.sin(angle) * factor],
        axis=1,
    ).astype(ml_dtypes.bfloat16)
    slots = np.arange(NLAT)
    lat = (slots // ROWS) * ROWS + row_order()[slots % ROWS]
    phi = np.pi * (lat + 0.5) / NLAT - np.pi / 2
    sine, cosine = np.sin(phi), np.cos(phi)
    quad = (np.pi * cosine / math.sqrt(NLAT)).reshape(N_LAT, 1, ROWS)
    quad = np.tile(quad, (1, 1, 2 * GROUP)).astype(np.float32)
    lat_rows = np.zeros((8, HALF), np.float32)
    lat_rows[0], lat_rows[1] = sine[:HALF], np.log(cosine[:HALF])
    start = np.zeros((1, 384), np.float32)
    start[0, :M] = [
        0.5 * math.log(0.5) + 0.5 * (math.lgamma(m + 1.5) - math.lgamma(m + 1.0) - math.lgamma(1.5)) for m in range(M)
    ]
    return trig, quad, lat_rows, start


def to_column(row):
    n = row.shape[1]
    return jnp.sum(jnp.where(iota((n, n), 0) == iota((n, n), 1), row, jnp.zeros_like(row)), axis=1, keepdims=True)


def make_weights(w1_ref, bias1_ref, w2_ref, order_ref, bias2_ref, slots_in, o1_ref, o2_ref, ob_ref):
    width, rows = o1_ref.shape[1], o2_ref.shape[0]
    variables, fields = w1_ref.shape[1], bias2_ref.shape[1]
    order = order_ref[...]
    base = VARS * LV
    column = iota((1, width), 1)
    var_col = over_levels(column)
    level_col = column - LV * var_col
    if slots_in:
        wide_order = jnp.concatenate([jnp.zeros((1, base), jnp.int32), order, jnp.zeros((1, width - base - ITEMS), jnp.int32)], axis=1)
        slot_field = (wide_order >= LV).astype(jnp.int32)
        var_col = jnp.where(column < base, var_col + FIELDS, slot_field)
        level_col = jnp.where(column < base, level_col, wide_order - LV * slot_field)
    level_col = jnp.where(column < width - 16, level_col, -100)
    pick = (iota((variables, width), 0) == var_col).astype(F32).astype(BF)
    same = (iota((CH, CH), 0) == iota((CH, CH), 1)).astype(F32).astype(BF)
    blocks = []
    for tap in range(3):
        turned = lax.dot_general(same, w1_ref[tap], NT, preferred_element_type=F32)
        blocks.append(dot((0.5 * turned).astype(BF), pick))
    bias = 0.5 * to_column(bias1_ref[...])
    high = bias.astype(BF).astype(F32)
    low = bias - high
    bias_block = jnp.where(column == width - 16, high, jnp.where(column == width - 15, low, 0.0))
    for level in range(LV):
        block = bias_block
        for tap in range(3):
            block = jnp.where(level_col == level + 2 * (tap - 1), blocks[tap], block)
        o1_ref[level * CH : (level + 1) * CH, :] = block.astype(BF)
    hidden = o2_ref.shape[1]
    if slots_in:
        row = iota((rows, 1), 0)
        level_out = (row >> 3) - 2
        field_row = row & 7
    else:
        row = to_column(order.astype(F32)).astype(jnp.int32)
        field_row = (row >= LV).astype(jnp.int32)
        level_out = row - LV * field_row
    spread2 = ((iota((CH, hidden), 1) & (CH - 1)) == iota((CH, hidden), 0)).astype(F32).astype(BF)
    level_hid = iota((1, hidden), 1) >> 6
    total2 = jnp.zeros((rows, hidden), F32)
    bias2 = jnp.zeros((rows, 128), F32)
    for tap in range(3):
        block = jnp.zeros((rows, CH), F32)
        for field in range(fields):
            taps = w2_ref[field].astype(F32)[tap : tap + 1] if slots_in else w2_ref[tap].astype(F32)[field : field + 1]
            block = jnp.where(field_row == field, taps, block)
        wide = dot(block.astype(BF), spread2)
        total2 = jnp.where(level_hid == level_out + 2 * (tap - 1), wide, total2)
    o2_ref[...] = total2.astype(BF)
    for field in range(fields):
        bias2 = jnp.where(field_row == field, bias2_ref[0:1, field : field + 1], bias2)
    ob_ref[...] = bias2


def weights_kernel(w1_ref, bias1_ref, w2_ref, order_ref, bias2_ref, o1_ref, o2_ref, ob_ref):
    make_weights(w1_ref, bias1_ref, w2_ref, order_ref, bias2_ref, True, o1_ref, o2_ref, ob_ref)


def second_weights(w1, bias1, w2, bias2, order):
    full = lambda *shape: pl.BlockSpec(shape, lambda i: (0,) * len(shape))
    width, rows = VARS * LV + ITEMS + 16, 8 * BAND
    return pl.pallas_call(
        weights_kernel,
        out_shape=(
            pltpu.HBM((HID, width), BF),
            pltpu.HBM((rows, 4 * CH), BF),
            pltpu.HBM((rows, 128), F32),
        ),
        grid=(1,),
        in_specs=[full(*w1.shape), full(1, CH), full(*w2.shape), full(1, ITEMS), full(1, bias2.shape[0])],
        out_specs=(full(HID, width), full(rows, 4 * CH), full(rows, 128)),
        compiler_params=pltpu.CompilerParams(vmem_limit_bytes=20 * 2**20),
        cost_estimate=pl.CostEstimate(flops=2 * 10**8, bytes_accessed=2 * 10**6, transcendentals=0),
        name="second_weights",
    )(hbm(w1), hbm(bias1.reshape(1, CH)), hbm(w2), hbm(order.reshape(1, ITEMS)), hbm(bias2.reshape(1, -1)))


def hidden_layer(w1_ref, v_ref, h_ref, cols):
    tall = HID // 2
    c1, c2 = 2 * math.sqrt(2 / math.pi), 8 * 0.044715 * math.sqrt(2 / math.pi)
    for row in range(0, HID, tall):
        y = dot(w1_ref[row : row + tall, :], v_ref[:, cols])
        u = y * (c1 + c2 * (y * y))
        h_ref[row : row + tall, cols] = (y + y * jnp.tanh(u)).astype(BF)


def first_kernel(
    block, state_ref, c1_ref, bias1_ref, c2_ref, order_ref, bias2_ref, out_ref, w1_ref, w2_ref, b2_ref, v_ref, h_ref, o_ref
):
    step = pl.program_id(0)

    @pl.when(step == 0)
    def _():
        make_weights(c1_ref, bias1_ref, c2_ref, order_ref, bias2_ref, False, w1_ref, w2_ref, b2_ref)
        v_ref[VARS * LV :, :] = jnp.ones((16, block), BF)

    v_ref[: VARS * LV, :] = state_ref[...]
    bias = b2_ref[...]
    for col in range(0, block, 256):
        hidden_layer(w1_ref, v_ref, h_ref, slice(col, col + 256))
        result = dot(w2_ref[...], h_ref[:, col : col + 256])
        for half in range(2):
            tile = step * (block // 128) + col // 128 + half
            o_ref[pl.ds(tile, ITEMS, stride=TILES + 1), :] = result[:, half * 128 : (half + 1) * 128] + bias

    @pl.when(step == pl.num_programs(0) - 1)
    def _():
        for item in range(ITEMS):
            out_ref[item] = o_ref[item * (TILES + 1) : item * (TILES + 1) + TILES, :].astype(BF)


def first_conv(state, w1, bias1, w2, bias2, order, block=COLUMNS):
    full = lambda *shape: pl.BlockSpec(shape, lambda i: (0,) * len(shape))
    return pl.pallas_call(
        functools.partial(first_kernel, block),
        grid=(COLUMNS // block,),
        out_shape=pltpu.HBM((ITEMS, TILES, 128), BF),
        in_specs=[
            pl.BlockSpec((VARS * LV, block), lambda i: (0, i)),
            full(*w1.shape),
            full(1, CH),
            full(*w2.shape),
            full(1, ITEMS),
            full(1, bias2.shape[0]),
        ],
        out_specs=full(ITEMS, TILES, 128),
        scratch_shapes=[
            pltpu.VMEM((HID, VARS * LV + 16), BF),
            pltpu.VMEM((ITEMS, HID), BF),
            pltpu.VMEM((ITEMS, 128), F32),
            pltpu.VMEM((VARS * LV + 16, block), BF),
            pltpu.VMEM((HID, block), BF),
            pltpu.VMEM((ITEMS * (TILES + 1), 128), F32),
        ],
        compiler_params=pltpu.CompilerParams(vmem_limit_bytes=40 * 2**20),
        cost_estimate=pl.CostEstimate(flops=3 * 10**9, bytes_accessed=2 * 10**6, transcendentals=HID * COLUMNS),
        name="first_conv",
    )(hbm(state), hbm(w1), hbm(bias1.reshape(1, CH)), hbm(w2), hbm(order.reshape(1, ITEMS)), hbm(bias2.reshape(1, -1)))


def second_kernel(block, state_ref, filt_ref, w1_ref, w2_ref, b2_ref, out_ref, v_ref, h_ref, f_ref, e_ref):
    step = pl.program_id(0)
    base = VARS * LV

    @pl.when(step == 0)
    def _():
        v_ref[base + ITEMS :, :] = jnp.ones((16, block), BF)
        for item in range(ITEMS):
            f_ref[item * (TILES + 1) : item * (TILES + 1) + TILES, :] = filt_ref[item].astype(F32)

    v_ref[:base, :] = state_ref[...]
    for tile in range(block // 128):
        piece = f_ref[pl.ds(step * (block // 128) + tile, ITEMS, stride=TILES + 1), :]
        v_ref[base : base + ITEMS, tile * 128 : (tile + 1) * 128] = piece.astype(BF)
    bias = b2_ref[0:8, :]
    for col in range(0, block, 256):
        hidden_layer(w1_ref, v_ref, h_ref, slice(col, col + 256))
        levels = [None] * LV
        for group in range(LV // 4):
            part = dot(w2_ref[...], h_ref[group * 4 * CH : (group + 1) * 4 * CH, col : col + 256])
            for at in range(BAND):
                level = 4 * group - 2 + at
                if 0 <= level < LV:
                    piece = part[8 * at : 8 * at + 8]
                    levels[level] = piece if levels[level] is None else levels[level] + piece
        for half in range(2):
            lanes = slice(col + half * 128, col + half * 128 + 128)
            for level in range(LV):
                e_ref[half, 9 * level : 9 * level + 8, :] = levels[level][:, half * 128 : (half + 1) * 128] + bias
            for variable in range(VARS):
                out_ref[variable * LV : (variable + 1) * LV, lanes] = e_ref[half, pl.ds(variable, LV, stride=9), :]


def second_conv(state, filtered, w1, w2, b2, block=2048):
    full = lambda *shape: pl.BlockSpec(shape, lambda i: (0,) * len(shape))
    width = VARS * LV + ITEMS + 16
    return pl.pallas_call(
        functools.partial(second_kernel, block),
        grid=(COLUMNS // block,),
        out_shape=pltpu.HBM((VARS * LV, COLUMNS), F32),
        in_specs=[
            pl.BlockSpec((VARS * LV, block), lambda i: (0, i)),
            pl.BlockSpec(memory_space=pltpu.VMEM),
            pl.BlockSpec(memory_space=pltpu.VMEM),
            pl.BlockSpec(memory_space=pltpu.VMEM),
            pl.BlockSpec(memory_space=pltpu.VMEM),
        ],
        out_specs=pl.BlockSpec((VARS * LV, block), lambda i: (0, i)),
        scratch_shapes=[
            pltpu.VMEM((width, block), BF),
            pltpu.VMEM((HID, block), BF),
            pltpu.VMEM((ITEMS * (TILES + 1), 128), F32),
            pltpu.VMEM((2, 9 * LV, 128), F32),
        ],
        compiler_params=pltpu.CompilerParams(vmem_limit_bytes=40 * 2**20),
        cost_estimate=pl.CostEstimate(flops=4 * 10**9, bytes_accessed=4 * 10**6, transcendentals=HID * COLUMNS),
        name="second_conv",
    )(hbm(state), filtered, w1, w2, b2)


CHUNK = 176
STRIDE = CHUNK + 1
LANES = -(-CHUNK // 128) * 128


def table_kernel(wave_ref, lat_ref, start_ref, out_ref, now_ref, old_ref, log_ref, ratio_ref, s_ref):
    step = pl.program_id(0)
    wave = jnp.broadcast_to(wave_ref[...], (MH, 128))
    sine = [lat_ref[0:1, 128 * h : 128 * h + 128] for h in range(2)]

    @pl.when(step == 0)
    def _():
        match = iota((MH, 384), 1).astype(F32) == wave_ref[...]
        start = jnp.sum(jnp.where(match, start_ref[...], 0.0), axis=1, keepdims=True)
        for h in range(2):
            log_cos = lat_ref[1:2, 128 * h : 128 * h + 128]
            log_ref[h] = jnp.where(wave > 500.0, -1e4, start + wave * log_cos)
            now_ref[h] = jnp.zeros((MH, 128), F32)
            old_ref[h] = jnp.zeros((MH, 128), F32)
        ratio_ref[...] = jnp.zeros((MH, 128), F32)

    now = [now_ref[h] for h in range(2)]
    old = [old_ref[h] for h in range(2)]
    log_scale = [log_ref[h] for h in range(2)]
    ratio = ratio_ref[...]
    scale = [None, None]
    k = (step * CHUNK).astype(F32) + iota((MH, LANES), 1).astype(F32)
    m = jnp.broadcast_to(wave_ref[...], (MH, LANES))
    n = m + k
    top = 4.0 * (n * n) - 1.0
    bottom = k * (m + n)
    root = lax.rsqrt(jnp.maximum(top * bottom, 1e-30))
    ups = jnp.where(n <= M - 1.0, top * root, 0.0)
    ratios = bottom * root
    for kk in range(CHUNK):
        if kk % 8 == 0:
            for h in range(2):
                big = jnp.abs(now[h]) > 1e8
                shrink = jnp.where(big, 1e-12, 1.0)
                now[h] = now[h] * shrink
                old[h] = old[h] * shrink
                log_scale[h] = log_scale[h] + jnp.where(big, math.log(1e12), 0.0)
                scale[h] = jnp.exp(log_scale[h])
        up = jnp.broadcast_to(ups[:, kk : kk + 1], (MH, 128))
        for h in range(2):
            stepped = up * (sine[h] * now[h] - ratio * old[h])
            if kk == 0:
                stepped = jnp.where(step == 0, 1.0, stepped)
            old[h], now[h] = now[h], stepped
            s_ref[h, pl.ds(kk, MH, stride=STRIDE), :] = stepped * scale[h]
        ratio = jnp.broadcast_to(ratios[:, kk : kk + 1], (MH, 128))
    for h in range(2):
        now_ref[h], old_ref[h], log_ref[h] = now[h], old[h], log_scale[h]
    ratio_ref[...] = ratio
    for m in range(MH):
        for h in range(2):
            out_ref[m, :, 128 * h : 128 * h + 128] = s_ref[h, m * STRIDE : m * STRIDE + CHUNK, :].astype(BF)


def legendre_table(waves_f, lat_rows, start):
    full = lambda *shape: pl.BlockSpec(shape, lambda i: (0,) * len(shape))
    return pl.pallas_call(
        table_kernel,
        grid=(KP // CHUNK,),
        out_shape=pltpu.HBM((MH, KP, HALF), BF),
        in_specs=[full(MH, 1), full(8, HALF), full(1, 384)],
        out_specs=pl.BlockSpec((MH, CHUNK, HALF), lambda i: (0, i, 0)),
        scratch_shapes=[pltpu.VMEM((2, MH, 128), F32)] * 3
        + [pltpu.VMEM((MH, 128), F32), pltpu.VMEM((2, MH * STRIDE, 128), F32)],
        compiler_params=pltpu.CompilerParams(vmem_limit_bytes=20 * 2**20),
        cost_estimate=pl.CostEstimate(flops=2 * 10**8, bytes_accessed=9 * 10**6, transcendentals=0),
        name="legendre_table",
    )(waves_f, lat_rows, start)


def swap_halves(x):
    return pltpu.roll(x, 64, 1)


def forward_kernel(y_ref, f_ref, q_ref, out_ref, x0_ref, x1_ref):
    low = iota((TILES, 128), 1) < 64
    x0_ref[192:256, :] = jnp.zeros((64, NLON), BF)
    x1_ref[0:64, :] = jnp.zeros((64, NLON), BF)
    place0, place1 = (0, 64, 128), (128, 192, 64)
    for pair in range(N_LON // 2):
        for item in range(GROUP):
            a = y_ref[2 * pair, item].astype(F32)
            b = y_ref[2 * pair + 1, item].astype(F32)
            even = jnp.where(low, a, swap_halves(b)).astype(BF)
            odd = jnp.where(low, swap_halves(a), b).astype(BF)
            lanes = slice(128 * pair, 128 * pair + 128)
            for ref, place in ((x0_ref, place0), (x1_ref, place1)):
                ref[place[item] : place[item] + 32, lanes] = even
                ref[place[item] + 32 : place[item] + 64, lanes] = odd
    quad = q_ref[pl.ds(lax.axis_index("lat"), 1), :]
    cosines = lax.dot_general(f_ref[:, :NLON], x0_ref[...], NT, preferred_element_type=F32)
    sines = lax.dot_general(f_ref[:, NLON:], x1_ref[...], NT, preferred_element_type=F32)
    tiles = (cosines[:, :128], cosines[:, 128:] + sines[:, :128], sines[:, 128:])
    for t, value in enumerate(tiles):
        value = (value * quad[:, 128 * t : 128 * t + 128]).astype(BF)
        for group in range(N_LAT):
            out_ref[group, :, 128 * t : 128 * t + 128] = value[group * MP : (group + 1) * MP]


def forward_fourier(pieces, tables, quad):
    full = lambda *shape: pl.BlockSpec(shape, lambda i: (0,) * len(shape))
    return pl.pallas_call(
        forward_kernel,
        grid=(1,),
        out_shape=pltpu.HBM((N_LAT, MP, 384), BF),
        in_specs=[pl.BlockSpec(memory_space=pltpu.VMEM)] * 3,
        out_specs=full(N_LAT, MP, 384),
        scratch_shapes=[pltpu.VMEM((256, NLON), BF)] * 2,
        compiler_params=pltpu.CompilerParams(vmem_limit_bytes=20 * 2**20),
        cost_estimate=pl.CostEstimate(flops=4 * 10**8, bytes_accessed=3 * 10**6, transcendentals=0),
        name="forward_fourier",
    )(pieces, tables, quad)


def inverse_kernel(r_ref, f_ref, out_ref):
    turned = [r_ref[:, 128 * t : 128 * t + 128].astype(F32).T.astype(BF) for t in range(3)]
    cosines = jnp.concatenate([turned[0], turned[1][:64]], axis=0)
    sines = jnp.concatenate([turned[2], turned[1][64:]], axis=0)
    grid = dot(cosines, f_ref[:, :NLON]) + dot(sines, f_ref[:, NLON:])
    low = iota((TILES, 128), 1) < 64
    for pair in range(N_LON // 2):
        for item in range(GROUP):
            lanes = slice(128 * pair, 128 * pair + 128)
            even = grid[64 * item : 64 * item + 32, lanes]
            odd = grid[64 * item + 32 : 64 * item + 64, lanes]
            out_ref[2 * pair, item] = jnp.where(low, even, swap_halves(odd)).astype(BF)
            out_ref[2 * pair + 1, item] = jnp.where(low, swap_halves(even), odd).astype(BF)


def inverse_fourier(returned, tables):
    full = lambda *shape: pl.BlockSpec(shape, lambda i: (0,) * len(shape))
    return pl.pallas_call(
        inverse_kernel,
        grid=(1,),
        out_shape=pltpu.HBM((N_LON, GROUP, TILES, 128), BF),
        in_specs=[pl.BlockSpec(memory_space=pltpu.VMEM)] * 2,
        out_specs=full(N_LON, GROUP, TILES, 128),
        compiler_params=pltpu.CompilerParams(vmem_limit_bytes=20 * 2**20),
        cost_estimate=pl.CostEstimate(flops=4 * 10**8, bytes_accessed=3 * 10**6, transcendentals=0),
        name="inverse_fourier",
    )(returned, tables)


WAVES = 12
GROUPS = -(-OWNED // WAVES)
LAST = OWNED - (GROUPS - 1) * WAVES


def spectral_kernel(wave_ref, x_ref, t0_ref, t1_ref, gain_ref, spec_ref, out_ref, c_ref, n_ref, r_ref, m_ref, t_ref, sems):
    step = pl.program_id(0)
    low = iota((MP, 128), 1) < 64

    def table_copy(group):
        first, count = group * WAVES, LAST if group == GROUPS - 1 else WAVES
        source, at = (t0_ref, first) if first < MH else (t1_ref, first - MH)
        return pltpu.make_async_copy(source.at[pl.ds(at, count)], t_ref.at[pl.ds(first, count)], sems.at[group])

    @pl.when(step == 0)
    def _():
        for group in range(GROUPS):
            table_copy(group).start()

    mirror = (iota((HALF, HALF), 0) + iota((HALF, HALF), 1) == HALF - 1).astype(F32).astype(BF)

    @pl.when(step == 0)
    def _():
        for slab in (6, 7, 14, 15):
            for h in range(2):
                c_ref[h, slab * SLAB : slab * SLAB + MP, :] = jnp.zeros((MP, 128), F32)
        for slab in range(6):
            for h in range(4):
                r_ref[h, slab * SLAB + OWNED : slab * SLAB + MP, :] = jnp.zeros((MP - OWNED, 128), F32)
        for pair in range(N_LAT // 2):
            for tile in range(3):
                a = x_ref[2 * pair, :, 128 * tile : 128 * tile + 128].astype(F32)
                b = x_ref[2 * pair + 1, :, 128 * tile : 128 * tile + 128].astype(F32)
                both = jnp.where(low, a, swap_halves(b)), jnp.where(low, swap_halves(a), b)
                for half in range(2):
                    slab = slab_of(tile, half)
                    if pair < 2:
                        c_ref[pair, slab * SLAB : slab * SLAB + MP, :] = both[half]
                    else:
                        m_ref[slab * MP : slab * MP + MP, 128 * (pair - 2) : 128 * (pair - 2) + 128] = both[half].astype(BF)
        turned = dot(m_ref[...], mirror)
        for slab in range(6):
            for h in range(2):
                a = c_ref[h, slab * SLAB : slab * SLAB + MP, :]
                b = turned[slab * MP : slab * MP + MP, 128 * h : 128 * h + 128]
                c_ref[h, slab * SLAB : slab * SLAB + MP, :] = a + b
                c_ref[h, (8 + slab) * SLAB : (8 + slab) * SLAB + MP, :] = a - b

    even = iota((8, KP), 1) % 2 == 0
    gain = gain_ref[...]

    def waves(count):
        boths = []
        for mm in range(count):
            m = step * WAVES + mm
            left = jnp.concatenate([c_ref[h, pl.ds(m, 16, stride=SLAB), :] for h in range(2)], axis=1).astype(BF)
            boths.append(lax.dot_general(left, t_ref[m], NT, preferred_element_type=F32))
        rights = []
        for mm in range(count):
            m = step * WAVES + mm
            natural = jnp.where(even, boths[mm][:8], boths[mm][8:])
            n_ref[0, pl.ds(m, 8, stride=SLAB), :] = natural[:, :128]
            n_ref[1, pl.ds(m, 8, stride=SLAB), :] = natural[:, 128:256]
            n_ref[2, pl.ds(m, 8, stride=SLAB), :] = jnp.concatenate([natural[:, 256:], jnp.zeros((8, 384 - KP), F32)], axis=1)
            scaled = natural * pltpu.roll(gain, 768 - wave_ref[m], 1)[:, :KP]
            rights.append(jnp.concatenate([jnp.where(even, scaled, 0.0), jnp.where(even, 0.0, scaled)], axis=0).astype(BF))
        for mm in range(count):
            m = step * WAVES + mm
            back = dot(rights[mm], t_ref[m])
            north, south = back[:8] + back[8:], back[:8] - back[8:]
            for h in range(2):
                r_ref[h, pl.ds(m, 8, stride=SLAB), :] = north[:, 128 * h : 128 * h + 128]
                r_ref[2 + h, pl.ds(m, 8, stride=SLAB), :] = south[:, 128 * h : 128 * h + 128]

    for group in range(GROUPS):

        @pl.when(step == group)
        def _():
            table_copy(group).wait()

    pl.when(step < GROUPS - 1)(lambda: waves(WAVES))
    pl.when(step == GROUPS - 1)(lambda: waves(LAST))

    @pl.when(step == pl.num_programs(0) - 1)
    def _():
        for slab in range(6):
            for h in range(2):
                m_ref[slab * MP : slab * MP + MP, 128 * h : 128 * h + 128] = r_ref[2 + h, slab * SLAB : slab * SLAB + MP, :].astype(BF)
        turned = dot(m_ref[...], mirror)

        def tile_of(slab, j):
            if j < 2:
                return r_ref[j, slab * SLAB : slab * SLAB + MP, :]
            return turned[slab * MP : slab * MP + MP, 128 * (j - 2) : 128 * (j - 2) + 128]

        for pair in range(N_LAT // 2):
            for tile in range(3):
                a = tile_of(slab_of(tile, 0), pair)
                b = tile_of(slab_of(tile, 1), pair)
                lanes = slice(128 * tile, 128 * tile + 128)
                out_ref[2 * pair, :, lanes] = jnp.where(low, a, swap_halves(b)).astype(BF)
                out_ref[2 * pair + 1, :, lanes] = jnp.where(low, swap_halves(a), b).astype(BF)
        wide = iota((MP, 768), 1) < M
        zeros = jnp.zeros((MP, 384), F32)
        for item in range(GROUP):
            parts = []
            for part in range(2):
                at = (part * GROUP + item) * SLAB
                parts.append(jnp.concatenate([n_ref[h, at : at + MP, :] for h in range(3)] + [zeros], axis=1))
            value = jnp.where(wide, parts[0], pltpu.roll(parts[1], M, 1))
            spec_ref[item] = value[:OWNED, : 2 * M]


def spectral_step(waves, coeffs, table0, table1, gain):
    full = lambda *shape: pl.BlockSpec(shape, lambda i, w: (0,) * len(shape))
    return pl.pallas_call(
        spectral_kernel,
        grid_spec=pltpu.PrefetchScalarGridSpec(
            num_scalar_prefetch=1,
            grid=(GROUPS,),
            in_specs=[
                pl.BlockSpec(memory_space=pltpu.VMEM),
                pl.BlockSpec(memory_space=pltpu.HBM),
                pl.BlockSpec(memory_space=pltpu.HBM),
                pl.BlockSpec(memory_space=pltpu.VMEM),
            ],
            out_specs=(full(GROUP, OWNED, 2 * M), full(N_LAT, MP, 384)),
            scratch_shapes=[
                pltpu.VMEM((2, 16 * SLAB, 128), F32),
                pltpu.VMEM((3, 8 * SLAB, 128), F32),
                pltpu.VMEM((4, 8 * SLAB, 128), F32),
                pltpu.VMEM((6 * MP, HALF), BF),
                pltpu.VMEM((OWNED, KP, HALF), BF),
                pltpu.SemaphoreType.DMA((GROUPS,)),
            ],
        ),
        out_shape=(
            pltpu.HBM((GROUP, OWNED, 2 * M), F32),
            pltpu.HBM((N_LAT, MP, 384), BF),
        ),
        compiler_params=pltpu.CompilerParams(vmem_limit_bytes=24 * 2**20),
        cost_estimate=pl.CostEstimate(flops=4 * 10**9, bytes_accessed=10**7, transcendentals=0),
        name="spectral_step",
    )(waves, coeffs, hbm(table0), hbm(table1), gain)


def one_hot(grouped):
    return (grouped.reshape(N_LAT * MP)[:, None] == jnp.arange(M, dtype=jnp.int32)[None, :]).astype(BF)


def per_device(
    state, conv_in, bias_in, conv_out, bias_out, spectral_gain, mix_in, blend_bias, mix_out, mix_out_bias, level_order, wave_order
):
    trig, quad, lat_rows, start = constants()
    band = lax.axis_index("lat")
    columns = state.reshape(VARS * LV, COLUMNS)

    tendency = first_conv(columns, conv_in.transpose(1, 2, 0), bias_in, conv_out.transpose(1, 0, 2), bias_out, level_order)
    tendency, wave_order, spectral_gain = lax.optimization_barrier((tendency, wave_order, spectral_gain))
    pieces = lax.all_to_all(tendency.reshape(N_LON, GROUP, TILES, 128), "lon", 0, 0, tiled=True)

    grouped = jnp.pad(wave_order.reshape(N_LAT, OWNED), ((0, 0), (0, MP - OWNED)), constant_values=-1)
    tables = dot(one_hot(grouped), jnp.asarray(trig[:, : 2 * NLON])).astype(BF)
    owned = lax.dynamic_slice_in_dim(grouped, band, 1, 0)[0]
    waves_f = jnp.where(owned < 0, 1000, owned).astype(F32)[:, None]
    lat_rows, start = jnp.asarray(lat_rows), jnp.asarray(start)
    band_quad = jnp.asarray(quad[:, 0])
    gain = jnp.broadcast_to(jnp.pad(spectral_gain, (0, 768 - M))[None], (8, 768))
    owned = jnp.maximum(owned, 0)
    table0 = legendre_table(waves_f[:MH], lat_rows, start)
    pieces, table0, tables, gain, owned, band_quad = lax.optimization_barrier(
        (pieces, table0, tables, gain, owned, band_quad)
    )

    coeffs = forward_fourier(pieces, tables, band_quad)
    coeffs, waves_late = lax.optimization_barrier((coeffs, waves_f[MH:]))
    coeffs = lax.all_to_all(coeffs, "lat", 0, 0, tiled=True)
    table1 = legendre_table(waves_late, lat_rows, start)
    coeffs, table1 = lax.optimization_barrier((coeffs, table1))

    spectrum, returned = spectral_step(owned, coeffs, table0, table1, gain)
    returned, mix_in, blend_bias, mix_out, mix_out_bias, level_order, grouped = lax.optimization_barrier(
        (returned, mix_in, blend_bias, mix_out, mix_out_bias, level_order, grouped)
    )
    returned = lax.all_to_all(returned, "lat", 0, 0, tiled=True)
    m1, m2, mb = second_weights(mix_in.transpose(1, 2, 0), blend_bias, mix_out, mix_out_bias, level_order)
    inverse_tables = dot(one_hot(grouped), jnp.asarray(trig[:, 2 * NLON :])).astype(BF)
    returned, m1, m2, mb, inverse_tables = lax.optimization_barrier((returned, m1, m2, mb, inverse_tables))
    grid_values = inverse_fourier(returned.reshape(N_LAT * MP, 384), inverse_tables)
    filtered = lax.all_to_all(grid_values, "lon", 0, 0, tiled=True)
    increment = second_conv(columns, filtered.reshape(ITEMS, TILES, 128), m1, m2, mb)
    return spectrum, increment.reshape(1, VARS, LV, COLUMNS)


def solution(mesh):
    return jax.shard_map(
        per_device,
        mesh=mesh,
        in_specs=(P(None, None, None, ("lat", "lon")),) + (P(),) * 11,
        out_specs=(P("lon", "lat", None), P(None, None, None, ("lat", "lon"))),
        check_vma=False,
    )
```
